128 devices in a mesh: rep: 2 (over y_hi), shard: 64 (over z, x, y_lo, core).
Axes of the slice: x: 4, y: 4 (y_hi: 2, y_lo: 2; y = y_hi * 2 + y_lo), z: 4, core: 2. Of those that a mesh axis runs over, the one named last changes fastest.
Arguments:
- hidden_in: bfloat16 [64, 256, 2048], P('shard', 'rep'), may hold values from -6 to 6
- lengths: int32 [64], P('shard'), may hold values from 64 to 256, as said below
- w_query: bfloat16 [2048, 2048], P('shard'), may hold values from -0.1875 to 0.1875
- w_key: bfloat16 [2048, 2048], P('shard'), may hold values from -0.1875 to 0.1875
- w_value: bfloat16 [2048, 2048], P('shard'), may hold values from -0.125 to 0.125
- w_output: bfloat16 [2048, 2048], P('shard'), may hold values from -0.5 to 0.5
- attn_gain: bfloat16 [2048], P('shard'), may hold values from 0.25 to 1.75
- attn_shift: bfloat16 [2048], P('shard'), may hold values from -1.5 to 1.5
- w_up: bfloat16 [2048, 8192], P('shard'), may hold values from -0.125 to 0.125
- w_down: bfloat16 [8192, 2048], P('shard'), may hold values from -0.375 to 0.375
- mlp_gain: bfloat16 [2048], P('shard'), may hold values from 0.25 to 1.75
- mlp_shift: bfloat16 [2048], P('shard'), may hold values from -1.5 to 1.5
- cotangent: bfloat16 [64, 256, 2048], P('shard', 'rep'), may hold values from -6 to 6
Outputs:
- output: bfloat16 [64, 256, 2048], P('shard', 'rep')
- input_grad: float32 [64, 256, 2048], P('shard', 'rep')
- grad_w_query: float32 [2048, 2048], P('shard')
- grad_w_key: float32 [2048, 2048], P('shard')
- grad_w_value: float32 [2048, 2048], P('shard')
- grad_w_output: float32 [2048, 2048], P('shard')
- grad_attn_gain: float32 [2048], P('shard')
- grad_attn_shift: float32 [2048], P('shard')
- grad_w_up: float32 [2048, 8192], P('shard')
- grad_w_down: float32 [8192, 2048], P('shard')
- grad_mlp_gain: float32 [2048], P('shard')
- grad_mlp_shift: float32 [2048], P('shard')
- rms_stats: float32 [3], replicated
The draws below stay inside these ranges and needn't reach their ends.
Inputs may be any that keep to these rules, and one draw needn't show every extreme that they name: lengths[s] is the number of valid slots of sequence s; slots t with lengths[s] <= t < 256 are padding.
All inputs are finite; a program needn't handle non-finite values.
Results may differ from the reference program's by a relative error of at most 0.019.
Values may be sent and summed in bfloat16 or wider, within the bound.
No kernel may reach another device: no remote copies, remote signals or barrier semaphores. Data moves between devices by JAX's collectives and lax.ppermute only.
A program may use at most 576 MiB of HBM per device.

```python
import math
import jax
import jax.numpy as jnp
from jax import lax

D = 2048
FF = 8192
HEAD_DIM = 128
SEQ_LEN = 256
SEQS = 64


def draw_lengths(key, part):
    key_jitter, key_top, key_bottom = jax.random.split(jax.random.fold_in(key, 11), 3)
    index = jnp.arange(SEQS, dtype=jnp.int32)
    least = SEQ_LEN // 4
    span = SEQ_LEN - least
    base = least + span * index // max(SEQS - 1, 1)
    jitter = jax.random.randint(key_jitter, (SEQS,), -(SEQ_LEN // 8), SEQ_LEN // 8 + 1, dtype=jnp.int32)
    drawn = jnp.clip(base + jitter, least, SEQ_LEN)
    quarter = max(SEQS // 4, 1)
    top_index = SEQS - 1 - jax.random.randint(key_top, (), 0, quarter, dtype=jnp.int32)
    bottom_index = jax.random.randint(key_bottom, (), 0, quarter, dtype=jnp.int32)
    drawn = jnp.where(index == top_index, SEQ_LEN, drawn)
    drawn = jnp.where(index == bottom_index, least, drawn)
    return drawn.astype(jnp.int32)


def steps_of(own_key, shape, cuts, low, high):
    def one(dim, shards_of):
        heights = jax.random.uniform(jax.random.fold_in(jax.random.fold_in(own_key, 6), dim), (shards_of,), jnp.float32, low / len(cuts), high / len(cuts))
        return jnp.repeat(jnp.exp(heights), shape[dim] // shards_of).reshape((-1,) + (1,) * (len(shape) - dim - 1))

    gain = one(*cuts[0])
    for cut in cuts[1:]:
        gain = gain * one(*cut)
    return gain


def gaussian(key, shape, width, limit, cuts=(), kind=jnp.bfloat16):
    factor_of = steps_of(key, shape, cuts, -0.22, 0.18) if cuts else 1.0
    values = jax.random.normal(key, shape, jnp.float32) * width * factor_of
    return jnp.minimum(jnp.maximum(values, -limit), limit).astype(kind)


def setup_inputs(seed: int = 0) -> dict:
    streams_of = jax.random.split(jax.random.key(seed), 14)
    hidden_in = gaussian(streams_of[0], (SEQS, SEQ_LEN, D), 1.0, 6.0, ((0, 64), (1, 2)))
    lengths = draw_lengths(jax.random.fold_in(streams_of[13], 71), 0)
    w_query = gaussian(streams_of[2], (D, D), (D // 2) ** -0.5, 0.1875, ((0, 64),))
    w_key = gaussian(streams_of[3], (D, D), (D // 2) ** -0.5, 0.1875, ((0, 64),))
    w_value = gaussian(streams_of[4], (D, D), D ** -0.5, 0.125, ((0, 64),))
    w_output = gaussian(streams_of[5], (D, D), (D // 16) ** -0.5, 0.5, ((0, 64),))
    attn_gain = jnp.clip(1.0 + 0.15 * jax.random.normal(streams_of[6], (D,), jnp.float32), 0.25, 1.75).astype(jnp.bfloat16)
    attn_shift = gaussian(streams_of[7], (D,), 0.3, 1.5, ((0, 64),))
    w_up = gaussian(streams_of[8], (D, FF), D ** -0.5, 0.125, ((0, 64),))
    w_down = gaussian(streams_of[9], (FF, D), (FF // 32) ** -0.5, 0.375, ((0, 64),))
    mlp_gain = jnp.clip(1.0 + 0.15 * jax.random.normal(streams_of[10], (D,), jnp.float32), 0.25, 1.75).astype(jnp.bfloat16)
    mlp_shift = gaussian(streams_of[11], (D,), 0.3, 1.5, ((0, 64),))
    cotangent = gaussian(streams_of[12], (SEQS, SEQ_LEN, D), 1.0, 6.0, ((0, 64), (1, 2)))
    return {"hidden_in": hidden_in, "lengths": lengths, "w_query": w_query, "w_key": w_key, "w_value": w_value, "w_output": w_output, "attn_gain": attn_gain, "attn_shift": attn_shift, "w_up": w_up, "w_down": w_down, "mlp_gain": mlp_gain, "mlp_shift": mlp_shift, "cotangent": cotangent}


@jax.custom_vjp
def low(v):
    return lax.optimization_barrier(v.astype(jnp.bfloat16)).astype(jnp.float32)

@jax.custom_vjp
def low_back(v):
    return v

def low_keep(v):
    return (low(v), None)

def low_pass(kept, grad):
    return (grad,)

def back_keep(v):
    return (v, None)

def back_low(kept, grad):
    return (low(grad),)
low.defvjp(low_keep, low_pass)
low_back.defvjp(back_keep, back_low)
highest = lax.Precision.HIGHEST
norm_eps = 1e-12
masked_score = -1e+30

def product(left_side, right_side):
    return jnp.dot(left_side, right_side, precision=highest, preferred_element_type=jnp.float32)

def layer_norm(values, gain_vec, shift_vec):
    center = values - lax.optimization_barrier(jnp.mean(values, axis=-1, keepdims=True))
    spread = lax.optimization_barrier(jnp.mean(center * center, axis=-1, keepdims=True))
    return center * lax.rsqrt(spread + norm_eps) * gain_vec + shift_vec

def rounded_both(values):
    return low(low_back(values))

def forward_block(tok_rows, key_valid, w_query, w_key, w_value, w_output, attn_gain, attn_shift, w_up, w_down, mlp_gain, mlp_shift):
    seq_count, length = key_valid.shape
    head_count = D // HEAD_DIM
    queries = rounded_both(product(tok_rows, w_query)).reshape(seq_count, length, head_count, HEAD_DIM)
    key_vecs = rounded_both(product(tok_rows, w_key)).reshape(seq_count, length, head_count, HEAD_DIM)
    value_vecs = rounded_both(product(tok_rows, w_value)).reshape(seq_count, length, head_count, HEAD_DIM)
    scores = jnp.einsum('gqhd,gkhd->ghqk', queries, key_vecs, precision=highest) * HEAD_DIM ** (-0.5)
    scores = low_back(scores)
    scores = jnp.where(key_valid[:, None, None, :] > 0.5, scores, masked_score)
    attn_probs = jax.nn.softmax(scores, axis=-1)
    context = jnp.einsum('ghqk,gkhd->gqhd', low(attn_probs), value_vecs, precision=highest)
    context = rounded_both(context.reshape(seq_count * length, D))
    attn_out = low_back(product(context, w_output))
    resid_one = tok_rows + attn_out
    normed_one = layer_norm(resid_one, attn_gain, attn_shift)
    pre_act = low_back(product(low(normed_one), w_up))
    act_low = low(jax.nn.gelu(pre_act, approximate=True))
    mlp_out = low_back(product(act_low, w_down))
    resid_two = normed_one + mlp_out
    return (layer_norm(resid_two, mlp_gain, mlp_shift), (resid_one, attn_out, mlp_out))

def reference(hidden_in, lengths, w_query, w_key, w_value, w_output, attn_gain, attn_shift, w_up, w_down, mlp_gain, mlp_shift, cotangent):
    params = tuple((matrix.astype(jnp.float32) for matrix in (w_query, w_key, w_value, w_output, attn_gain, attn_shift, w_up, w_down, mlp_gain, mlp_shift)))
    per_turn = math.gcd(SEQS, max(1, 4096 // SEQ_LEN))
    turn_count = SEQS // per_turn
    inputs_all = hidden_in.astype(jnp.float32).reshape(turn_count, per_turn, SEQ_LEN, D)
    cot_all = cotangent.astype(jnp.float32).reshape(turn_count, per_turn, SEQ_LEN, D)
    len_all = lengths.astype(jnp.int32).reshape(turn_count, per_turn)
    positions = jnp.arange(SEQ_LEN, dtype=jnp.int32)

    def one_turn(carry, sliced):
        grad_sums, stat_sums = carry
        tok_block, cot_block, len_block = sliced
        key_valid = (positions[None, :] < len_block[:, None]).astype(jnp.float32)
        tok_rows = tok_block.reshape(per_turn * SEQ_LEN, D)

        def apply_block(tok_arg, *param_args):
            return forward_block(tok_arg, key_valid, *param_args)
        outputs, pullback, kept = jax.vjp(apply_block, tok_rows, *params, has_aux=True)
        row_valid = key_valid.reshape(per_turn * SEQ_LEN, 1)
        grad_all = pullback(cot_block.reshape(per_turn * SEQ_LEN, D) * row_valid)
        new_sums = tuple((running + addend for running, addend in zip(grad_sums, grad_all[1:])))
        resid_one, attn_out, mlp_out = kept
        stat_terms = jnp.stack([jnp.sum(row_valid * resid_one * resid_one), jnp.sum(row_valid * attn_out * attn_out), jnp.sum(row_valid * mlp_out * mlp_out), jnp.sum(key_valid)])
        return ((new_sums, stat_sums + stat_terms), (outputs.astype(jnp.bfloat16).reshape(per_turn, SEQ_LEN, D), grad_all[0].reshape(per_turn, SEQ_LEN, D)))
    start = (tuple((jnp.zeros(matrix.shape, jnp.float32) for matrix in params)), jnp.zeros((4,), jnp.float32))
    (grad_sums, stat_sums), (outputs, input_grads) = lax.scan(one_turn, start, (inputs_all, cot_all, len_all))
    output = outputs.reshape(SEQS, SEQ_LEN, D)
    input_grad = input_grads.reshape(SEQS, SEQ_LEN, D)
    rms_stats = jnp.sqrt(stat_sums[:3] / (stat_sums[3] * D))
    return (output, input_grad, grad_sums[0], grad_sums[1], grad_sums[2], grad_sums[3], grad_sums[4], grad_sums[5], grad_sums[6], grad_sums[7], grad_sums[8], grad_sums[9], rms_stats)
```

```python
import functools

import jax
import jax.numpy as jnp
from jax import lax
from jax.experimental import pallas as pl
from jax.experimental.pallas import tpu as pltpu
from jax.sharding import Mesh
from jax.sharding import PartitionSpec as P

HEAD_DIM = 128
AXES = ("rep", "z", "x", "yl", "c")
SHARD = ("z", "x", "yl", "c")
ZXC = ("z", "x", "c")
Y4 = ("rep", "yl")
Y8 = ("rep", "yl", "c")
norm_eps = 1e-12
masked_score = -1e30
bf16 = jnp.bfloat16
f32 = jnp.float32
i32 = jnp.int32
MIB = 1 << 20
REP, ZZ, XX, YL, CC, LEN = range(6)


def shifted(by, count=4):
    return [(i, (i + by) % count) for i in range(count)]


def xored(by, count):
    return [(i, i ^ by) for i in range(count)]


def from_offset(value, axes, offset):
    return lax.ppermute(value, axes, shifted(-offset))


def to_core(value):
    return lax.ppermute(value, "c", xored(1, 2))


def y_gather(value):
    return [value] + [from_offset(value, Y4, d) for d in (1, 2, 3)]


def x_gather(value):
    return [value] + [from_offset(value, "x", d) for d in (1, 2, 3)]


def sum_parts(parts, axis):
    return [parts[0]] + [lax.ppermute(parts[d], axis, shifted(d)) for d in (1, 2, 3)]


def diagonal(value, to_z, by):
    pairs = []
    for rep in range(2):
        for yl in range(2):
            y = rep * 2 + yl
            at = lambda z: rep * 8 + (z % 4) * 2 + yl
            pairs.append((at(y), at(y + by)) if to_z else (at(y - by), at(y)))
    return lax.ppermute(value, ("rep", "z", "yl"), pairs)


def along_y(value, by):
    pairs = []
    for y in range(4):
        at = lambda v: ((v % 4) // 2) * 8 + y * 2 + v % 2
        pairs.append((at(y), at(y + by)))
    return lax.ppermute(value, ("rep", "z", "yl"), pairs)


def call(kernel, outs, operands, specs, out_specs, grid=(1,), scalars=(), scratch=(), vmem=28):
    return pl.pallas_call(
        kernel,
        grid_spec=pltpu.PrefetchScalarGridSpec(
            num_scalar_prefetch=len(scalars),
            grid=grid,
            in_specs=specs,
            out_specs=out_specs,
            scratch_shapes=scratch,
        ),
        out_shape=outs,
        compiler_params=pltpu.CompilerParams(vmem_limit_bytes=vmem * MIB),
        cost_estimate=pl.CostEstimate(flops=1000, bytes_accessed=1000, transcendentals=0),
    )(*scalars, *operands)


def out(shape, dtype=bf16):
    return jax.ShapeDtypeStruct(shape, dtype)


def whole(shape):
    return pl.BlockSpec(shape, lambda *_: (0,) * len(shape))


def swap_middle(value):
    width = value.shape[1]
    chunk = (lax.broadcasted_iota(i32, value.shape, 1) >> 5) & 3
    ahead = pltpu.roll(value, width - 32, 1)
    behind = pltpu.roll(value, 32, 1)
    return jnp.where(chunk == 1, ahead, jnp.where(chunk == 2, behind, value))


def swap_kernel(tok_ref, out_ref):
    out_ref[...] = swap_middle(tok_ref[...].astype(f32)).astype(bf16)


def prep_kernel(sp, wq_ref, wk_ref, wv_ref, up_ref, g1, s1, g2, s2, keep_ref, send_ref):
    rep, yl = sp[REP], sp[YL]
    s = yl * 2 + sp[CC]
    lane = lax.broadcasted_iota(i32, (1, 128), 1)
    rows = []
    for ref in (g1, s1, g2, s2):
        value = ref[...].astype(f32)
        tiled = jnp.concatenate([value, value, value, value], axis=1)
        rows.append(jnp.where((lane >> 5) == s, tiled, 0.0))
    rows.append(jnp.where(lane == s, sp[LEN].astype(f32), 0.0))
    vec = jnp.concatenate(rows + [jnp.zeros((27, 128), f32)], axis=0).astype(bf16)
    keep_ref[:, 3584:] = vec
    send_ref[:, 3584:] = vec
    for target, dest in ((yl, keep_ref), (1 - yl, send_ref)):
        for i, ref in enumerate((wq_ref, wk_ref, wv_ref)):
            start = pl.multiple_of((rep * 2 + target) * 512, 512)
            block = ref[:, pl.ds(start, 512)]
            for head in range(4):
                dest[:, (head * 3 + i) * 128 : (head * 3 + i + 1) * 128] = block[
                    :, head * 128 : (head + 1) * 128
                ]
        for zx in range(16):
            start = pl.multiple_of(zx * 512 + target * 256, 256)
            block = up_ref[:, pl.ds(start, 256)]
            low = jnp.concatenate([block[:, 0:64], block[:, 128:192]], axis=1)
            high = jnp.concatenate([block[:, 64:128], block[:, 192:256]], axis=1)
            dest[:, 1536 + zx * 128 : 1536 + (zx + 1) * 128] = jnp.where(rep == 0, low, high)


def qkv_piece_kernel(sp, keep_ref, got_ref, out_ref):
    own = pl.ds(pl.multiple_of(sp[YL] * 32, 32), 32)
    other = pl.ds(pl.multiple_of((1 - sp[YL]) * 32, 32), 32)
    out_ref[own, :1536] = keep_ref[:, :1536]
    out_ref[other, :1536] = got_ref[:, :1536]
    vec = (keep_ref[:, 3584:].astype(f32) + got_ref[:, 3584:].astype(f32)).astype(bf16)
    out_ref[0:32, 1536:] = vec
    out_ref[32:64, 1536:] = jnp.zeros_like(vec)


def mlp_piece_kernel(sp, keep_ref, got_ref, down_ref, after1_ref, after2_ref, out_ref):
    own = pl.ds(pl.multiple_of(sp[YL] * 32, 32), 32)
    other = pl.ds(pl.multiple_of((1 - sp[YL]) * 32, 32), 32)
    out_ref[0, own, :] = keep_ref[:, 1536:3584]
    out_ref[0, other, :] = got_ref[:, 1536:3584]
    out_ref[1] = down_ref[pl.ds(pl.multiple_of(sp[REP] * 64, 64), 64), :]


def cat_kernel(t0, t1, t2, t3, after_ref, out_ref):
    for d, ref in enumerate((t0, t1, t2, t3)):
        out_ref[d * 128 : (d + 1) * 128, :] = ref[...]


def out_rows_kernel(sp, own_ref, got_ref, out_ref):
    out_ref[pl.ds(pl.multiple_of(sp[YL] * 32, 32), 32), :] = own_ref[...]
    out_ref[pl.ds(pl.multiple_of((1 - sp[YL]) * 32, 32), 32), :] = got_ref[...]


def proj_kernel(sp, own_ref, other_ref, proj_ref):
    for d in range(4):
        for ref, core in ((own_ref, sp[CC]), (other_ref, 1 - sp[CC])):
            for yl_of in range(2):
                row = pl.multiple_of(((sp[XX] + d) & 3) * 128 + yl_of * 64 + core * 32, 32)
                proj_ref[pl.ds(row, 32), :] = ref[d, yl_of * 32 : (yl_of + 1) * 32, :]


def qkv_kernel(sp, tok_ref, w_ref, vec_in_ref, out_ref, vec_ref, len_ref):
    @pl.when(pl.program_id(0) == 0)
    def _():
        for zx in range(16):
            pair = vec_in_ref[2 * zx].astype(f32) + vec_in_ref[2 * zx + 1].astype(f32)
            vec_ref[:, zx * 128 : (zx + 1) * 128] = pair
        own = (sp[ZZ] * 4 + sp[XX]) * 2
        len_ref[...] = vec_in_ref[own].astype(f32) + vec_in_ref[own + 1].astype(f32)

    weights = w_ref[...].reshape(2048, 256)
    out_ref[...] = jnp.dot(tok_ref[...], weights, preferred_element_type=f32).astype(bf16)


def softmax_of(q, k, open_row):
    raw = lax.dot_general(q, k, (((1,), (1,)), ((), ())), preferred_element_type=f32)
    scores = jnp.where(open_row, raw * (HEAD_DIM**-0.5), masked_score)
    top = jnp.max(scores, axis=-1, keepdims=True)
    exponent = jnp.exp(scores - top)
    return exponent * (1.0 / jnp.sum(exponent, axis=-1, keepdims=True))


def open_keys(sp, lens):
    e, p = pl.program_id(0), pl.program_id(1)
    length = lens[((sp[YL] + p) & 1) * 2 + ((sp[CC] + e) & 1)]
    swap = ((sp[REP] * 2 + sp[YL] + p) & 3) >> 1
    lane = lax.broadcasted_iota(i32, (1, 256), 1)
    position = jnp.where(swap == 1, (lane + 128) & 255, lane)
    return position < length


def head_part(ref, head, i):
    return ref[0, :, 0, :, (head * 3 + i) * 128 : (head * 3 + i + 1) * 128].reshape(256, 128)


def attend_kernel(sp, lens, qkv_ref, ctx_ref):
    open_row = open_keys(sp, lens)
    for head in range(2):
        q, k, v = (head_part(qkv_ref, head, i) for i in range(3))
        probs = softmax_of(q, k, open_row).astype(bf16)
        ctx = jnp.dot(probs, v, preferred_element_type=f32).astype(bf16)
        ctx_ref[0, :, 0, :, head * 128 : (head + 1) * 128] = ctx.reshape(2, 128, 128)


def attend_back_kernel(sp, lens, qkv_ref, own_ref, other_ref, out_ref):
    open_row = open_keys(sp, lens)
    scale = HEAD_DIM**-0.5
    first = pl.program_id(0) == 0
    for head in range(2):
        q, k, v = (head_part(qkv_ref, head, i) for i in range(3))
        cols = slice(head * 128, (head + 1) * 128)
        grad = jnp.where(first, own_ref[:, 0, :, cols], other_ref[:, 0, :, cols]).reshape(256, 128)
        probs = softmax_of(q, k, open_row)
        grad_probs = lax.dot_general(grad, v, (((1,), (1,)), ((), ())), preferred_element_type=f32)
        inner = jnp.sum(probs * grad_probs, axis=-1, keepdims=True)
        grad_scores = (probs * (grad_probs - inner)).astype(bf16)
        grad_q = jnp.dot(grad_scores, k, preferred_element_type=f32) * scale
        over = (((0,), (0,)), ((), ()))
        grad_k = lax.dot_general(grad_scores, q, over, preferred_element_type=f32) * scale
        grad_v = lax.dot_general(probs.astype(bf16), grad, over, preferred_element_type=f32)
        for i, part in enumerate((grad_q, grad_k, grad_v)):
            out_ref[0, :, 0, :, (head * 3 + i) * 128 : (head * 3 + i + 1) * 128] = part.astype(
                bf16
            ).reshape(2, 128, 128)


def group_block(columns):
    return pl.BlockSpec((1, 2, 1, 128, columns), lambda e, p, *_: (e, 0, p, 0, 0))


def to_four(result, refs):
    for d, ref in enumerate(refs):
        ref[...] = result[d * 128 : (d + 1) * 128].astype(bf16)


def out_kernel(sp, own_ref, got_ref, proj_ref, ctx_ref, *refs):
    @pl.when(pl.program_id(0) == 0)
    def _():
        ctx_ref[:, pl.ds(pl.multiple_of(sp[CC] * 256, 256), 256)] = own_ref[0]
        ctx_ref[:, pl.ds(pl.multiple_of((1 - sp[CC]) * 256, 256), 256)] = got_ref[0]

    to_four(jnp.dot(ctx_ref[...], proj_ref[...], preferred_element_type=f32), refs)


def terms_of(refs):
    return sum(r[...].astype(f32) for r in refs[1:]) + refs[0][...].astype(f32)


def valid_rows(sp):
    position = sp[REP] * 128 + lax.broadcasted_iota(i32, (128, 1), 0)
    return (position < sp[LEN]).astype(f32)


def lane_of(values):
    lane = lax.broadcasted_iota(i32, (8, 128), 1)
    total = jnp.zeros((8, 128), f32)
    for i, value in enumerate(values):
        total = jnp.where(lane == i, value, total)
    return total


def normed(values):
    center = values - jnp.mean(values, axis=-1, keepdims=True)
    spread = jnp.mean(center * center, axis=-1, keepdims=True)
    scale = lax.rsqrt(spread + norm_eps)
    return center * scale, scale


def norm_one_kernel(sp, p0, p1, p2, p3, tok_ref, vec_ref, hidden_ref, norm_ref, scale_ref, stat_ref):
    attn = terms_of((p0, p1, p2, p3))
    resid = tok_ref[...].astype(f32) + attn
    norm, scale = normed(resid)
    hidden = norm * vec_ref[0:1, :] + vec_ref[1:2, :]
    hidden_ref[...] = swap_middle(hidden).astype(bf16)
    norm_ref[...] = norm
    scale_ref[...] = jnp.broadcast_to(scale, scale_ref.shape)
    valid = valid_rows(sp)
    stat_ref[...] = lane_of((jnp.sum(valid * (resid * resid)), jnp.sum(valid * (attn * attn))))


def norm_two_kernel(
    sp, p0, p1, p2, p3, norm_ref, vec_ref, cot_ref, stat_ref, out_ref, low_ref, grad_ref, vg_ref, st_ref
):
    mlp = terms_of((p0, p1, p2, p3))
    resid = norm_ref[...] * vec_ref[0:1, :] + vec_ref[1:2, :] + mlp
    norm, scale = normed(resid)
    out_ref[...] = (norm * vec_ref[2:3, :] + vec_ref[3:4, :]).astype(bf16)
    valid = valid_rows(sp)
    grad_out = cot_ref[...].astype(f32) * valid
    vg_ref[0:1, :] = jnp.sum(grad_out * norm, axis=0, keepdims=True)
    vg_ref[1:2, :] = jnp.sum(grad_out, axis=0, keepdims=True)
    e = grad_out * vec_ref[2:3, :]
    mean_e = jnp.mean(e, axis=-1, keepdims=True)
    mean_en = jnp.mean(e * norm, axis=-1, keepdims=True)
    grad = scale * (e - mean_e - norm * mean_en)
    grad_ref[...] = grad
    low_ref[...] = grad.astype(bf16)
    lane = lax.broadcasted_iota(i32, (8, 128), 1)
    more = jnp.where(lane == 2, jnp.sum(valid * (mlp * mlp)), jnp.sum(valid))
    st_ref[...] = jnp.where(lane < 2, stat_ref[...], more)


def norm_one_back_kernel(
    p0, p1, p2, p3, grad2_ref, norm_ref, scale_ref, vec_ref, low_ref, grad_ref, vg_ref
):
    grad = grad2_ref[...] + swap_middle(terms_of((p0, p1, p2, p3)))
    norm = norm_ref[...]
    vg_ref[0:1, :] = jnp.sum(grad * norm, axis=0, keepdims=True)
    vg_ref[1:2, :] = jnp.sum(grad, axis=0, keepdims=True)
    e = grad * vec_ref[0:1, :]
    mean_e = jnp.mean(e, axis=-1, keepdims=True)
    mean_en = jnp.mean(e * norm, axis=-1, keepdims=True)
    back = scale_ref[:, 0:1] * (e - mean_e - norm * mean_en)
    grad_ref[...] = back
    low_ref[...] = back.astype(bf16)


def last_kernel(p0, p1, p2, p3, grad_ref, out_ref):
    out_ref[...] = grad_ref[...] + swap_middle(terms_of((p0, p1, p2, p3)))


def join(refs, all_ref):
    @pl.when(pl.program_id(0) == 0)
    def _():
        for d, ref in enumerate(refs):
            all_ref[d * 128 : (d + 1) * 128, :] = ref[...]


def mlp_kernel(h0, h1, h2, h3, up_ref, down_ref, act_ref, slope_ref, all_ref, *rest):
    refs, total_ref = rest[:4], rest[4]
    join((h0, h1, h2, h3), all_ref)
    v = jnp.dot(all_ref[...], up_ref[...].reshape(2048, 512), preferred_element_type=f32)
    root = 0.7978845608028654
    square = v * v
    t = jnp.tanh(root * v * (1.0 + 0.044715 * square))
    half = 0.5 * (1.0 + t)
    act = (v * half).astype(bf16)
    act_ref[...] = act
    slope = half + 0.5 * v * (1.0 - t * t) * (root * (1.0 + 3 * 0.044715 * square))
    slope_ref[...] = slope.astype(bf16)
    down = down_ref[...].reshape(512, 2048)
    accumulate(jnp.dot(act, down, preferred_element_type=f32), total_ref, refs)


def accumulate(term, total_ref, refs):
    step, last = pl.program_id(0), pl.num_programs(0) - 1

    @pl.when(step == 0)
    def _():
        total_ref[...] = term

    @pl.when((step > 0) & (step < last))
    def _():
        total_ref[...] += term

    @pl.when(step == last)
    def _():
        to_four(total_ref[...] + term, refs)


BACK = (((1,), (1,)), ((), ()))
OVER = (((0,), (0,)), ((), ()))


def mlp_back_kernel(g0, g1, g2, g3, up_ref, down_ref, slope_ref, pre_ref, all_ref, *rest):
    refs, total_ref = rest[:4], rest[4]
    join((g0, g1, g2, g3), all_ref)
    down = down_ref[...].reshape(512, 2048)
    grad = lax.dot_general(all_ref[...], down, BACK, preferred_element_type=f32)
    pre = (grad * slope_ref[...].astype(f32)).astype(bf16)
    pre_ref[...] = pre
    up = up_ref[...].reshape(2048, 512)
    term = lax.dot_general(pre, up, BACK, preferred_element_type=f32)
    accumulate(term, total_ref, refs)


def mlp_terms_kernel(hidden_ref, pre_ref, act_ref, grad_ref, after_ref, out_ref):
    @pl.when(pl.program_id(0) == 0)
    def _():
        r = lax.dot_general(hidden_ref[...], pre_ref[...], OVER, preferred_element_type=f32)
        out_ref[...] = r.astype(bf16).reshape(out_ref.shape)

    @pl.when(pl.program_id(0) == 1)
    def _():
        r = lax.dot_general(act_ref[...], grad_ref[...], OVER, preferred_element_type=f32)
        out_ref[...] = r.astype(bf16).reshape(out_ref.shape)


def ctx_back_kernel(sp, g0, g1, g2, g3, proj_ref, own_ref, other_ref, all_ref):
    for d, ref in enumerate((g0, g1, g2, g3)):
        all_ref[d * 128 : (d + 1) * 128, :] = ref[...]
    for ref, core in ((own_ref, sp[CC]), (other_ref, 1 - sp[CC])):
        weights = proj_ref[pl.ds(pl.multiple_of(core * 256, 256), 256), :]
        ref[...] = lax.dot_general(
            all_ref[...], weights, BACK, preferred_element_type=f32
        ).astype(bf16)


def proj_terms_kernel(sp, ctx_ref, grad_ref, after_ref, mine_ref, send_ref, term_ref):
    term = lax.dot_general(ctx_ref[...], grad_ref[...], OVER, preferred_element_type=f32)
    term_ref[...] = term.astype(bf16)
    for d in range(4):
        for ref, core in ((mine_ref, sp[CC]), (send_ref, 1 - sp[CC])):
            for yl_of in range(2):
                row = pl.multiple_of(((sp[XX] + d) & 3) * 128 + yl_of * 64 + core * 32, 32)
                ref[d, yl_of * 32 : (yl_of + 1) * 32, :] = term_ref[pl.ds(row, 32), :]


def qkv_terms_kernel(sp, tok_ref, grad_ref, vg1_ref, vg2_ref, stat_ref, *rest):
    a_refs, b_refs, term_ref = rest[:4], rest[4:8], rest[8]
    term = lax.dot_general(tok_ref[...], grad_ref[...], OVER, preferred_element_type=f32)
    term_ref[...] = term.astype(bf16)
    dz = (pl.program_id(0) - sp[ZZ]) & 3
    for dx in range(4):
        start = pl.multiple_of(((sp[XX] + dx) & 3) * 128, 128)
        rows = pl.ds(start, 128)
        vec = [vg1_ref[0:2, rows], vg2_ref[0:2, rows], stat_ref[0:4]]
        vec = jnp.concatenate(vec + [jnp.zeros((8, 128), f32)], axis=0).astype(bf16)
        vec = jnp.concatenate([vec, jnp.zeros((16, 256), bf16)], axis=1)
        b_refs[dx][dz] = term_ref[rows, 384:]
        for k in range(4):

            @pl.when(dz == k)
            def _():
                a_refs[k][dx, 0:128, :] = term_ref[rows, :384]
                a_refs[k][dx, 128:144, :] = vec


def proj_add_kernel(mine_ref, got_ref, after_ref, *refs):
    for d, ref in enumerate(refs):
        ref[...] = (mine_ref[d].astype(f32) + got_ref[d].astype(f32)).astype(bf16)


def middle_kernel(*refs):
    a, b, proj = refs[0:4], refs[4:8], refs[8:12]
    outs = refs[13:]
    total = terms_of(a).astype(bf16)
    for d in range(4):
        outs[d][...] = total[d]
    total = terms_of(b).astype(bf16)
    for d in range(4):
        outs[4 + d][...] = total[d]
    outs[8][...] = terms_of(proj).astype(bf16)


def tok_back_kernel(sp, own_ref, got_ref, w_ref, after_ref, *rest):
    refs, cat_ref = rest[:4], rest[4]

    @pl.when(pl.program_id(0) == 0)
    def _():
        cat_ref[:, pl.ds(pl.multiple_of(sp[CC] * 768, 256), 768)] = own_ref[0]
        cat_ref[:, pl.ds(pl.multiple_of((1 - sp[CC]) * 768, 256), 768)] = got_ref[0]

    weights = w_ref[...].reshape(256, 1536)
    to_four(lax.dot_general(cat_ref[...], weights, BACK, preferred_element_type=f32), refs)


def pieces_kernel(sp, *refs):
    a, b, proj = refs[0:4], refs[4:8], refs[8:12]
    outs, near_ref, away_ref, sum_ref, proj_ref = refs[13:21], *refs[21:25]
    sum_ref[:, :384] = terms_of(a).astype(bf16)
    sum_ref[0:128, 384:] = terms_of(b).astype(bf16)
    sum_ref[128:144, 384:] = jnp.zeros((16, 384), bf16)
    for d in range(8):
        yl_of, c_of = sp[YL] ^ ((d >> 1) & 1), sp[CC] ^ (d & 1)
        row = pl.multiple_of(c_of * 64 + yl_of * 32, 32)
        outs[d][0:32, :] = sum_ref[pl.ds(row, 32), :]
        outs[d][32:48, :] = sum_ref[128:144, :]
    proj_ref[...] = terms_of(proj).astype(bf16)
    near_ref[...] = proj_ref[pl.ds(pl.multiple_of(sp[YL] * 32, 32), 32), :]
    away_ref[...] = proj_ref[pl.ds(pl.multiple_of((1 - sp[YL]) * 32, 32), 32), :]


def final_kernel(sp, *refs):
    me = sp[REP] * 4 + sp[YL] * 2 + sp[CC]
    pieces, near, given = refs[:8], refs[8], refs[9:12]
    q_ref, k_ref, v_ref, proj_ref, g1, s1, g2, s2, rms_ref = refs[12:]
    for d in range(8):
        column = pl.multiple_of((me ^ d) * 256, 256)
        for i, ref in enumerate((q_ref, k_ref, v_ref)):
            for head in range(2):
                ref[:, pl.ds(column + head * 128, 128)] = pieces[d][
                    0:32, (head * 3 + i) * 128 : (head * 3 + i + 1) * 128
                ].astype(f32)
    on_diagonal = sp[ZZ] == sp[REP] * 2 + sp[YL]
    proj_ref[...] = jnp.where(on_diagonal, near[...].astype(f32), terms_of(given))
    vec = sum(piece[32:48, :128].astype(f32) for piece in pieces)
    s = sp[YL] * 2 + sp[CC]
    own = jnp.where(s == 0, vec[:, 0:32], vec[:, 32:64])
    own = jnp.where(s == 2, vec[:, 64:96], own)
    own = jnp.where(s == 3, vec[:, 96:128], own)
    for i, ref in enumerate((g1, s1, g2, s2)):
        ref[...] = own[i : i + 1]
    rms_ref[...] = jnp.sqrt(vec[4:5] / (vec[4:5, 3:4] * 2048.0))


def mlp_split_kernel(sp, sum_ref, rep_ref, away_ref):
    rep_ref[0:32, :] = sum_ref[0, pl.ds(pl.multiple_of(sp[YL] * 32, 32), 32), :]
    rep_ref[32:96, :] = sum_ref[1]
    away_ref[...] = sum_ref[0, pl.ds(pl.multiple_of((1 - sp[YL]) * 32, 32), 32), :]


def final_mlp_kernel(sp, own_ref, yl_ref, rep_ref, both_ref, up_ref, down_ref):
    rep, yl = sp[REP], sp[YL]
    mine = own_ref[0, pl.ds(pl.multiple_of(yl * 32, 32), 32), :]
    first_rep, first_yl = rep == 0, yl == 0
    got = {(0, 0): mine, (0, 1): yl_ref[...], (1, 0): rep_ref[0:32], (1, 1): both_ref[...]}
    for yl_of in range(2):
        same = (yl == yl_of)
        near = jnp.where(same, got[0, 0], got[0, 1]).astype(f32)
        far = jnp.where(same, got[1, 0], got[1, 1]).astype(f32)
        low = jnp.where(first_rep, near, far)
        high = jnp.where(first_rep, far, near)
        for zx in range(16):
            for c in range(2):
                src = slice(zx * 128 + c * 64, zx * 128 + c * 64 + 64)
                at = zx * 512 + yl_of * 256 + c * 128
                up_ref[:, at : at + 128] = jnp.concatenate([low[:, src], high[:, src]], axis=1)
    own_rows = pl.ds(pl.multiple_of(rep * 64, 64), 64)
    far_rows = pl.ds(pl.multiple_of((1 - rep) * 64, 64), 64)
    down_ref[own_rows, :] = own_ref[1].astype(f32)
    down_ref[far_rows, :] = rep_ref[32:96].astype(f32)


def per_device(
    hidden_in,
    lengths,
    w_query,
    w_key,
    w_value,
    w_output,
    attn_gain,
    attn_shift,
    w_up,
    w_down,
    mlp_gain,
    mlp_shift,
    cotangent,
):
    rep, z, x, yl, c = (lax.axis_index(a) for a in AXES)
    s, y = yl * 2 + c, rep * 2 + yl
    any_place = pl.BlockSpec(memory_space=pl.ANY)
    tok = hidden_in.reshape(128, 2048)
    cot = cotangent.reshape(128, 2048)
    sp = jnp.stack([rep, z, x, yl, c, lengths[0], lengths[0], lengths[0]]).astype(i32)
    rows = whole((128, 2048))

    keep, send = call(
        prep_kernel,
        [out((32, 3712))] * 2,
        (
            w_query,
            w_key,
            w_value,
            w_up,
            *(v.reshape(1, 32) for v in (attn_gain, attn_shift, mlp_gain, mlp_shift)),
        ),
        [whole((32, 2048))] * 3 + [whole((32, 8192))] + [whole((1, 32))] * 4,
        [whole((32, 3712))] * 2,
        scalars=(sp,),
        vmem=60,
    )
    got = lax.ppermute(send, "yl", xored(1, 2))
    (qkv_piece,) = call(
        qkv_piece_kernel,
        [out((64, 1664))],
        (keep, got),
        [whole((32, 3712))] * 2,
        [whole((64, 1664))],
        scalars=(sp,),
        vmem=16,
    )
    qkv_w = lax.all_gather(qkv_piece, ZXC, axis=0)

    first_yl, on_diagonal = yl == 0, y == z
    out_got = lax.ppermute(w_output, "yl", xored(1, 2))
    (out_piece,) = call(
        out_rows_kernel,
        [out((64, 2048))],
        (w_output, out_got),
        [whole((32, 2048))] * 2,
        [whole((64, 2048))],
        scalars=(sp,),
        vmem=16,
    )
    spread = [diagonal(out_piece, True, by) for by in (1, 2, 3)]
    out_piece = jnp.where(on_diagonal, out_piece, spread[0] + spread[1] + spread[2])
    out_own = jnp.stack(x_gather(out_piece))
    block4 = whole((4, 64, 2048))
    (proj,) = call(
        proj_kernel,
        [out((512, 2048))],
        (out_own, to_core(out_own)),
        [block4, block4],
        [whole((512, 2048))],
        scalars=(sp,),
        vmem=16,
    )

    (tok_swapped,) = call(swap_kernel, [out((128, 2048))], (tok,), [rows], [rows], vmem=16)
    (tok_mine,) = call(
        cat_kernel,
        [out((512, 2048))],
        (*y_gather(tok_swapped), out_own),
        [rows] * 4 + [any_place],
        [whole((512, 2048))],
        vmem=16,
    )
    tok_all = jnp.concatenate([tok_mine, to_core(tok_mine)], axis=0)
    (mlp_piece,) = call(
        mlp_piece_kernel,
        [out((2, 64, 2048))],
        (keep, got, w_down, proj, tok_all),
        [whole((32, 3712))] * 2 + [whole((128, 2048)), any_place, any_place],
        [whole((2, 64, 2048))],
        scalars=(sp,),
        vmem=16,
    )
    mlp_w = lax.all_gather(mlp_piece, ZXC, axis=0)

    qkv_all, vecs, lens = call(
        qkv_kernel,
        [out((1024, 768)), out((16, 2048), f32), out((16, 128), f32)],
        (tok_all, qkv_w, qkv_w),
        [
            whole((1024, 2048)),
            pl.BlockSpec((32, 64, 256), lambda n, sp: (0, 0, sp[CC] * 3 + n)),
            pl.BlockSpec((32, 16, 128), lambda n, sp: (0, 0, 12)),
        ],
        [
            pl.BlockSpec((1024, 256), lambda n, sp: (0, n)),
            whole((16, 2048)),
            whole((16, 128)),
        ],
        grid=(3,),
        scalars=(sp,),
        vmem=60,
    )
    lens = lens[4, :4].astype(i32)
    qkv_all = qkv_all.reshape(2, 2, 2, 128, 768)
    (ctx_all,) = call(
        attend_kernel,
        [out((2, 2, 2, 128, 256))],
        (qkv_all,),
        [group_block(768)],
        [group_block(256)],
        grid=(2, 2),
        scalars=(sp, lens),
        vmem=16,
    )
    ctx_all = ctx_all.reshape(2, 512, 256)
    ctx_got = to_core(ctx_all)
    ctx, *attn_parts = call(
        out_kernel,
        [out((512, 512))] + [out((128, 2048))] * 4,
        (ctx_all, ctx_got, proj),
        [
            pl.BlockSpec((1, 512, 256), lambda n, sp: (0, 0, 0)),
            pl.BlockSpec((1, 512, 256), lambda n, sp: (1, 0, 0)),
            pl.BlockSpec((512, 512), lambda n, sp: (0, n)),
        ],
        [whole((512, 512))] + [pl.BlockSpec((128, 512), lambda n, sp: (0, n))] * 4,
        grid=(4,),
        scalars=(sp,),
    )
    attn_terms = sum_parts(attn_parts, Y4)
    vec_block = whole((16, 2048))
    hidden_low, norm_one, scale_one, stat_one = call(
        norm_one_kernel,
        [out((128, 2048)), out((128, 2048), f32), out((128, 128), f32), out((8, 128), f32)],
        (*attn_terms, tok, vecs),
        [rows] * 5 + [vec_block],
        [rows, rows, whole((128, 128)), whole((8, 128))],
        scalars=(sp,),
        vmem=16,
    )

    four = [rows] * 4
    column = pl.BlockSpec((512, 512), lambda n: (0, n))
    group = whole((512, 2048))
    up_block = pl.BlockSpec((32, 1, 64, 512), lambda n: (0, 0, 0, n))
    down_block = pl.BlockSpec((8, 1, 64, 2048), lambda n: (n, 1, 0, 0))
    total = pltpu.VMEM((512, 2048), f32)
    act, slope, hidden, *mlp_parts = call(
        mlp_kernel,
        [out((512, 2048))] * 3 + [out((128, 2048))] * 4,
        (*y_gather(hidden_low), mlp_w, mlp_w),
        four + [up_block, down_block],
        [column, column, group] + four,
        grid=(4,),
        scratch=[total],
        vmem=60,
    )
    output, grad_low, grad_two, vec_two, stats = call(
        norm_two_kernel,
        [
            out((128, 2048)),
            out((128, 2048)),
            out((128, 2048), f32),
            out((8, 2048), f32),
            out((8, 128), f32),
        ],
        (*sum_parts(mlp_parts, Y4), norm_one, vecs, cot, stat_one),
        four + [rows, vec_block, rows, whole((8, 128))],
        [rows, rows, rows, whole((8, 2048)), whole((8, 128))],
        scalars=(sp,),
        vmem=16,
    )

    pre_grad, grad_mlp, *hidden_parts = call(
        mlp_back_kernel,
        [out((512, 2048))] * 2 + [out((128, 2048))] * 4,
        (*y_gather(grad_low), mlp_w, mlp_w, slope),
        four + [up_block, down_block, column],
        [column, group] + four,
        grid=(4,),
        scratch=[total],
        vmem=60,
    )
    (mlp_terms,) = call(
        mlp_terms_kernel,
        [out((32, 2, 64, 2048))],
        (hidden, pre_grad, act, grad_mlp, hidden_parts[0]),
        [
            pl.BlockSpec((512, 512), lambda w, n: (0, jnp.where(w == 0, n, 3))),
            whole((512, 2048)),
            pl.BlockSpec((512, 512), lambda w, n: (0, jnp.where(w == 1, n, 0))),
            whole((512, 2048)),
            any_place,
        ],
        [pl.BlockSpec((8, 1, 64, 2048), lambda w, n: (n, w, 0, 0))],
        grid=(2, 4),
    )
    mlp_sum = lax.psum_scatter(mlp_terms, ZXC, scatter_dimension=0, tiled=True)
    mlp_sum = mlp_sum.reshape(2, 64, 2048)
    attn_low, grad_one, vec_one = call(
        norm_one_back_kernel,
        [out((128, 2048)), out((128, 2048), f32), out((8, 2048), f32)],
        (*sum_parts(hidden_parts, Y4), grad_two, norm_one, scale_one, vecs),
        four + [rows, rows, whole((128, 128)), vec_block],
        [rows, rows, whole((8, 2048))],
        vmem=16,
    )

    ctx_grad, ctx_grad_send, grad_attn = call(
        ctx_back_kernel,
        [out((512, 256)), out((512, 256)), out((512, 2048))],
        (*y_gather(attn_low), proj),
        four + [whole((512, 2048))],
        [whole((512, 256)), whole((512, 256)), whole((512, 2048))],
        scalars=(sp,),
        vmem=16,
    )
    ctx_grad_got = to_core(ctx_grad_send)
    half_block = pl.BlockSpec((2, 1, 128, 256), lambda e, p, *_: (0, p, 0, 0))
    (qkv_grad,) = call(
        attend_back_kernel,
        [out((2, 2, 2, 128, 768))],
        (qkv_all, ctx_grad.reshape(2, 2, 128, 256), ctx_grad_got.reshape(2, 2, 128, 256)),
        [group_block(768), half_block, half_block],
        [group_block(768)],
        grid=(2, 2),
        scalars=(sp, lens),
        vmem=16,
    )
    qkv_grad = qkv_grad.reshape(2, 512, 768)
    qkv_grad_got = to_core(qkv_grad)

    step_vec = pl.BlockSpec((8, 512), lambda n, sp: (0, n))
    blocks = call(
        qkv_terms_kernel,
        [out((4, 144, 384))] * 4 + [out((4, 128, 384))] * 4,
        (tok_all, qkv_grad.reshape(1024, 768), vec_one, vec_two, stats),
        [
            pl.BlockSpec((1024, 512), lambda n, sp: (0, n)),
            whole((1024, 768)),
            step_vec,
            step_vec,
            whole((8, 128)),
        ],
        [whole((4, 144, 384))] * 4 + [whole((4, 128, 384))] * 4,
        grid=(4,),
        scalars=(sp,),
        scratch=[pltpu.VMEM((512, 768), bf16)],
    )
    proj_block = pl.BlockSpec((4, 64, 512), lambda n, sp: (0, 0, n))
    proj_terms, proj_send = call(
        proj_terms_kernel,
        [out((4, 64, 2048))] * 2,
        (ctx, grad_attn, blocks[0]),
        [whole((512, 512)), pl.BlockSpec((512, 512), lambda n, sp: (0, n)), any_place],
        [proj_block, proj_block],
        grid=(4,),
        scalars=(sp,),
        scratch=[pltpu.VMEM((512, 512), bf16)],
    )
    tok_parts = call(
        tok_back_kernel,
        [out((128, 2048))] * 4,
        (qkv_grad, qkv_grad_got, qkv_w, blocks[0]),
        [
            pl.BlockSpec((1, 512, 768), lambda n, sp: (0, 0, 0)),
            pl.BlockSpec((1, 512, 768), lambda n, sp: (1, 0, 0)),
            pl.BlockSpec((4, 64, 1536), lambda n, sp: (n, 0, 0)),
            any_place,
        ],
        [pl.BlockSpec((128, 256), lambda n, sp: (0, n))] * 4,
        grid=(8,),
        scalars=(sp,),
        scratch=[pltpu.VMEM((512, 1536), bf16)],
    )
    (input_grad,) = call(
        last_kernel,
        [out((128, 2048), f32)],
        (*sum_parts(tok_parts, Y4), grad_one),
        four + [rows],
        [rows],
        vmem=16,
    )

    proj_parts = call(
        proj_add_kernel,
        [out((64, 2048))] * 4,
        (proj_terms, to_core(proj_send), tok_parts[0]),
        [block4, block4, any_place],
        [whole((64, 2048))] * 4,
        vmem=16,
    )
    middle = call(
        middle_kernel,
        [out((144, 384))] * 4 + [out((128, 384))] * 4 + [out((64, 2048))],
        (
            *sum_parts(blocks[:4], "z"),
            *sum_parts(blocks[4:], "x"),
            *sum_parts(proj_parts, "x"),
            input_grad,
        ),
        [whole((4, 144, 384))] * 4
        + [whole((4, 128, 384))] * 4
        + [whole((64, 2048))] * 4
        + [any_place],
        [whole((144, 384))] * 4 + [whole((128, 384))] * 4 + [whole((64, 2048))],
        vmem=16,
    )
    rep_part, up_away = call(
        mlp_split_kernel,
        [out((96, 2048)), out((32, 2048))],
        (mlp_sum,),
        [whole((2, 64, 2048))],
        [whole((96, 2048)), whole((32, 2048))],
        scalars=(sp,),
        vmem=16,
    )
    grad_up, grad_down = call(
        final_mlp_kernel,
        [out((32, 8192), f32), out((128, 2048), f32)],
        (
            mlp_sum,
            lax.ppermute(up_away, Y4, xored(1, 4)),
            lax.ppermute(rep_part, Y4, xored(2, 4)),
            lax.ppermute(up_away, Y4, xored(3, 4)),
        ),
        [whole((2, 64, 2048)), whole((32, 2048)), whole((96, 2048)), whole((32, 2048))],
        [whole((32, 8192)), whole((128, 2048))],
        scalars=(sp,),
        vmem=16,
    )
    *pieces, near, away = call(
        pieces_kernel,
        [out((48, 768))] * 8 + [out((32, 2048))] * 2,
        (
            *sum_parts(middle[:4], "x"),
            *sum_parts(middle[4:8], "z"),
            middle[8],
            *(diagonal(middle[8], False, by) for by in (1, 2, 3)),
            grad_down,
        ),
        [whole((144, 384))] * 4
        + [whole((128, 384))] * 4
        + [whole((64, 2048))] * 4
        + [any_place],
        [whole((48, 768))] * 8 + [whole((32, 2048))] * 2,
        scalars=(sp,),
        scratch=[pltpu.VMEM((144, 768), bf16), pltpu.VMEM((64, 2048), bf16)],
        vmem=16,
    )
    arrived = [pieces[0]] + [lax.ppermute(pieces[d], Y8, xored(d, 8)) for d in range(1, 8)]
    given = [along_y(away, 1), along_y(near, 2), along_y(away, 3)]
    one_row = whole((1, 32))
    grad_q, grad_k, grad_v, grad_proj, g1, s1, g2, s2, rms = call(
        final_kernel,
        [out((32, 2048), f32)] * 4 + [out((1, 32), f32)] * 4 + [out((1, 128), f32)],
        (*arrived, near, *given),
        [whole((48, 768))] * 8 + [whole((32, 2048))] * 4,
        [whole((32, 2048))] * 4 + [one_row] * 4 + [whole((1, 128))],
        scalars=(sp,),
        vmem=16,
    )
    vec_mine = [v.reshape(32) for v in (g1, s1, g2, s2)]
    rms_stats = rms[0, :3]
    return (
        output.reshape(1, 128, 2048),
        input_grad.reshape(1, 128, 2048),
        grad_q,
        grad_k,
        grad_v,
        grad_proj,
        vec_mine[0],
        vec_mine[1],
        grad_up,
        grad_down,
        vec_mine[2],
        vec_mine[3],
        rms_stats,
    )


def solution(mesh):
    split = Mesh(mesh.devices.reshape(2, 4, 4, 2, 2), AXES)
    rows, vec, seq = P(SHARD, None), P(SHARD), P(SHARD, "rep", None)
    return jax.shard_map(
        per_device,
        mesh=split,
        in_specs=(seq, vec, rows, rows, rows, rows, vec, vec, rows, rows, vec, vec, seq),
        out_specs=(seq, seq, rows, rows, rows, rows, vec, vec, rows, rows, vec, vec, P()),
        check_vma=False,
    )
```

```python
import functools

import jax
import jax.numpy as jnp
from jax import lax
from jax.experimental import pallas as pl
from jax.experimental.pallas import tpu as pltpu
from jax.sharding import Mesh
from jax.sharding import PartitionSpec as P

HEAD_DIM = 128
AXES = ("rep", "z", "x", "yl", "c")
SHARD = ("z", "x", "yl", "c")
ZXC = ("z", "x", "c")
Y4 = ("rep", "yl")
Y8 = ("rep", "yl", "c")
norm_eps = 1e-12
masked_score = -1e30
bf16 = jnp.bfloat16
f32 = jnp.float32
i32 = jnp.int32
MIB = 1 << 20
REP, ZZ, XX, YL, CC, LEN = range(6)


def shifted(by, count=4):
    return [(i, (i + by) % count) for i in range(count)]


def xored(by, count):
    return [(i, i ^ by) for i in range(count)]


def from_offset(value, axes, offset):
    return lax.ppermute(value, axes, shifted(-offset))


def to_core(value):
    return lax.ppermute(value, "c", xored(1, 2))


def y_gather(value):
    return [value] + [from_offset(value, Y4, d) for d in (1, 2, 3)]


def x_gather(value):
    return [value] + [from_offset(value, "x", d) for d in (1, 2, 3)]


def sum_parts(parts, axis):
    return [parts[0]] + [lax.ppermute(parts[d], axis, shifted(d)) for d in (1, 2, 3)]


def diagonal(value, to_z, by):
    pairs = []
    for rep in range(2):
        for yl in range(2):
            y = rep * 2 + yl
            at = lambda z: rep * 8 + (z % 4) * 2 + yl
            pairs.append((at(y), at(y + by)) if to_z else (at(y - by), at(y)))
    return lax.ppermute(value, ("rep", "z", "yl"), pairs)


def along_y(value, by):
    pairs = []
    for y in range(4):
        at = lambda v: ((v % 4) // 2) * 8 + y * 2 + v % 2
        pairs.append((at(y), at(y + by)))
    return lax.ppermute(value, ("rep", "z", "yl"), pairs)


def call(kernel, outs, operands, specs, out_specs, grid=(1,), scalars=(), scratch=(), vmem=28, cost=1000):
    return pl.pallas_call(
        kernel,
        grid_spec=pltpu.PrefetchScalarGridSpec(
            num_scalar_prefetch=len(scalars),
            grid=grid,
            in_specs=specs,
            out_specs=out_specs,
            scratch_shapes=scratch,
        ),
        out_shape=outs,
        compiler_params=pltpu.CompilerParams(vmem_limit_bytes=vmem * MIB),
        cost_estimate=pl.CostEstimate(flops=cost, bytes_accessed=1000, transcendentals=0),
    )(*scalars, *operands)


def call_resident(kernel, outs, operands, weights, vmem=14):
    place = pl.BlockSpec(memory_space=pltpu.VMEM)
    held = [pltpu.with_memory_space_constraint(w, pltpu.VMEM) for w in weights]
    return pl.pallas_call(
        kernel,
        in_specs=[place] * (len(operands) - 1)
        + [pl.BlockSpec(memory_space=pl.ANY)]
        + [place] * len(weights),
        out_specs=[place] * len(outs),
        out_shape=outs,
        compiler_params=pltpu.CompilerParams(vmem_limit_bytes=vmem * MIB),
        cost_estimate=pl.CostEstimate(flops=1000, bytes_accessed=1000, transcendentals=0),
    )(*operands, *held)


def load_kernel(w_ref, up_ref, down_ref, sem):
    copies = [
        pltpu.make_async_copy(w_ref.at[:, i], ref, sem.at[i])
        for i, ref in enumerate((up_ref, down_ref))
    ]
    for copy in copies:
        copy.start()
    for copy in copies:
        copy.wait()


def load_weights(weights):
    return pl.pallas_call(
        load_kernel,
        in_specs=[pl.BlockSpec(memory_space=pl.ANY)],
        out_specs=[pl.BlockSpec(memory_space=pltpu.VMEM)] * 2,
        out_shape=[pltpu.VMEM((32, 64, 2048), bf16)] * 2,
        scratch_shapes=[pltpu.SemaphoreType.DMA((2,))],
        compiler_params=pltpu.CompilerParams(vmem_limit_bytes=4 * MIB),
        cost_estimate=pl.CostEstimate(flops=1000, bytes_accessed=1000, transcendentals=0),
    )(pltpu.with_memory_space_constraint(weights, pltpu.HBM))


def out(shape, dtype=bf16):
    return jax.ShapeDtypeStruct(shape, dtype)


def whole(shape):
    return pl.BlockSpec(shape, lambda *_: (0,) * len(shape))


def swap_middle(value):
    width = value.shape[1]
    chunk = (lax.broadcasted_iota(i32, value.shape, 1) >> 5) & 3
    ahead = pltpu.roll(value, width - 32, 1)
    behind = pltpu.roll(value, 32, 1)
    return jnp.where(chunk == 1, ahead, jnp.where(chunk == 2, behind, value))


def swap_kernel(tok_ref, out_ref):
    out_ref[...] = swap_middle(tok_ref[...].astype(f32)).astype(bf16)


def prep_kernel(sp, wq_ref, wk_ref, wv_ref, up_ref, g1, s1, g2, s2, keep_ref, send_ref):
    rep, yl = sp[REP], sp[YL]
    s = yl * 2 + sp[CC]
    lane = lax.broadcasted_iota(i32, (1, 128), 1)
    rows = []
    for ref in (g1, s1, g2, s2):
        value = ref[...].astype(f32)
        tiled = jnp.concatenate([value, value, value, value], axis=1)
        rows.append(jnp.where((lane >> 5) == s, tiled, 0.0))
    rows.append(jnp.where(lane == s, sp[LEN].astype(f32), 0.0))
    vec = jnp.concatenate(rows + [jnp.zeros((27, 128), f32)], axis=0).astype(bf16)
    keep_ref[:, 3584:] = vec
    send_ref[:, 3584:] = vec
    for target, dest in ((yl, keep_ref), (1 - yl, send_ref)):
        for i, ref in enumerate((wq_ref, wk_ref, wv_ref)):
            start = pl.multiple_of((rep * 2 + target) * 512, 512)
            block = ref[:, pl.ds(start, 512)]
            for head in range(4):
                dest[:, (head * 3 + i) * 128 : (head * 3 + i + 1) * 128] = block[
                    :, head * 128 : (head + 1) * 128
                ]
        for zx in range(16):
            start = pl.multiple_of(zx * 512 + target * 256, 256)
            block = up_ref[:, pl.ds(start, 256)]
            low = jnp.concatenate([block[:, 0:64], block[:, 128:192]], axis=1)
            high = jnp.concatenate([block[:, 64:128], block[:, 192:256]], axis=1)
            dest[:, 1536 + zx * 128 : 1536 + (zx + 1) * 128] = jnp.where(rep == 0, low, high)


def qkv_piece_kernel(sp, keep_ref, got_ref, out_ref):
    own = pl.ds(pl.multiple_of(sp[YL] * 32, 32), 32)
    other = pl.ds(pl.multiple_of((1 - sp[YL]) * 32, 32), 32)
    out_ref[own, :1536] = keep_ref[:, :1536]
    out_ref[other, :1536] = got_ref[:, :1536]
    vec = (keep_ref[:, 3584:].astype(f32) + got_ref[:, 3584:].astype(f32)).astype(bf16)
    out_ref[0:32, 1536:] = vec
    out_ref[32:64, 1536:] = jnp.zeros_like(vec)


def mlp_piece_kernel(sp, keep_ref, got_ref, down_ref, after1_ref, after2_ref, out_ref):
    own = pl.ds(pl.multiple_of(sp[YL] * 32, 32), 32)
    other = pl.ds(pl.multiple_of((1 - sp[YL]) * 32, 32), 32)
    out_ref[0, own, :] = keep_ref[:, 1536:3584]
    out_ref[0, other, :] = got_ref[:, 1536:3584]
    out_ref[1] = down_ref[pl.ds(pl.multiple_of(sp[REP] * 64, 64), 64), :]


def cat_kernel(t0, t1, t2, t3, after_ref, out_ref):
    for d, ref in enumerate((t0, t1, t2, t3)):
        out_ref[d * 128 : (d + 1) * 128, :] = ref[...]


def out_rows_kernel(sp, own_ref, got_ref, out_ref):
    out_ref[pl.ds(pl.multiple_of(sp[YL] * 32, 32), 32), :] = own_ref[...]
    out_ref[pl.ds(pl.multiple_of((1 - sp[YL]) * 32, 32), 32), :] = got_ref[...]


def proj_kernel(sp, own_ref, other_ref, proj_ref):
    for d in range(4):
        for ref, core in ((own_ref, sp[CC]), (other_ref, 1 - sp[CC])):
            for yl_of in range(2):
                row = pl.multiple_of(((sp[XX] + d) & 3) * 128 + yl_of * 64 + core * 32, 32)
                proj_ref[pl.ds(row, 32), :] = ref[d, yl_of * 32 : (yl_of + 1) * 32, :]


def qkv_kernel(sp, tok_ref, w_ref, vec_in_ref, out_ref, vec_ref, len_ref):
    @pl.when(pl.program_id(0) == 0)
    def _():
        for zx in range(16):
            pair = vec_in_ref[2 * zx].astype(f32) + vec_in_ref[2 * zx + 1].astype(f32)
            vec_ref[:, zx * 128 : (zx + 1) * 128] = pair
        own = (sp[ZZ] * 4 + sp[XX]) * 2
        len_ref[...] = vec_in_ref[own].astype(f32) + vec_in_ref[own + 1].astype(f32)

    weights = w_ref[...].reshape(2048, 256)
    out_ref[...] = jnp.dot(tok_ref[...], weights, preferred_element_type=f32).astype(bf16)


def softmax_of(q, k, open_row):
    raw = lax.dot_general(q, k, (((1,), (1,)), ((), ())), preferred_element_type=f32)
    scores = jnp.where(open_row, raw * (HEAD_DIM**-0.5), masked_score)
    top = jnp.max(scores, axis=-1, keepdims=True)
    exponent = jnp.exp(scores - top)
    return exponent * (1.0 / jnp.sum(exponent, axis=-1, keepdims=True))


def open_keys(sp, lens):
    e, p = pl.program_id(0), pl.program_id(1)
    length = lens[((sp[YL] + p) & 1) * 2 + ((sp[CC] + e) & 1)]
    swap = ((sp[REP] * 2 + sp[YL] + p) & 3) >> 1
    lane = lax.broadcasted_iota(i32, (1, 256), 1)
    position = jnp.where(swap == 1, (lane + 128) & 255, lane)
    return position < length


def head_part(ref, head, i):
    return ref[0, :, 0, :, (head * 3 + i) * 128 : (head * 3 + i + 1) * 128].reshape(256, 128)


def attend_kernel(sp, lens, qkv_ref, ctx_ref):
    open_row = open_keys(sp, lens)
    for head in range(2):
        q, k, v = (head_part(qkv_ref, head, i) for i in range(3))
        probs = softmax_of(q, k, open_row).astype(bf16)
        ctx = jnp.dot(probs, v, preferred_element_type=f32).astype(bf16)
        ctx_ref[0, :, 0, :, head * 128 : (head + 1) * 128] = ctx.reshape(2, 128, 128)


def attend_back_kernel(sp, lens, qkv_ref, own_ref, other_ref, out_ref):
    open_row = open_keys(sp, lens)
    scale = HEAD_DIM**-0.5
    first = pl.program_id(0) == 0
    for head in range(2):
        q, k, v = (head_part(qkv_ref, head, i) for i in range(3))
        cols = slice(head * 128, (head + 1) * 128)
        grad = jnp.where(first, own_ref[:, 0, :, cols], other_ref[:, 0, :, cols]).reshape(256, 128)
        probs = softmax_of(q, k, open_row)
        grad_probs = lax.dot_general(grad, v, (((1,), (1,)), ((), ())), preferred_element_type=f32)
        inner = jnp.sum(probs * grad_probs, axis=-1, keepdims=True)
        grad_scores = (probs * (grad_probs - inner)).astype(bf16)
        grad_q = jnp.dot(grad_scores, k, preferred_element_type=f32) * scale
        over = (((0,), (0,)), ((), ()))
        grad_k = lax.dot_general(grad_scores, q, over, preferred_element_type=f32) * scale
        grad_v = lax.dot_general(probs.astype(bf16), grad, over, preferred_element_type=f32)
        for i, part in enumerate((grad_q, grad_k, grad_v)):
            out_ref[0, :, 0, :, (head * 3 + i) * 128 : (head * 3 + i + 1) * 128] = part.astype(
                bf16
            ).reshape(2, 128, 128)


def group_block(columns):
    return pl.BlockSpec((1, 2, 1, 128, columns), lambda e, p, *_: (e, 0, p, 0, 0))


def to_four(result, refs):
    rows = result.shape[0] // len(refs)
    for d, ref in enumerate(refs):
        ref[...] = result[d * rows : (d + 1) * rows].astype(bf16)


def out_kernel(sp, own_ref, got_ref, proj_ref, ctx_ref, *refs):
    @pl.when(pl.program_id(0) == 0)
    def _():
        ctx_ref[:, pl.ds(pl.multiple_of(sp[CC] * 256, 256), 256)] = own_ref[0]
        ctx_ref[:, pl.ds(pl.multiple_of((1 - sp[CC]) * 256, 256), 256)] = got_ref[0]

    to_four(jnp.dot(ctx_ref[...], proj_ref[...], preferred_element_type=f32), refs)


def terms_of(refs):
    return sum(r[...].astype(f32) for r in refs[1:]) + refs[0][...].astype(f32)


def valid_rows(sp, half):
    position = sp[REP] * 128 + half * 64 + lax.broadcasted_iota(i32, (64, 1), 0)
    return (position < sp[LEN]).astype(f32)


def lane_of(values):
    lane = lax.broadcasted_iota(i32, (8, 128), 1)
    total = jnp.zeros((8, 128), f32)
    for i, value in enumerate(values):
        total = jnp.where(lane == i, value, total)
    return total


def normed(values):
    center = values - jnp.mean(values, axis=-1, keepdims=True)
    spread = jnp.mean(center * center, axis=-1, keepdims=True)
    scale = lax.rsqrt(spread + norm_eps)
    return center * scale, scale


def norm_one_kernel(half, sp, p0, p1, p2, p3, tok_ref, vec_ref, hidden_ref, norm_ref, scale_ref, stat_ref):
    attn = terms_of((p0, p1, p2, p3))
    resid = tok_ref[...].astype(f32) + attn
    norm, scale = normed(resid)
    hidden = norm * vec_ref[0:1, :] + vec_ref[1:2, :]
    hidden_ref[...] = swap_middle(hidden).astype(bf16)
    norm_ref[...] = norm
    scale_ref[...] = jnp.broadcast_to(scale, scale_ref.shape)
    valid = valid_rows(sp, half)
    stat_ref[...] = lane_of((jnp.sum(valid * (resid * resid)), jnp.sum(valid * (attn * attn))))


def norm_two_kernel(
    half, sp, p0, p1, p2, p3, norm_ref, vec_ref, cot_ref, stat_ref, out_ref, low_ref, grad_ref, vg_ref, st_ref
):
    mlp = terms_of((p0, p1, p2, p3))
    resid = norm_ref[...] * vec_ref[0:1, :] + vec_ref[1:2, :] + mlp
    norm, scale = normed(resid)
    out_ref[...] = (norm * vec_ref[2:3, :] + vec_ref[3:4, :]).astype(bf16)
    valid = valid_rows(sp, half)
    grad_out = cot_ref[...].astype(f32) * valid
    vg_ref[0:1, :] = jnp.sum(grad_out * norm, axis=0, keepdims=True)
    vg_ref[1:2, :] = jnp.sum(grad_out, axis=0, keepdims=True)
    e = grad_out * vec_ref[2:3, :]
    mean_e = jnp.mean(e, axis=-1, keepdims=True)
    mean_en = jnp.mean(e * norm, axis=-1, keepdims=True)
    grad = scale * (e - mean_e - norm * mean_en)
    grad_ref[...] = grad
    low_ref[...] = grad.astype(bf16)
    lane = lax.broadcasted_iota(i32, (8, 128), 1)
    more = jnp.where(lane == 2, jnp.sum(valid * (mlp * mlp)), jnp.sum(valid))
    st_ref[...] = jnp.where(lane < 2, stat_ref[...], more)


def norm_one_back_kernel(
    p0, p1, p2, p3, grad2_ref, norm_ref, scale_ref, vec_ref, after_ref, low_ref, grad_ref, vg_ref
):
    grad = grad2_ref[...] + swap_middle(terms_of((p0, p1, p2, p3)))
    norm = norm_ref[...]
    vg_ref[0:1, :] = jnp.sum(grad * norm, axis=0, keepdims=True)
    vg_ref[1:2, :] = jnp.sum(grad, axis=0, keepdims=True)
    e = grad * vec_ref[0:1, :]
    mean_e = jnp.mean(e, axis=-1, keepdims=True)
    mean_en = jnp.mean(e * norm, axis=-1, keepdims=True)
    back = scale_ref[:, 0:1] * (e - mean_e - norm * mean_en)
    grad_ref[...] = back
    low_ref[...] = back.astype(bf16)


def last_kernel(p0, p1, p2, p3, grad_a_ref, grad_b_ref, out_ref, mark_ref):
    mark_ref[...] = jnp.zeros_like(mark_ref)
    total = swap_middle(terms_of((p0, p1, p2, p3)))
    out_ref[0:64, :] = grad_a_ref[...] + total[0:64]
    out_ref[64:128, :] = grad_b_ref[...] + total[64:128]


CHUNKS = [slice(i * 512, (i + 1) * 512) for i in range(4)]
UNITS = [slice(i * 8, (i + 1) * 8) for i in range(4)]


def join(refs, all_ref):
    for d, ref in enumerate(refs):
        all_ref[d * 64 : (d + 1) * 64, :] = ref[...]


def split_rows(result, refs, columns):
    for d, ref in enumerate(refs):
        ref[:, columns] = result[d * 64 : (d + 1) * 64].astype(bf16)


def mlp_kernel(
    h0, h1, h2, h3, after_ref, up_ref, down_ref, act_ref, slope_ref, all_ref, mark_ref, *refs
):
    mark_ref[...] = jnp.zeros_like(mark_ref)
    join((h0, h1, h2, h3), all_ref)
    root = 0.7978845608028654
    for chunk in CHUNKS:
        up = up_ref[:, :, chunk].reshape(2048, 512)
        v = jnp.dot(all_ref[...], up, preferred_element_type=f32)
        square = v * v
        t = jnp.tanh(root * v * (1.0 + 0.044715 * square))
        half = 0.5 * (1.0 + t)
        act_ref[:, chunk] = (v * half).astype(bf16)
        slope = half + 0.5 * v * (1.0 - t * t) * (root * (1.0 + 3 * 0.044715 * square))
        slope_ref[:, chunk] = slope.astype(bf16)
    for chunk in CHUNKS:
        down = down_ref[:, :, chunk].reshape(2048, 512)
        split_rows(jnp.dot(act_ref[...], down, preferred_element_type=f32), refs, chunk)


BACK = (((1,), (1,)), ((), ()))
OVER = (((0,), (0,)), ((), ()))


def mlp_back_kernel(
    g0, g1, g2, g3, slope_ref, after_ref, up_ref, down_ref, pre_ref, all_ref, mark_ref, *refs
):
    mark_ref[...] = jnp.zeros_like(mark_ref)
    join((g0, g1, g2, g3), all_ref)
    for chunk, units in zip(CHUNKS, UNITS):
        down = down_ref[units].reshape(512, 2048)
        grad = lax.dot_general(all_ref[...], down, BACK, preferred_element_type=f32)
        pre_ref[:, chunk] = (grad * slope_ref[:, chunk].astype(f32)).astype(bf16)
    for chunk, units in zip(CHUNKS, UNITS):
        up = up_ref[units].reshape(512, 2048)
        term = lax.dot_general(pre_ref[...], up, BACK, preferred_element_type=f32)
        split_rows(term, refs, chunk)


def mlp_terms_kernel(h0, h1, p0, p1, a0, a1, g0, g1, after_ref, out_ref, mark_ref):
    mark_ref[...] = jnp.zeros_like(mark_ref)

    def both(left, right):
        total = sum(
            lax.dot_general(l[...], r[...], OVER, preferred_element_type=f32)
            for l, r in zip(left, right)
        )
        out_ref[...] = total.astype(bf16).reshape(out_ref.shape)

    @pl.when(pl.program_id(0) == 0)
    def _():
        both((h0, h1), (p0, p1))

    @pl.when(pl.program_id(0) == 1)
    def _():
        both((a0, a1), (g0, g1))


def ctx_back_kernel(sp, *refs):
    proj_ref, own_ref, other_ref, all_ref = refs[8:]
    for i, ref in enumerate(refs[:8]):
        row = (i % 4) * 128 + (i // 4) * 64
        all_ref[row : row + 64, :] = ref[...]
    for ref, core in ((own_ref, sp[CC]), (other_ref, 1 - sp[CC])):
        weights = proj_ref[pl.ds(pl.multiple_of(core * 256, 256), 256), :]
        ref[...] = lax.dot_general(
            all_ref[...], weights, BACK, preferred_element_type=f32
        ).astype(bf16)


def proj_terms_kernel(sp, ctx_ref, grad_ref, mine_ref, send_ref, term_ref):
    term = lax.dot_general(ctx_ref[...], grad_ref[...], OVER, preferred_element_type=f32)
    term_ref[...] = term.astype(bf16)
    for d in range(4):
        for ref, core in ((mine_ref, sp[CC]), (send_ref, 1 - sp[CC])):
            for yl_of in range(2):
                row = pl.multiple_of(((sp[XX] + d) & 3) * 128 + yl_of * 64 + core * 32, 32)
                ref[d, yl_of * 32 : (yl_of + 1) * 32, :] = term_ref[pl.ds(row, 32), :]


def qkv_terms_kernel(
    sp, tok_ref, grad_ref, v1a, v1b, v2a, v2b, sta, stb, mine_ref, got_ref, after_ref, *rest
):
    a_refs, b_refs, term_ref = rest[:4], rest[4:8], rest[8]
    term = lax.dot_general(tok_ref[...], grad_ref[...], OVER, preferred_element_type=f32)
    term_ref[...] = term.astype(bf16)
    step = pl.program_id(0)
    dz = (step - sp[ZZ]) & 3
    for dx in range(4):
        start = pl.multiple_of(((sp[XX] + dx) & 3) * 128, 128)
        rows = pl.ds(start, 128)
        vec = [v1a[0:2, rows] + v1b[0:2, rows], v2a[0:2, rows] + v2b[0:2, rows]]
        vec += [sta[0:4] + stb[0:4]]
        vec = jnp.concatenate(vec + [jnp.zeros((8, 128), f32)], axis=0).astype(bf16)
        vec = jnp.concatenate([vec, jnp.zeros((16, 384), bf16)], axis=1)
        for j in range(2):
            at = pl.multiple_of((dz * 2 + j) * 128, 128)
            b_refs[dx][pl.ds(at, 128), :] = term_ref[rows, 512 + j * 128 : 640 + j * 128]
        total = mine_ref[dx].astype(f32) + got_ref[dx].astype(f32)
        total = total.astype(bf16)
        for j in range(4):
            at = pl.multiple_of(1024 + (step * 4 + j) * 64, 64)
            b_refs[dx][pl.ds(at, 64), :] = total[:, j * 128 : (j + 1) * 128]
        for k in range(4):

            @pl.when(dz == k)
            def _():
                a_refs[k][(sp[XX] + dx) & 3, 0:128, :] = term_ref[rows, :512]
                a_refs[k][(sp[XX] + dx) & 3, 128:144, :] = vec


def middle_kernel(*refs):
    a, b = refs[0:4], refs[4:8]
    a_ref, proj_ref, b_refs = refs[8], refs[9], refs[10:14]
    a_ref[...] = terms_of(a).astype(bf16)
    total = terms_of(b).astype(bf16)
    for d in range(4):
        for j in range(2):
            at = (d * 2 + j) * 128
            b_refs[d][:, j * 128 : (j + 1) * 128] = total[at : at + 128]
    for j in range(16):
        proj_ref[:, j * 128 : (j + 1) * 128] = total[1024 + j * 64 : 1088 + j * 64]


def tok_back_kernel(sp, own_ref, got_ref, w_ref, after_ref, *rest):
    refs, cat_ref = rest[:4], rest[4]

    @pl.when(pl.program_id(0) == 0)
    def _():
        cat_ref[:, pl.ds(pl.multiple_of(sp[CC] * 768, 256), 768)] = own_ref[0]
        cat_ref[:, pl.ds(pl.multiple_of((1 - sp[CC]) * 768, 256), 768)] = got_ref[0]

    weights = w_ref[...].reshape(256, 1536)
    to_four(lax.dot_general(cat_ref[...], weights, BACK, preferred_element_type=f32), refs)


def pieces_kernel(sp, *refs):
    b, proj = refs[1:5], refs[5:9]
    out_ref, near_ref, away_ref, proj_ref = refs[10:14]
    first = terms_of([refs[0].at[x] for x in range(4)]).astype(bf16)
    second = terms_of(b).astype(bf16)
    for m in range(8):
        row = (m & 1) * 64 + ((m >> 1) & 1) * 32
        out_ref[m, 0:32, :512] = first[row : row + 32]
        out_ref[m, 0:32, 512:] = second[row : row + 32]
        out_ref[m, 32:48, :512] = first[128:144]
        out_ref[m, 32:48, 512:] = jnp.zeros((16, 256), bf16)
    proj_ref[...] = terms_of(proj).astype(bf16)
    near_ref[...] = proj_ref[pl.ds(pl.multiple_of(sp[YL] * 32, 32), 32), :]
    away_ref[...] = proj_ref[pl.ds(pl.multiple_of((1 - sp[YL]) * 32, 32), 32), :]


def final_kernel(sp, got_ref, *refs):
    near, given = refs[0], refs[1:4]
    q_ref, k_ref, v_ref, proj_ref, g1, s1, g2, s2, rms_ref = refs[5:]
    for m in range(8):
        for i, ref in enumerate((q_ref, k_ref, v_ref)):
            for head in range(2):
                at = m * 256 + head * 128
                ref[:, at : at + 128] = got_ref[
                    m, 0:32, (head * 3 + i) * 128 : (head * 3 + i + 1) * 128
                ].astype(f32)
    on_diagonal = sp[ZZ] == sp[REP] * 2 + sp[YL]
    proj_ref[...] = jnp.where(on_diagonal, near[...].astype(f32), terms_of(given))
    vec = sum(got_ref[m, 32:48, :128].astype(f32) for m in range(8))
    s = sp[YL] * 2 + sp[CC]
    own = jnp.where(s == 0, vec[:, 0:32], vec[:, 32:64])
    own = jnp.where(s == 2, vec[:, 64:96], own)
    own = jnp.where(s == 3, vec[:, 96:128], own)
    for i, ref in enumerate((g1, s1, g2, s2)):
        ref[...] = own[i : i + 1]
    rms_ref[...] = jnp.sqrt(vec[4:5] / (vec[4:5, 3:4] * 2048.0))


def mlp_split_kernel(sp, sum_ref, after_ref, rep_ref, away_ref):
    rep_ref[0:32, :] = sum_ref[0, pl.ds(pl.multiple_of(sp[YL] * 32, 32), 32), :]
    rep_ref[32:96, :] = sum_ref[1]
    away_ref[...] = sum_ref[0, pl.ds(pl.multiple_of((1 - sp[YL]) * 32, 32), 32), :]


def final_mlp_kernel(sp, own_ref, yl_ref, rep_ref, both_ref, up_ref, down_ref, mark_ref):
    mark_ref[...] = jnp.zeros_like(mark_ref)
    rep, yl = sp[REP], sp[YL]
    mine = own_ref[0, pl.ds(pl.multiple_of(yl * 32, 32), 32), :]
    first_rep, first_yl = rep == 0, yl == 0
    got = {(0, 0): mine, (0, 1): yl_ref[...], (1, 0): rep_ref[0:32], (1, 1): both_ref[...]}
    for yl_of in range(2):
        same = (yl == yl_of)
        near = jnp.where(same, got[0, 0], got[0, 1]).astype(f32)
        far = jnp.where(same, got[1, 0], got[1, 1]).astype(f32)
        low = jnp.where(first_rep, near, far)
        high = jnp.where(first_rep, far, near)
        for zx in range(16):
            for c in range(2):
                src = slice(zx * 128 + c * 64, zx * 128 + c * 64 + 64)
                at = zx * 512 + yl_of * 256 + c * 128
                up_ref[:, at : at + 128] = jnp.concatenate([low[:, src], high[:, src]], axis=1)
    own_rows = pl.ds(pl.multiple_of(rep * 64, 64), 64)
    far_rows = pl.ds(pl.multiple_of((1 - rep) * 64, 64), 64)
    down_ref[own_rows, :] = own_ref[1].astype(f32)
    down_ref[far_rows, :] = rep_ref[32:96].astype(f32)


def per_device(
    hidden_in,
    lengths,
    w_query,
    w_key,
    w_value,
    w_output,
    attn_gain,
    attn_shift,
    w_up,
    w_down,
    mlp_gain,
    mlp_shift,
    cotangent,
):
    rep, z, x, yl, c = (lax.axis_index(a) for a in AXES)
    s, y = yl * 2 + c, rep * 2 + yl
    any_place = pl.BlockSpec(memory_space=pl.ANY)
    tok = hidden_in.reshape(128, 2048)
    cot = cotangent.reshape(128, 2048)
    sp = jnp.stack([rep, z, x, yl, c, lengths[0], lengths[0], lengths[0]]).astype(i32)
    rows = whole((128, 2048))

    keep, send = call(
        prep_kernel,
        [out((32, 3712))] * 2,
        (
            w_query,
            w_key,
            w_value,
            w_up,
            *(v.reshape(1, 32) for v in (attn_gain, attn_shift, mlp_gain, mlp_shift)),
        ),
        [whole((32, 2048))] * 3 + [whole((32, 8192))] + [whole((1, 32))] * 4,
        [whole((32, 3712))] * 2,
        scalars=(sp,),
        vmem=60,
    )
    got = lax.ppermute(send, "yl", xored(1, 2))
    (qkv_piece,) = call(
        qkv_piece_kernel,
        [out((64, 1664))],
        (keep, got),
        [whole((32, 3712))] * 2,
        [whole((64, 1664))],
        scalars=(sp,),
        vmem=16,
    )
    qkv_w = lax.all_gather(qkv_piece, ZXC, axis=0)

    first_yl, on_diagonal = yl == 0, y == z
    out_got = lax.ppermute(w_output, "yl", xored(1, 2))
    (out_piece,) = call(
        out_rows_kernel,
        [out((64, 2048))],
        (w_output, out_got),
        [whole((32, 2048))] * 2,
        [whole((64, 2048))],
        scalars=(sp,),
        vmem=16,
    )
    spread = [diagonal(out_piece, True, by) for by in (1, 2, 3)]
    out_piece = jnp.where(on_diagonal, out_piece, spread[0] + spread[1] + spread[2])
    out_own = jnp.stack(x_gather(out_piece))
    block4 = whole((4, 64, 2048))
    (proj,) = call(
        proj_kernel,
        [out((512, 2048))],
        (out_own, to_core(out_own)),
        [block4, block4],
        [whole((512, 2048))],
        scalars=(sp,),
        vmem=16,
    )

    (tok_swapped,) = call(swap_kernel, [out((128, 2048))], (tok,), [rows], [rows], vmem=16)
    (tok_mine,) = call(
        cat_kernel,
        [out((512, 2048))],
        (*y_gather(tok_swapped), out_own),
        [rows] * 4 + [any_place],
        [whole((512, 2048))],
        vmem=16,
    )
    tok_all = jnp.concatenate([tok_mine, to_core(tok_mine)], axis=0)
    (mlp_piece,) = call(
        mlp_piece_kernel,
        [out((2, 64, 2048))],
        (keep, got, w_down, proj, tok_all),
        [whole((32, 3712))] * 2 + [whole((128, 2048)), any_place, any_place],
        [whole((2, 64, 2048))],
        scalars=(sp,),
        vmem=16,
    )
    mlp_w = lax.all_gather(mlp_piece, ZXC, axis=0)

    qkv_all, vecs, lens = call(
        qkv_kernel,
        [out((1024, 768)), out((16, 2048), f32), out((16, 128), f32)],
        (tok_all, qkv_w, qkv_w),
        [
            whole((1024, 2048)),
            pl.BlockSpec((32, 64, 256), lambda n, sp: (0, 0, sp[CC] * 3 + n)),
            pl.BlockSpec((32, 16, 128), lambda n, sp: (0, 0, 12)),
        ],
        [
            pl.BlockSpec((1024, 256), lambda n, sp: (0, n)),
            whole((16, 2048)),
            whole((16, 128)),
        ],
        grid=(3,),
        scalars=(sp,),
        vmem=60,
    )
    lens = lens[4, :4].astype(i32)
    qkv_all = qkv_all.reshape(2, 2, 2, 128, 768)
    (ctx_all,) = call(
        attend_kernel,
        [out((2, 2, 2, 128, 256))],
        (qkv_all,),
        [group_block(768)],
        [group_block(256)],
        grid=(2, 2),
        scalars=(sp, lens),
        vmem=16,
    )
    ctx_all = ctx_all.reshape(2, 512, 256)
    ctx_got = to_core(ctx_all)
    ctx, *attn_parts = call(
        out_kernel,
        [out((512, 512))] + [out((64, 2048))] * 8,
        (ctx_all, ctx_got, proj),
        [
            pl.BlockSpec((1, 512, 256), lambda n, sp: (0, 0, 0)),
            pl.BlockSpec((1, 512, 256), lambda n, sp: (1, 0, 0)),
            pl.BlockSpec((512, 512), lambda n, sp: (0, n)),
        ],
        [whole((512, 512))] + [pl.BlockSpec((64, 512), lambda n, sp: (0, n))] * 8,
        grid=(4,),
        scalars=(sp,),
    )
    vec_block, rows, halves = whole((16, 2048)), whole((64, 2048)), (0, 1)
    tok_half = [pl.BlockSpec((64, 2048), lambda *_, h=h: (h, 0)) for h in halves]
    norm_outs = [
        call(
            functools.partial(norm_one_kernel, h),
            [out((64, 2048)), out((64, 2048), f32), out((64, 128), f32), out((8, 128), f32)],
            (*sum_parts(attn_parts[h::2], Y4), tok, vecs),
            [rows] * 4 + [tok_half[h], vec_block],
            [rows, rows, whole((64, 128)), whole((8, 128))],
            scalars=(sp,),
            vmem=16,
        )
        for h in halves
    ]
    norm_one = [o[1] for o in norm_outs]
    scale_one = [o[2] for o in norm_outs]

    four = [rows] * 4
    group = whole((256, 2048))
    mlp_held, mark = load_weights(mlp_w), out((8, 128), f32)
    mlp_outs = []
    for h in halves:
        after = mlp_outs[0][3] if h else norm_outs[0][3]
        mlp_outs.append(
            call_resident(
                mlp_kernel,
                [out((256, 2048))] * 3 + [mark] + [out((64, 2048))] * 4,
                (*y_gather(norm_outs[h][0]), after),
                mlp_held,
            )
        )
    two_outs = [
        call(
            functools.partial(norm_two_kernel, h),
            [
                out((64, 2048)),
                out((64, 2048)),
                out((64, 2048), f32),
                out((8, 2048), f32),
                out((8, 128), f32),
            ],
            (*sum_parts(mlp_outs[h][4:], Y4), norm_one[h], vecs, cot, norm_outs[h][3]),
            four + [rows, vec_block, tok_half[h], whole((8, 128))],
            [rows, rows, rows, whole((8, 2048)), whole((8, 128))],
            scalars=(sp,),
            vmem=16,
        )
        for h in halves
    ]
    output = jnp.concatenate([two_outs[h][0] for h in halves], axis=0)

    back_outs = []
    for h in halves:
        after = back_outs[0][2] if h else two_outs[0][4]
        back_outs.append(
            call_resident(
                mlp_back_kernel,
                [out((256, 2048))] * 2 + [mark] + [out((64, 2048))] * 4,
                (*y_gather(two_outs[h][1]), mlp_outs[h][1], after),
                mlp_held,
            )
        )
    hidden_terms = [sum_parts(back_outs[h][3:], Y4) for h in halves]

    def norm_one_back(h, after):
        return call(
            norm_one_back_kernel,
            [out((64, 2048)), out((64, 2048), f32), out((8, 2048), f32)],
            (*hidden_terms[h], two_outs[h][2], norm_one[h], scale_one[h], vecs, after),
            four + [rows, rows, whole((64, 128)), vec_block, any_place],
            [rows, rows, whole((8, 2048))],
            vmem=16,
            cost=300_000_000_000 if h else 1000,
        )

    one_outs = [norm_one_back(0, back_outs[0][2])]
    hidden_col = pl.BlockSpec((256, 512), lambda w, n: (0, jnp.where(w == 0, n, 3)))
    act_col = pl.BlockSpec((256, 512), lambda w, n: (0, jnp.where(w == 1, n, 0)))
    mlp_terms, terms_mark = call(
        mlp_terms_kernel,
        [out((32, 2, 64, 2048)), mark],
        (
            *(mlp_outs[h][2] for h in halves),
            *(back_outs[h][0] for h in halves),
            *(mlp_outs[h][0] for h in halves),
            *(back_outs[h][1] for h in halves),
            one_outs[0][2],
        ),
        [hidden_col] * 2 + [group] * 2 + [act_col] * 2 + [group] * 2 + [any_place],
        [pl.BlockSpec((8, 1, 64, 2048), lambda w, n: (n, w, 0, 0)), whole((8, 128))],
        grid=(2, 4),
        vmem=60,
    )
    one_outs.append(norm_one_back(1, terms_mark))
    attn_gathers = [y_gather(one_outs[h][0]) for h in halves]
    mlp_sum = lax.psum_scatter(mlp_terms, ZXC, scatter_dimension=0, tiled=True)
    mlp_sum = mlp_sum.reshape(2, 64, 2048)
    ctx_grad, ctx_grad_send, grad_attn = call(
        ctx_back_kernel,
        [out((512, 256)), out((512, 256)), out((512, 2048))],
        (*attn_gathers[0], *attn_gathers[1], proj),
        four * 2 + [whole((512, 2048))],
        [whole((512, 256)), whole((512, 256)), whole((512, 2048))],
        scalars=(sp,),
        vmem=16,
    )
    ctx_grad_got = to_core(ctx_grad_send)
    proj_block = pl.BlockSpec((4, 64, 512), lambda n, sp: (0, 0, n))
    proj_terms, proj_send = call(
        proj_terms_kernel,
        [out((4, 64, 2048))] * 2,
        (ctx, grad_attn),
        [whole((512, 512)), pl.BlockSpec((512, 512), lambda n, sp: (0, n))],
        [proj_block, proj_block],
        grid=(4,),
        scalars=(sp,),
        scratch=[pltpu.VMEM((512, 512), bf16)],
    )
    proj_got = to_core(proj_send)
    half_block = pl.BlockSpec((2, 1, 128, 256), lambda e, p, *_: (0, p, 0, 0))
    (qkv_grad,) = call(
        attend_back_kernel,
        [out((2, 2, 2, 128, 768))],
        (qkv_all, ctx_grad.reshape(2, 2, 128, 256), ctx_grad_got.reshape(2, 2, 128, 256)),
        [group_block(768), half_block, half_block],
        [group_block(768)],
        grid=(2, 2),
        scalars=(sp, lens),
        vmem=16,
        cost=20_000_000_000,
    )
    qkv_grad = qkv_grad.reshape(2, 512, 768)
    qkv_grad_got = to_core(qkv_grad)

    step_vec = pl.BlockSpec((8, 512), lambda n, sp: (0, n))
    blocks = call(
        qkv_terms_kernel,
        [out((4, 144, 512))] * 4 + [out((2048, 128))] * 4,
        (
            tok_all,
            qkv_grad.reshape(1024, 768),
            *(one_outs[h][2] for h in halves),
            *(two_outs[h][3] for h in halves),
            *(two_outs[h][4] for h in halves),
            proj_terms,
            proj_got,
            qkv_grad_got,
        ),
        [
            pl.BlockSpec((1024, 512), lambda n, sp: (0, n)),
            whole((1024, 768)),
            *[step_vec] * 4,
            whole((8, 128)),
            whole((8, 128)),
            proj_block,
            proj_block,
            any_place,
        ],
        [whole((4, 144, 512))] * 4 + [whole((2048, 128))] * 4,
        grid=(4,),
        scalars=(sp,),
        scratch=[pltpu.VMEM((512, 768), bf16)],
        cost=20_000_000_000,
    )
    a_terms, b_terms = sum_parts(blocks[:4], "z"), sum_parts(blocks[4:], "x")
    tok_parts = call(
        tok_back_kernel,
        [out((128, 2048))] * 4,
        (qkv_grad, qkv_grad_got, qkv_w, b_terms[1]),
        [
            pl.BlockSpec((1, 512, 768), lambda n, sp: (0, 0, 0)),
            pl.BlockSpec((1, 512, 768), lambda n, sp: (1, 0, 0)),
            pl.BlockSpec((4, 64, 1536), lambda n, sp: (n, 0, 0)),
            any_place,
        ],
        [pl.BlockSpec((128, 256), lambda n, sp: (0, n))] * 4,
        grid=(8,),
        scalars=(sp,),
        scratch=[pltpu.VMEM((512, 1536), bf16)],
    )
    input_grad, grad_mark = call(
        last_kernel,
        [out((128, 2048), f32), mark],
        (*sum_parts(tok_parts, Y4), one_outs[0][1], one_outs[1][1]),
        [whole((128, 2048))] * 4 + [rows] * 2,
        [whole((128, 2048)), whole((8, 128))],
        vmem=16,
    )

    a_line, proj_line, *b_line = call(
        middle_kernel,
        [out((4, 144, 512)), out((64, 2048))] + [out((128, 256))] * 4,
        (*a_terms, *b_terms),
        [whole((4, 144, 512))] * 4 + [whole((2048, 128))] * 4,
        [whole((4, 144, 512)), whole((64, 2048))] + [whole((128, 256))] * 4,
        vmem=60,
        cost=20_000_000_000,
    )
    pieces, near, away = call(
        pieces_kernel,
        [out((8, 48, 768))] + [out((32, 2048))] * 2,
        (
            lax.all_to_all(a_line, "x", 0, 0, tiled=True),
            *sum_parts(b_line, "z"),
            proj_line,
            *(diagonal(proj_line, False, by) for by in (1, 2, 3)),
            grad_mark,
        ),
        [whole((4, 144, 512))]
        + [whole((128, 256))] * 4
        + [whole((64, 2048))] * 4
        + [any_place],
        [whole((8, 48, 768))] + [whole((32, 2048))] * 2,
        scalars=(sp,),
        scratch=[pltpu.VMEM((64, 2048), bf16)],
        vmem=60,
        cost=20_000_000_000,
    )
    arrived = lax.all_to_all(pieces, Y8, 0, 0, tiled=True)
    given = [along_y(away, 1), along_y(near, 2), along_y(away, 3)]
    rep_part, up_away = call(
        mlp_split_kernel,
        [out((96, 2048)), out((32, 2048))],
        (mlp_sum, near),
        [whole((2, 64, 2048)), any_place],
        [whole((96, 2048)), whole((32, 2048))],
        scalars=(sp,),
        vmem=60,
    )
    grad_up, grad_down, mlp_mark = call(
        final_mlp_kernel,
        [out((32, 8192), f32), out((128, 2048), f32), mark],
        (
            mlp_sum,
            lax.ppermute(up_away, Y4, xored(1, 4)),
            lax.ppermute(rep_part, Y4, xored(2, 4)),
            lax.ppermute(up_away, Y4, xored(3, 4)),
        ),
        [whole((2, 64, 2048)), whole((32, 2048)), whole((96, 2048)), whole((32, 2048))],
        [whole((32, 8192)), whole((128, 2048)), whole((8, 128))],
        scalars=(sp,),
        vmem=60,
    )
    one_row = whole((1, 32))
    grad_q, grad_k, grad_v, grad_proj, g1, s1, g2, s2, rms = call(
        final_kernel,
        [out((32, 2048), f32)] * 4 + [out((1, 32), f32)] * 4 + [out((1, 128), f32)],
        (arrived, near, *given, mlp_mark),
        [whole((8, 48, 768))] + [whole((32, 2048))] * 4 + [any_place],
        [whole((32, 2048))] * 4 + [one_row] * 4 + [whole((1, 128))],
        scalars=(sp,),
        vmem=60,
    )
    vec_mine = [v.reshape(32) for v in (g1, s1, g2, s2)]
    rms_stats = rms[0, :3]
    return (
        output.reshape(1, 128, 2048),
        input_grad.reshape(1, 128, 2048),
        grad_q,
        grad_k,
        grad_v,
        grad_proj,
        vec_mine[0],
        vec_mine[1],
        grad_up,
        grad_down,
        vec_mine[2],
        vec_mine[3],
        rms_stats,
    )


def solution(mesh):
    split = Mesh(mesh.devices.reshape(2, 4, 4, 2, 2), AXES)
    rows, vec, seq = P(SHARD, None), P(SHARD), P(SHARD, "rep", None)
    return jax.shard_map(
        per_device,
        mesh=split,
        in_specs=(seq, vec, rows, rows, rows, rows, vec, vec, rows, rows, vec, vec, seq),
        out_specs=(seq, seq, rows, rows, rows, rows, vec, vec, rows, rows, vec, vec, P()),
        check_vma=False,
    )
```

```python
import functools

import jax
import jax.numpy as jnp
from jax import lax
from jax.experimental import pallas as pl
from jax.experimental.pallas import tpu as pltpu
from jax.sharding import Mesh
from jax.sharding import PartitionSpec as P

HEAD_DIM = 128
AXES = ("rep", "z", "x", "yl", "c")
SHARD = ("z", "x", "yl", "c")
ZXC = ("z", "x", "c")
Y4 = ("rep", "yl")
Y8 = ("rep", "yl", "c")
norm_eps = 1e-12
masked_score = -1e30
bf16 = jnp.bfloat16
f32 = jnp.float32
i32 = jnp.int32
MIB = 1 << 20
REP, ZZ, XX, YL, CC, LEN = range(6)


def shifted(by, count=4):
    return [(i, (i + by) % count) for i in range(count)]


def xored(by, count):
    return [(i, i ^ by) for i in range(count)]


def from_offset(value, axes, offset):
    return lax.ppermute(value, axes, shifted(-offset))


def to_core(value):
    return lax.ppermute(value, "c", xored(1, 2))


def y_gather(value):
    return [value] + [from_offset(value, Y4, d) for d in (1, 2, 3)]


def x_gather(value):
    return [value] + [from_offset(value, "x", d) for d in (1, 2, 3)]


def sum_parts(parts, axis):
    return [parts[0]] + [lax.ppermute(parts[d], axis, shifted(d)) for d in (1, 2, 3)]


def diagonal(value, to_z, by):
    pairs = []
    for rep in range(2):
        for yl in range(2):
            y = rep * 2 + yl
            at = lambda z: rep * 8 + (z % 4) * 2 + yl
            pairs.append((at(y), at(y + by)) if to_z else (at(y - by), at(y)))
    return lax.ppermute(value, ("rep", "z", "yl"), pairs)


def along_y(value, by):
    pairs = []
    for y in range(4):
        at = lambda v: ((v % 4) // 2) * 8 + y * 2 + v % 2
        pairs.append((at(y), at(y + by)))
    return lax.ppermute(value, ("rep", "z", "yl"), pairs)


def call(kernel, outs, operands, specs, out_specs, grid=(1,), scalars=(), scratch=(), vmem=28, cost=1000):
    return pl.pallas_call(
        kernel,
        grid_spec=pltpu.PrefetchScalarGridSpec(
            num_scalar_prefetch=len(scalars),
            grid=grid,
            in_specs=specs,
            out_specs=out_specs,
            scratch_shapes=scratch,
        ),
        out_shape=outs,
        compiler_params=pltpu.CompilerParams(vmem_limit_bytes=vmem * MIB),
        cost_estimate=pl.CostEstimate(flops=cost, bytes_accessed=1000, transcendentals=0),
    )(*scalars, *operands)


def call_resident(kernel, outs, operands, weights, vmem=14):
    place = pl.BlockSpec(memory_space=pltpu.VMEM)
    held = [pltpu.with_memory_space_constraint(w, pltpu.VMEM) for w in weights]
    return pl.pallas_call(
        kernel,
        in_specs=[place] * (len(operands) - 1)
        + [pl.BlockSpec(memory_space=pl.ANY)]
        + [place] * len(weights),
        out_specs=[place] * len(outs),
        out_shape=outs,
        compiler_params=pltpu.CompilerParams(vmem_limit_bytes=vmem * MIB),
        cost_estimate=pl.CostEstimate(flops=1000, bytes_accessed=1000, transcendentals=0),
    )(*operands, *held)


def out(shape, dtype=bf16):
    return jax.ShapeDtypeStruct(shape, dtype)


def whole(shape):
    return pl.BlockSpec(shape, lambda *_: (0,) * len(shape))


def swap_middle(value):
    width = value.shape[1]
    chunk = (lax.broadcasted_iota(i32, value.shape, 1) >> 5) & 3
    ahead = pltpu.roll(value, width - 32, 1)
    behind = pltpu.roll(value, 32, 1)
    return jnp.where(chunk == 1, ahead, jnp.where(chunk == 2, behind, value))


def swap_kernel(tok_ref, out_ref):
    out_ref[...] = swap_middle(tok_ref[...].astype(f32)).astype(bf16)


def prep_kernel(sp, wq_ref, wk_ref, wv_ref, g1, s1, g2, s2, keep_ref, send_ref):
    rep, yl = sp[REP], sp[YL]
    s = yl * 2 + sp[CC]
    lane = lax.broadcasted_iota(i32, (1, 128), 1)
    rows = []
    for ref in (g1, s1, g2, s2):
        value = ref[...].astype(f32)
        tiled = jnp.concatenate([value, value, value, value], axis=1)
        rows.append(jnp.where((lane >> 5) == s, tiled, 0.0))
    rows.append(jnp.where(lane == s, sp[LEN].astype(f32), 0.0))
    vec = jnp.concatenate(rows + [jnp.zeros((27, 128), f32)], axis=0).astype(bf16)
    keep_ref[:, 1536:] = vec
    send_ref[:, 1536:] = vec
    for target, dest in ((yl, keep_ref), (1 - yl, send_ref)):
        for i, ref in enumerate((wq_ref, wk_ref, wv_ref)):
            start = pl.multiple_of((rep * 2 + target) * 512, 512)
            block = ref[:, pl.ds(start, 512)]
            for head in range(4):
                dest[:, (head * 3 + i) * 128 : (head * 3 + i + 1) * 128] = block[
                    :, head * 128 : (head + 1) * 128
                ]


def prep_up_kernel(sp, up_ref, keep_ref, send_ref):
    rep, yl = sp[REP], sp[YL]
    for target, dest in ((yl, keep_ref), (1 - yl, send_ref)):
        for zx in range(16):
            start = pl.multiple_of(zx * 512 + target * 256, 256)
            block = up_ref[:, pl.ds(start, 256)]
            low = jnp.concatenate([block[:, 0:64], block[:, 128:192]], axis=1)
            high = jnp.concatenate([block[:, 64:128], block[:, 192:256]], axis=1)
            dest[:, zx * 128 : (zx + 1) * 128] = jnp.where(rep == 0, low, high)


def qkv_piece_kernel(sp, keep_ref, got_ref, out_ref):
    own = pl.ds(pl.multiple_of(sp[YL] * 32, 32), 32)
    other = pl.ds(pl.multiple_of((1 - sp[YL]) * 32, 32), 32)
    out_ref[own, :1536] = keep_ref[:, :1536]
    out_ref[other, :1536] = got_ref[:, :1536]
    vec = (keep_ref[:, 1536:].astype(f32) + got_ref[:, 1536:].astype(f32)).astype(bf16)
    out_ref[0:32, 1536:] = vec
    out_ref[32:64, 1536:] = jnp.zeros_like(vec)


def mlp_piece_kernel(sp, keep_ref, got_ref, down_ref, after1_ref, after2_ref, out_ref):
    own = pl.ds(pl.multiple_of(sp[YL] * 32, 32), 32)
    other = pl.ds(pl.multiple_of((1 - sp[YL]) * 32, 32), 32)
    out_ref[0, own, :] = keep_ref[...]
    out_ref[0, other, :] = got_ref[...]
    out_ref[1] = down_ref[pl.ds(pl.multiple_of(sp[REP] * 64, 64), 64), :]


def cat_kernel(t0, t1, t2, t3, after_ref, out_ref):
    for d, ref in enumerate((t0, t1, t2, t3)):
        out_ref[d * 128 : (d + 1) * 128, :] = ref[...]


def out_rows_kernel(sp, own_ref, got_ref, out_ref):
    out_ref[pl.ds(pl.multiple_of(sp[YL] * 32, 32), 32), :] = own_ref[...]
    out_ref[pl.ds(pl.multiple_of((1 - sp[YL]) * 32, 32), 32), :] = got_ref[...]


def proj_kernel(sp, own_ref, other_ref, proj_ref):
    for d in range(4):
        for ref, core in ((own_ref, sp[CC]), (other_ref, 1 - sp[CC])):
            for yl_of in range(2):
                row = pl.multiple_of(((sp[XX] + d) & 3) * 128 + yl_of * 64 + core * 32, 32)
                proj_ref[pl.ds(row, 32), :] = ref[d, yl_of * 32 : (yl_of + 1) * 32, :]


def qkv_kernel(sp, tok_ref, w_ref, vec_in_ref, out_ref, vec_ref, len_ref):
    @pl.when(pl.program_id(0) == 0)
    def _():
        for zx in range(16):
            pair = vec_in_ref[2 * zx].astype(f32) + vec_in_ref[2 * zx + 1].astype(f32)
            vec_ref[:, zx * 128 : (zx + 1) * 128] = pair
        own = (sp[ZZ] * 4 + sp[XX]) * 2
        len_ref[...] = vec_in_ref[own].astype(f32) + vec_in_ref[own + 1].astype(f32)

    weights = w_ref[...].reshape(2048, 256)
    out_ref[...] = jnp.dot(tok_ref[...], weights, preferred_element_type=f32).astype(bf16)


def softmax_of(q, k, open_row):
    raw = lax.dot_general(q, k, (((1,), (1,)), ((), ())), preferred_element_type=f32)
    scores = jnp.where(open_row, raw * (HEAD_DIM**-0.5), masked_score)
    top = jnp.max(scores, axis=-1, keepdims=True)
    exponent = jnp.exp(scores - top)
    return exponent * (1.0 / jnp.sum(exponent, axis=-1, keepdims=True))


def open_keys(sp, lens):
    e, p = pl.program_id(0), pl.program_id(1)
    length = lens[((sp[YL] + p) & 1) * 2 + ((sp[CC] + e) & 1)]
    swap = ((sp[REP] * 2 + sp[YL] + p) & 3) >> 1
    lane = lax.broadcasted_iota(i32, (1, 256), 1)
    position = jnp.where(swap == 1, (lane + 128) & 255, lane)
    return position < length


def head_part(ref, head, i):
    return ref[0, :, 0, :, (head * 3 + i) * 128 : (head * 3 + i + 1) * 128].reshape(256, 128)


def attend_kernel(sp, lens, qkv_ref, ctx_ref):
    open_row = open_keys(sp, lens)
    for head in range(2):
        q, k, v = (head_part(qkv_ref, head, i) for i in range(3))
        probs = softmax_of(q, k, open_row).astype(bf16)
        ctx = jnp.dot(probs, v, preferred_element_type=f32).astype(bf16)
        ctx_ref[0, :, 0, :, head * 128 : (head + 1) * 128] = ctx.reshape(2, 128, 128)


def attend_back_kernel(sp, lens, qkv_ref, own_ref, other_ref, out_ref):
    open_row = open_keys(sp, lens)
    scale = HEAD_DIM**-0.5
    first = pl.program_id(0) == 0
    for head in range(2):
        q, k, v = (head_part(qkv_ref, head, i) for i in range(3))
        cols = slice(head * 128, (head + 1) * 128)
        grad = jnp.where(first, own_ref[:, 0, :, cols], other_ref[:, 0, :, cols]).reshape(256, 128)
        probs = softmax_of(q, k, open_row)
        grad_probs = lax.dot_general(grad, v, (((1,), (1,)), ((), ())), preferred_element_type=f32)
        inner = jnp.sum(probs * grad_probs, axis=-1, keepdims=True)
        grad_scores = (probs * (grad_probs - inner)).astype(bf16)
        grad_q = jnp.dot(grad_scores, k, preferred_element_type=f32) * scale
        over = (((0,), (0,)), ((), ()))
        grad_k = lax.dot_general(grad_scores, q, over, preferred_element_type=f32) * scale
        grad_v = lax.dot_general(probs.astype(bf16), grad, over, preferred_element_type=f32)
        for i, part in enumerate((grad_q, grad_k, grad_v)):
            out_ref[0, :, 0, :, (head * 3 + i) * 128 : (head * 3 + i + 1) * 128] = part.astype(
                bf16
            ).reshape(2, 128, 128)


def group_block(columns):
    return pl.BlockSpec((1, 2, 1, 128, columns), lambda e, p, *_: (e, 0, p, 0, 0))


def to_four(result, refs):
    rows = result.shape[0] // len(refs)
    for d, ref in enumerate(refs):
        ref[...] = result[d * rows : (d + 1) * rows].astype(bf16)


def out_kernel(sp, own_ref, got_ref, proj_ref, ctx_ref, *refs):
    @pl.when(pl.program_id(0) == 0)
    def _():
        ctx_ref[:, pl.ds(pl.multiple_of(sp[CC] * 256, 256), 256)] = own_ref[0]
        ctx_ref[:, pl.ds(pl.multiple_of((1 - sp[CC]) * 256, 256), 256)] = got_ref[0]

    to_four(jnp.dot(ctx_ref[...], proj_ref[...], preferred_element_type=f32), refs)


def terms_of(refs):
    return sum(r[...].astype(f32) for r in refs[1:]) + refs[0][...].astype(f32)


def valid_rows(sp, half):
    position = sp[REP] * 128 + half * 64 + lax.broadcasted_iota(i32, (64, 1), 0)
    return (position < sp[LEN]).astype(f32)


def lane_of(values):
    lane = lax.broadcasted_iota(i32, (8, 128), 1)
    total = jnp.zeros((8, 128), f32)
    for i, value in enumerate(values):
        total = jnp.where(lane == i, value, total)
    return total


def normed(values):
    center = values - jnp.mean(values, axis=-1, keepdims=True)
    spread = jnp.mean(center * center, axis=-1, keepdims=True)
    scale = lax.rsqrt(spread + norm_eps)
    return center * scale, scale


def norm_one_kernel(half, sp, p0, p1, p2, p3, tok_ref, vec_ref, hidden_ref, norm_ref, scale_ref, stat_ref):
    attn = terms_of((p0, p1, p2, p3))
    resid = tok_ref[...].astype(f32) + attn
    norm, scale = normed(resid)
    hidden = norm * vec_ref[0:1, :] + vec_ref[1:2, :]
    hidden_ref[...] = swap_middle(hidden).astype(bf16)
    norm_ref[...] = norm
    scale_ref[...] = jnp.broadcast_to(scale, scale_ref.shape)
    valid = valid_rows(sp, half)
    stat_ref[...] = lane_of((jnp.sum(valid * (resid * resid)), jnp.sum(valid * (attn * attn))))


def norm_two_kernel(
    half, sp, p0, p1, p2, p3, norm_ref, vec_ref, cot_ref, stat_ref, out_ref, low_ref, grad_ref, vg_ref, st_ref
):
    mlp = terms_of((p0, p1, p2, p3))
    resid = norm_ref[...] * vec_ref[0:1, :] + vec_ref[1:2, :] + mlp
    norm, scale = normed(resid)
    out_ref[...] = (norm * vec_ref[2:3, :] + vec_ref[3:4, :]).astype(bf16)
    valid = valid_rows(sp, half)
    grad_out = cot_ref[...].astype(f32) * valid
    vg_ref[0:1, :] = jnp.sum(grad_out * norm, axis=0, keepdims=True)
    vg_ref[1:2, :] = jnp.sum(grad_out, axis=0, keepdims=True)
    e = grad_out * vec_ref[2:3, :]
    mean_e = jnp.mean(e, axis=-1, keepdims=True)
    mean_en = jnp.mean(e * norm, axis=-1, keepdims=True)
    grad = scale * (e - mean_e - norm * mean_en)
    grad_ref[...] = grad
    low_ref[...] = grad.astype(bf16)
    lane = lax.broadcasted_iota(i32, (8, 128), 1)
    more = jnp.where(lane == 2, jnp.sum(valid * (mlp * mlp)), jnp.sum(valid))
    st_ref[...] = jnp.where(lane < 2, stat_ref[...], more)


def norm_one_back_kernel(
    p0, p1, p2, p3, grad2_ref, norm_ref, scale_ref, vec_ref, after_ref, low_ref, grad_ref, vg_ref
):
    grad = grad2_ref[...] + swap_middle(terms_of((p0, p1, p2, p3)))
    norm = norm_ref[...]
    vg_ref[0:1, :] = jnp.sum(grad * norm, axis=0, keepdims=True)
    vg_ref[1:2, :] = jnp.sum(grad, axis=0, keepdims=True)
    e = grad * vec_ref[0:1, :]
    mean_e = jnp.mean(e, axis=-1, keepdims=True)
    mean_en = jnp.mean(e * norm, axis=-1, keepdims=True)
    back = scale_ref[:, 0:1] * (e - mean_e - norm * mean_en)
    grad_ref[...] = back
    low_ref[...] = back.astype(bf16)


def last_kernel(p0, p1, p2, p3, grad_a_ref, grad_b_ref, out_ref, mark_ref):
    mark_ref[...] = jnp.zeros_like(mark_ref)
    total = swap_middle(terms_of((p0, p1, p2, p3)))
    out_ref[0:64, :] = grad_a_ref[...] + total[0:64]
    out_ref[64:128, :] = grad_b_ref[...] + total[64:128]


CHUNKS = [slice(i * 512, (i + 1) * 512) for i in range(4)]
UNITS = [slice(i * 8, (i + 1) * 8) for i in range(4)]


def join(refs, all_ref):
    for d, ref in enumerate(refs):
        all_ref[d * 64 : (d + 1) * 64, :] = ref[...]


def split_rows(result, refs, columns):
    for d, ref in enumerate(refs):
        ref[:, columns] = result[d * 64 : (d + 1) * 64].astype(bf16)


def mlp_kernel(
    h0, h1, h2, h3, after_ref, up_ref, down_ref, act_ref, slope_ref, all_ref, mark_ref, *refs,
    arrived=lambda i: None,
):
    mark_ref[...] = jnp.zeros_like(mark_ref)
    join((h0, h1, h2, h3), all_ref)
    root = 0.7978845608028654
    for i, chunk in enumerate(CHUNKS):
        arrived(i)
        up = up_ref[:, :, chunk].reshape(2048, 512)
        v = jnp.dot(all_ref[...], up, preferred_element_type=f32)
        square = v * v
        t = jnp.tanh(root * v * (1.0 + 0.044715 * square))
        half = 0.5 * (1.0 + t)
        act_ref[:, chunk] = (v * half).astype(bf16)
        slope = half + 0.5 * v * (1.0 - t * t) * (root * (1.0 + 3 * 0.044715 * square))
        slope_ref[:, chunk] = slope.astype(bf16)
    for i, chunk in enumerate(CHUNKS):
        arrived(4 + i)
        down = down_ref[:, :, chunk].reshape(2048, 512)
        split_rows(jnp.dot(act_ref[...], down, preferred_element_type=f32), refs, chunk)


def mlp_first_kernel(h0, h1, h2, h3, after_ref, w_ref, act_ref, slope_ref, all_ref, mark_ref, *rest):
    refs, (up_ref, down_ref, sem) = rest[:4], rest[4:]
    copies = [
        pltpu.make_async_copy(w_ref.at[:, i, :, chunk], ref.at[:, :, chunk], sem.at[i * 4 + j])
        for i, ref in enumerate((up_ref, down_ref))
        for j, chunk in enumerate(pl.ds(k * 512, 512) for k in range(4))
    ]
    for copy in copies[:3]:
        copy.start()

    def arrived(i):
        copies[i].wait()
        if i + 3 < 8:
            copies[i + 3].start()

    mlp_kernel(
        h0, h1, h2, h3, after_ref, up_ref, down_ref, act_ref, slope_ref, all_ref, mark_ref, *refs,
        arrived=arrived,
    )


BACK = (((1,), (1,)), ((), ()))
OVER = (((0,), (0,)), ((), ()))


def mlp_back_kernel(
    g0, g1, g2, g3, slope_ref, after_ref, up_ref, down_ref, pre_ref, all_ref, mark_ref, *refs
):
    mark_ref[...] = jnp.zeros_like(mark_ref)
    join((g0, g1, g2, g3), all_ref)
    for chunk, units in zip(CHUNKS, UNITS):
        down = down_ref[units].reshape(512, 2048)
        grad = lax.dot_general(all_ref[...], down, BACK, preferred_element_type=f32)
        pre_ref[:, chunk] = (grad * slope_ref[:, chunk].astype(f32)).astype(bf16)
    for chunk, units in zip(CHUNKS, UNITS):
        up = up_ref[units].reshape(512, 2048)
        term = lax.dot_general(pre_ref[...], up, BACK, preferred_element_type=f32)
        split_rows(term, refs, chunk)


def mlp_terms_kernel(h0, h1, p0, p1, a0, a1, g0, g1, after_ref, out_ref, mark_ref):
    mark_ref[...] = jnp.zeros_like(mark_ref)

    def both(left, right):
        total = sum(
            lax.dot_general(l[...], r[...], OVER, preferred_element_type=f32)
            for l, r in zip(left, right)
        )
        out_ref[...] = total.astype(bf16).reshape(out_ref.shape)

    @pl.when(pl.program_id(0) == 0)
    def _():
        both((h0, h1), (p0, p1))

    @pl.when(pl.program_id(0) == 1)
    def _():
        both((a0, a1), (g0, g1))


def ctx_back_kernel(sp, *refs):
    proj_ref, own_ref, other_ref, all_ref = refs[8:]
    for i, ref in enumerate(refs[:8]):
        row = (i % 4) * 128 + (i // 4) * 64
        all_ref[row : row + 64, :] = ref[...]
    for ref, core in ((own_ref, sp[CC]), (other_ref, 1 - sp[CC])):
        weights = proj_ref[pl.ds(pl.multiple_of(core * 256, 256), 256), :]
        ref[...] = lax.dot_general(
            all_ref[...], weights, BACK, preferred_element_type=f32
        ).astype(bf16)


def proj_terms_kernel(sp, ctx_ref, grad_ref, mine_ref, send_ref, term_ref):
    term = lax.dot_general(ctx_ref[...], grad_ref[...], OVER, preferred_element_type=f32)
    term_ref[...] = term.astype(bf16)
    for d in range(4):
        for ref, core in ((mine_ref, sp[CC]), (send_ref, 1 - sp[CC])):
            for yl_of in range(2):
                row = pl.multiple_of(((sp[XX] + d) & 3) * 128 + yl_of * 64 + core * 32, 32)
                ref[d, yl_of * 32 : (yl_of + 1) * 32, :] = term_ref[pl.ds(row, 32), :]


def qkv_terms_kernel(
    sp, tok_ref, grad_ref, v1a, v1b, v2a, v2b, sta, stb, mine_ref, got_ref, after_ref, *rest
):
    a_refs, b_refs, term_ref = rest[:4], rest[4:8], rest[8]
    term = lax.dot_general(tok_ref[...], grad_ref[...], OVER, preferred_element_type=f32)
    term_ref[...] = term.astype(bf16)
    step = pl.program_id(0)
    dz = (step - sp[ZZ]) & 3
    for dx in range(4):
        start = pl.multiple_of(((sp[XX] + dx) & 3) * 128, 128)
        rows = pl.ds(start, 128)
        vec = [v1a[0:2, rows] + v1b[0:2, rows], v2a[0:2, rows] + v2b[0:2, rows]]
        vec += [sta[0:4] + stb[0:4]]
        vec = jnp.concatenate(vec + [jnp.zeros((8, 128), f32)], axis=0).astype(bf16)
        vec = jnp.concatenate([vec, jnp.zeros((16, 384), bf16)], axis=1)
        for j in range(2):
            at = pl.multiple_of((dz * 2 + j) * 128, 128)
            b_refs[dx][pl.ds(at, 128), :] = term_ref[rows, 512 + j * 128 : 640 + j * 128]
        total = mine_ref[dx].astype(f32) + got_ref[dx].astype(f32)
        total = total.astype(bf16)
        for j in range(4):
            at = pl.multiple_of(1024 + (step * 4 + j) * 64, 64)
            b_refs[dx][pl.ds(at, 64), :] = total[:, j * 128 : (j + 1) * 128]
        for k in range(4):

            @pl.when(dz == k)
            def _():
                a_refs[k][(sp[XX] + dx) & 3, 0:128, :] = term_ref[rows, :512]
                a_refs[k][(sp[XX] + dx) & 3, 128:144, :] = vec


def middle_kernel(*refs):
    a, b = refs[0:4], refs[4:8]
    a_ref, proj_ref, b_refs = refs[8], refs[9], refs[10:14]
    a_ref[...] = terms_of(a).astype(bf16)
    total = terms_of(b).astype(bf16)
    for d in range(4):
        for j in range(2):
            at = (d * 2 + j) * 128
            b_refs[d][:, j * 128 : (j + 1) * 128] = total[at : at + 128]
    for j in range(16):
        proj_ref[:, j * 128 : (j + 1) * 128] = total[1024 + j * 64 : 1088 + j * 64]


def tok_back_kernel(sp, own_ref, got_ref, w_ref, after_ref, *rest):
    refs, cat_ref = rest[:4], rest[4]

    @pl.when(pl.program_id(0) == 0)
    def _():
        cat_ref[:, pl.ds(pl.multiple_of(sp[CC] * 768, 256), 768)] = own_ref[0]
        cat_ref[:, pl.ds(pl.multiple_of((1 - sp[CC]) * 768, 256), 768)] = got_ref[0]

    weights = w_ref[...].reshape(256, 1536)
    to_four(lax.dot_general(cat_ref[...], weights, BACK, preferred_element_type=f32), refs)


def pieces_kernel(sp, *refs):
    b, proj = refs[1:5], refs[5:9]
    out_ref, near_ref, away_ref, proj_ref = refs[10:14]
    first = terms_of([refs[0].at[x] for x in range(4)]).astype(bf16)
    second = terms_of(b).astype(bf16)
    for m in range(8):
        row = (m & 1) * 64 + ((m >> 1) & 1) * 32
        out_ref[m, 0:32, :512] = first[row : row + 32]
        out_ref[m, 0:32, 512:] = second[row : row + 32]
        out_ref[m, 32:48, :512] = first[128:144]
        out_ref[m, 32:48, 512:] = jnp.zeros((16, 256), bf16)
    proj_ref[...] = terms_of(proj).astype(bf16)
    near_ref[...] = proj_ref[pl.ds(pl.multiple_of(sp[YL] * 32, 32), 32), :]
    away_ref[...] = proj_ref[pl.ds(pl.multiple_of((1 - sp[YL]) * 32, 32), 32), :]


def final_kernel(sp, got_ref, *refs):
    near, given = refs[0], refs[1:4]
    q_ref, k_ref, v_ref, proj_ref, g1, s1, g2, s2, rms_ref = refs[4:]
    for m in range(8):
        for i, ref in enumerate((q_ref, k_ref, v_ref)):
            for head in range(2):
                at = m * 256 + head * 128
                ref[:, at : at + 128] = got_ref[
                    m, 0:32, (head * 3 + i) * 128 : (head * 3 + i + 1) * 128
                ].astype(f32)
    on_diagonal = sp[ZZ] == sp[REP] * 2 + sp[YL]
    proj_ref[...] = jnp.where(on_diagonal, near[...].astype(f32), terms_of(given))
    vec = sum(got_ref[m, 32:48, :128].astype(f32) for m in range(8))
    s = sp[YL] * 2 + sp[CC]
    own = jnp.where(s == 0, vec[:, 0:32], vec[:, 32:64])
    own = jnp.where(s == 2, vec[:, 64:96], own)
    own = jnp.where(s == 3, vec[:, 96:128], own)
    for i, ref in enumerate((g1, s1, g2, s2)):
        ref[...] = own[i : i + 1]
    rms_ref[...] = jnp.sqrt(vec[4:5] / (vec[4:5, 3:4] * 2048.0))


def mlp_split_kernel(sp, sum_ref, after_ref, rep_ref, away_ref):
    rep_ref[0:32, :] = sum_ref[0, pl.ds(pl.multiple_of(sp[YL] * 32, 32), 32), :]
    rep_ref[32:96, :] = sum_ref[1]
    away_ref[...] = sum_ref[0, pl.ds(pl.multiple_of((1 - sp[YL]) * 32, 32), 32), :]


def final_mlp_kernel(sp, own_ref, yl_ref, rep_ref, both_ref, up_ref, down_ref, mark_ref):
    mark_ref[...] = jnp.zeros_like(mark_ref)
    rep, yl = sp[REP], sp[YL]
    mine = own_ref[0, pl.ds(pl.multiple_of(yl * 32, 32), 32), :]
    first_rep, first_yl = rep == 0, yl == 0
    got = {(0, 0): mine, (0, 1): yl_ref[...], (1, 0): rep_ref[0:32], (1, 1): both_ref[...]}
    for yl_of in range(2):
        same = (yl == yl_of)
        near = jnp.where(same, got[0, 0], got[0, 1]).astype(f32)
        far = jnp.where(same, got[1, 0], got[1, 1]).astype(f32)
        low = jnp.where(first_rep, near, far)
        high = jnp.where(first_rep, far, near)
        for zx in range(16):
            for c in range(2):
                src = slice(zx * 128 + c * 64, zx * 128 + c * 64 + 64)
                at = zx * 512 + yl_of * 256 + c * 128
                up_ref[:, at : at + 128] = jnp.concatenate([low[:, src], high[:, src]], axis=1)
    own_rows = pl.ds(pl.multiple_of(rep * 64, 64), 64)
    far_rows = pl.ds(pl.multiple_of((1 - rep) * 64, 64), 64)
    down_ref[own_rows, :] = own_ref[1].astype(f32)
    down_ref[far_rows, :] = rep_ref[32:96].astype(f32)


def per_device(
    hidden_in,
    lengths,
    w_query,
    w_key,
    w_value,
    w_output,
    attn_gain,
    attn_shift,
    w_up,
    w_down,
    mlp_gain,
    mlp_shift,
    cotangent,
):
    rep, z, x, yl, c = (lax.axis_index(a) for a in AXES)
    s, y = yl * 2 + c, rep * 2 + yl
    any_place = pl.BlockSpec(memory_space=pl.ANY)
    tok = hidden_in.reshape(128, 2048)
    cot = cotangent.reshape(128, 2048)
    sp = jnp.stack([rep, z, x, yl, c, lengths[0], lengths[0], lengths[0]]).astype(i32)
    rows = whole((128, 2048))

    keep, send = call(
        prep_kernel,
        [out((32, 1664))] * 2,
        (
            w_query,
            w_key,
            w_value,
            *(v.reshape(1, 32) for v in (attn_gain, attn_shift, mlp_gain, mlp_shift)),
        ),
        [whole((32, 2048))] * 3 + [whole((1, 32))] * 4,
        [whole((32, 1664))] * 2,
        scalars=(sp,),
        vmem=60,
    )
    got = lax.ppermute(send, "yl", xored(1, 2))
    keep_up, send_up = call(
        prep_up_kernel,
        [out((32, 2048))] * 2,
        (w_up,),
        [whole((32, 8192))],
        [whole((32, 2048))] * 2,
        scalars=(sp,),
        vmem=60,
    )
    got_up = lax.ppermute(send_up, "yl", xored(1, 2))
    (qkv_piece,) = call(
        qkv_piece_kernel,
        [out((64, 1664))],
        (keep, got),
        [whole((32, 1664))] * 2,
        [whole((64, 1664))],
        scalars=(sp,),
        vmem=16,
    )
    qkv_w = lax.all_gather(qkv_piece, ZXC, axis=0)

    first_yl, on_diagonal = yl == 0, y == z
    out_got = lax.ppermute(w_output, "yl", xored(1, 2))
    (out_piece,) = call(
        out_rows_kernel,
        [out((64, 2048))],
        (w_output, out_got),
        [whole((32, 2048))] * 2,
        [whole((64, 2048))],
        scalars=(sp,),
        vmem=16,
    )
    spread = [diagonal(out_piece, True, by) for by in (1, 2, 3)]
    out_piece = jnp.where(on_diagonal, out_piece, spread[0] + spread[1] + spread[2])
    out_own = jnp.stack(x_gather(out_piece))
    block4 = whole((4, 64, 2048))
    (proj,) = call(
        proj_kernel,
        [out((512, 2048))],
        (out_own, to_core(out_own)),
        [block4, block4],
        [whole((512, 2048))],
        scalars=(sp,),
        vmem=16,
    )

    (tok_swapped,) = call(swap_kernel, [out((128, 2048))], (tok,), [rows], [rows], vmem=16)
    (tok_mine,) = call(
        cat_kernel,
        [out((512, 2048))],
        (*y_gather(tok_swapped), out_own),
        [rows] * 4 + [any_place],
        [whole((512, 2048))],
        vmem=16,
    )
    tok_all = jnp.concatenate([tok_mine, to_core(tok_mine)], axis=0)
    (mlp_piece,) = call(
        mlp_piece_kernel,
        [out((2, 64, 2048))],
        (keep_up, got_up, w_down, out_own, tok_mine),
        [whole((32, 2048))] * 2 + [whole((128, 2048)), any_place, any_place],
        [whole((2, 64, 2048))],
        scalars=(sp,),
        vmem=16,
    )
    mlp_w = lax.all_gather(mlp_piece, ZXC, axis=0)

    qkv_all, vecs, lens = call(
        qkv_kernel,
        [out((1024, 768)), out((16, 2048), f32), out((16, 128), f32)],
        (tok_all, qkv_w, qkv_w),
        [
            whole((1024, 2048)),
            pl.BlockSpec((32, 64, 256), lambda n, sp: (0, 0, sp[CC] * 3 + n)),
            pl.BlockSpec((32, 16, 128), lambda n, sp: (0, 0, 12)),
        ],
        [
            pl.BlockSpec((1024, 256), lambda n, sp: (0, n)),
            whole((16, 2048)),
            whole((16, 128)),
        ],
        grid=(3,),
        scalars=(sp,),
        vmem=60,
    )
    lens = lens[4, :4].astype(i32)
    qkv_all = qkv_all.reshape(2, 2, 2, 128, 768)
    (ctx_all,) = call(
        attend_kernel,
        [out((2, 2, 2, 128, 256))],
        (qkv_all,),
        [group_block(768)],
        [group_block(256)],
        grid=(2, 2),
        scalars=(sp, lens),
        vmem=16,
    )
    ctx_all = ctx_all.reshape(2, 512, 256)
    ctx_got = to_core(ctx_all)
    ctx, *attn_parts = call(
        out_kernel,
        [out((512, 512))] + [out((64, 2048))] * 8,
        (ctx_all, ctx_got, proj),
        [
            pl.BlockSpec((1, 512, 256), lambda n, sp: (0, 0, 0)),
            pl.BlockSpec((1, 512, 256), lambda n, sp: (1, 0, 0)),
            pl.BlockSpec((512, 512), lambda n, sp: (0, n)),
        ],
        [whole((512, 512))] + [pl.BlockSpec((64, 512), lambda n, sp: (0, n))] * 8,
        grid=(4,),
        scalars=(sp,),
    )
    vec_block, rows, halves = whole((16, 2048)), whole((64, 2048)), (0, 1)
    tok_half = [pl.BlockSpec((64, 2048), lambda *_, h=h: (h, 0)) for h in halves]
    norm_outs = [
        call(
            functools.partial(norm_one_kernel, h),
            [out((64, 2048)), out((64, 2048), f32), out((64, 128), f32), out((8, 128), f32)],
            (*sum_parts(attn_parts[h::2], Y4), tok, vecs),
            [rows] * 4 + [tok_half[h], vec_block],
            [rows, rows, whole((64, 128)), whole((8, 128))],
            scalars=(sp,),
            vmem=16,
        )
        for h in halves
    ]
    norm_one = [o[1] for o in norm_outs]
    scale_one = [o[2] for o in norm_outs]

    four = [rows] * 4
    group = whole((256, 2048))
    mark = out((8, 128), f32)
    mlp_out = [out((256, 2048))] * 3 + [mark] + [out((64, 2048))] * 4
    placed, anywhere = pl.BlockSpec(memory_space=pltpu.VMEM), pl.BlockSpec(memory_space=pl.ANY)
    *first_out, up_held, down_held = pl.pallas_call(
        mlp_first_kernel,
        in_specs=[placed] * 4 + [anywhere] * 2,
        out_specs=[placed] * 10,
        out_shape=mlp_out + [pltpu.VMEM((32, 64, 2048), bf16)] * 2,
        scratch_shapes=[pltpu.SemaphoreType.DMA((8,))],
        compiler_params=pltpu.CompilerParams(vmem_limit_bytes=14 * MIB),
        cost_estimate=pl.CostEstimate(flops=1000, bytes_accessed=1000, transcendentals=0),
    )(
        *y_gather(norm_outs[0][0]),
        norm_outs[0][3],
        pltpu.with_memory_space_constraint(mlp_w, pltpu.HBM),
    )
    mlp_held = (up_held, down_held)
    mlp_outs = [
        first_out,
        call_resident(
            mlp_kernel, mlp_out, (*y_gather(norm_outs[1][0]), first_out[3]), mlp_held
        ),
    ]
    two_outs = [
        call(
            functools.partial(norm_two_kernel, h),
            [
                out((64, 2048)),
                out((64, 2048)),
                out((64, 2048), f32),
                out((8, 2048), f32),
                out((8, 128), f32),
            ],
            (*sum_parts(mlp_outs[h][4:], Y4), norm_one[h], vecs, cot, norm_outs[h][3]),
            four + [rows, vec_block, tok_half[h], whole((8, 128))],
            [rows, rows, rows, whole((8, 2048)), whole((8, 128))],
            scalars=(sp,),
            vmem=16,
        )
        for h in halves
    ]
    output = jnp.concatenate([two_outs[h][0] for h in halves], axis=0)

    back_outs = []
    for h in halves:
        after = back_outs[0][2] if h else two_outs[0][4]
        back_outs.append(
            call_resident(
                mlp_back_kernel,
                [out((256, 2048))] * 2 + [mark] + [out((64, 2048))] * 4,
                (*y_gather(two_outs[h][1]), mlp_outs[h][1], after),
                mlp_held,
            )
        )
    hidden_terms = [sum_parts(back_outs[h][3:], Y4) for h in halves]

    def norm_one_back(h, after):
        return call(
            norm_one_back_kernel,
            [out((64, 2048)), out((64, 2048), f32), out((8, 2048), f32)],
            (*hidden_terms[h], two_outs[h][2], norm_one[h], scale_one[h], vecs, after),
            four + [rows, rows, whole((64, 128)), vec_block, any_place],
            [rows, rows, whole((8, 2048))],
            vmem=16,
            cost=300_000_000_000 if h else 1000,
        )

    one_outs = [norm_one_back(0, back_outs[0][2])]
    hidden_col = pl.BlockSpec((256, 512), lambda w, n: (0, jnp.where(w == 0, n, 3)))
    act_col = pl.BlockSpec((256, 512), lambda w, n: (0, jnp.where(w == 1, n, 0)))
    mlp_terms, terms_mark = call(
        mlp_terms_kernel,
        [out((32, 2, 64, 2048)), mark],
        (
            *(mlp_outs[h][2] for h in halves),
            *(back_outs[h][0] for h in halves),
            *(mlp_outs[h][0] for h in halves),
            *(back_outs[h][1] for h in halves),
            one_outs[0][2],
        ),
        [hidden_col] * 2 + [group] * 2 + [act_col] * 2 + [group] * 2 + [any_place],
        [pl.BlockSpec((8, 1, 64, 2048), lambda w, n: (n, w, 0, 0)), whole((8, 128))],
        grid=(2, 4),
        vmem=60,
    )
    one_outs.append(norm_one_back(1, terms_mark))
    attn_gathers = [y_gather(one_outs[h][0]) for h in halves]
    mlp_sum = lax.psum_scatter(mlp_terms, ZXC, scatter_dimension=0, tiled=True)
    mlp_sum = mlp_sum.reshape(2, 64, 2048)
    ctx_grad, ctx_grad_send, grad_attn = call(
        ctx_back_kernel,
        [out((512, 256)), out((512, 256)), out((512, 2048))],
        (*attn_gathers[0], *attn_gathers[1], proj),
        four * 2 + [whole((512, 2048))],
        [whole((512, 256)), whole((512, 256)), whole((512, 2048))],
        scalars=(sp,),
        vmem=16,
    )
    ctx_grad_got = to_core(ctx_grad_send)
    proj_block = pl.BlockSpec((4, 64, 512), lambda n, sp: (0, 0, n))
    proj_terms, proj_send = call(
        proj_terms_kernel,
        [out((4, 64, 2048))] * 2,
        (ctx, grad_attn),
        [whole((512, 512)), pl.BlockSpec((512, 512), lambda n, sp: (0, n))],
        [proj_block, proj_block],
        grid=(4,),
        scalars=(sp,),
        scratch=[pltpu.VMEM((512, 512), bf16)],
    )
    proj_got = to_core(proj_send)
    half_block = pl.BlockSpec((2, 1, 128, 256), lambda e, p, *_: (0, p, 0, 0))
    (qkv_grad,) = call(
        attend_back_kernel,
        [out((2, 2, 2, 128, 768))],
        (qkv_all, ctx_grad.reshape(2, 2, 128, 256), ctx_grad_got.reshape(2, 2, 128, 256)),
        [group_block(768), half_block, half_block],
        [group_block(768)],
        grid=(2, 2),
        scalars=(sp, lens),
        vmem=16,
        cost=20_000_000_000,
    )
    qkv_grad = qkv_grad.reshape(2, 512, 768)
    qkv_grad_got = to_core(qkv_grad)

    step_vec = pl.BlockSpec((8, 512), lambda n, sp: (0, n))
    blocks = call(
        qkv_terms_kernel,
        [out((4, 144, 512))] * 4 + [out((2048, 128))] * 4,
        (
            tok_all,
            qkv_grad.reshape(1024, 768),
            *(one_outs[h][2] for h in halves),
            *(two_outs[h][3] for h in halves),
            *(two_outs[h][4] for h in halves),
            proj_terms,
            proj_got,
            qkv_grad_got,
        ),
        [
            pl.BlockSpec((1024, 512), lambda n, sp: (0, n)),
            whole((1024, 768)),
            *[step_vec] * 4,
            whole((8, 128)),
            whole((8, 128)),
            proj_block,
            proj_block,
            any_place,
        ],
        [whole((4, 144, 512))] * 4 + [whole((2048, 128))] * 4,
        grid=(4,),
        scalars=(sp,),
        scratch=[pltpu.VMEM((512, 768), bf16)],
        cost=20_000_000_000,
    )
    a_terms, b_terms = sum_parts(blocks[:4], "z"), sum_parts(blocks[4:], "x")
    tok_parts = call(
        tok_back_kernel,
        [out((128, 2048))] * 4,
        (qkv_grad, qkv_grad_got, qkv_w, b_terms[1]),
        [
            pl.BlockSpec((1, 512, 768), lambda n, sp: (0, 0, 0)),
            pl.BlockSpec((1, 512, 768), lambda n, sp: (1, 0, 0)),
            pl.BlockSpec((4, 64, 1536), lambda n, sp: (n, 0, 0)),
            any_place,
        ],
        [pl.BlockSpec((128, 256), lambda n, sp: (0, n))] * 4,
        grid=(8,),
        scalars=(sp,),
        scratch=[pltpu.VMEM((512, 1536), bf16)],
    )
    input_grad, grad_mark = call(
        last_kernel,
        [out((128, 2048), f32), mark],
        (*sum_parts(tok_parts, Y4), one_outs[0][1], one_outs[1][1]),
        [whole((128, 2048))] * 4 + [rows] * 2,
        [whole((128, 2048)), whole((8, 128))],
        vmem=16,
    )

    a_line, proj_line, *b_line = call(
        middle_kernel,
        [out((4, 144, 512)), out((64, 2048))] + [out((128, 256))] * 4,
        (*a_terms, *b_terms),
        [whole((4, 144, 512))] * 4 + [whole((2048, 128))] * 4,
        [whole((4, 144, 512)), whole((64, 2048))] + [whole((128, 256))] * 4,
        vmem=60,
        cost=20_000_000_000,
    )
    pieces, near, away = call(
        pieces_kernel,
        [out((8, 48, 768))] + [out((32, 2048))] * 2,
        (
            lax.all_to_all(a_line, "x", 0, 0, tiled=True),
            *sum_parts(b_line, "z"),
            proj_line,
            *(diagonal(proj_line, False, by) for by in (1, 2, 3)),
            grad_mark,
        ),
        [whole((4, 144, 512))]
        + [whole((128, 256))] * 4
        + [whole((64, 2048))] * 4
        + [any_place],
        [whole((8, 48, 768))] + [whole((32, 2048))] * 2,
        scalars=(sp,),
        scratch=[pltpu.VMEM((64, 2048), bf16)],
        vmem=60,
        cost=20_000_000_000,
    )
    arrived = lax.all_to_all(pieces, Y8, 0, 0, tiled=True)
    given = [along_y(away, 1), along_y(near, 2), along_y(away, 3)]
    rep_part, up_away = call(
        mlp_split_kernel,
        [out((96, 2048)), out((32, 2048))],
        (mlp_sum, near),
        [whole((2, 64, 2048)), any_place],
        [whole((96, 2048)), whole((32, 2048))],
        scalars=(sp,),
        vmem=60,
    )
    grad_up, grad_down, mlp_mark = call(
        final_mlp_kernel,
        [out((32, 8192), f32), out((128, 2048), f32), mark],
        (
            mlp_sum,
            lax.ppermute(up_away, Y4, xored(1, 4)),
            lax.ppermute(rep_part, Y4, xored(2, 4)),
            lax.ppermute(up_away, Y4, xored(3, 4)),
        ),
        [whole((2, 64, 2048)), whole((32, 2048)), whole((96, 2048)), whole((32, 2048))],
        [whole((32, 8192)), whole((128, 2048)), whole((8, 128))],
        scalars=(sp,),
        vmem=60,
    )
    one_row = whole((1, 32))
    grad_q, grad_k, grad_v, grad_proj, g1, s1, g2, s2, rms = call(
        final_kernel,
        [out((32, 2048), f32)] * 4 + [out((1, 32), f32)] * 4 + [out((1, 128), f32)],
        (arrived, near, *given),
        [whole((8, 48, 768))] + [whole((32, 2048))] * 4,
        [whole((32, 2048))] * 4 + [one_row] * 4 + [whole((1, 128))],
        scalars=(sp,),
        vmem=60,
        cost=300_000_000_000,
    )
    vec_mine = [v.reshape(32) for v in (g1, s1, g2, s2)]
    rms_stats = rms[0, :3]
    return (
        output.reshape(1, 128, 2048),
        input_grad.reshape(1, 128, 2048),
        grad_q,
        grad_k,
        grad_v,
        grad_proj,
        vec_mine[0],
        vec_mine[1],
        grad_up,
        grad_down,
        vec_mine[2],
        vec_mine[3],
        rms_stats,
    )


def solution(mesh):
    split = Mesh(mesh.devices.reshape(2, 4, 4, 2, 2), AXES)
    rows, vec, seq = P(SHARD, None), P(SHARD), P(SHARD, "rep", None)
    return jax.shard_map(
        per_device,
        mesh=split,
        in_specs=(seq, vec, rows, rows, rows, rows, vec, vec, rows, rows, vec, vec, seq),
        out_specs=(seq, seq, rows, rows, rows, rows, vec, vec, rows, rows, vec, vec, P()),
        check_vma=False,
    )
```

```python
import functools

import jax
import jax.numpy as jnp
from jax import lax
from jax.experimental import pallas as pl
from jax.experimental.pallas import tpu as pltpu
from jax.sharding import Mesh
from jax.sharding import PartitionSpec as P

HEAD_DIM = 128
AXES = ("rep", "z", "x", "yl", "c")
SHARD = ("z", "x", "yl", "c")
ZXC = ("z", "x", "c")
Y4 = ("rep", "yl")
Y8 = ("rep", "yl", "c")
norm_eps = 1e-12
masked_score = -1e30
bf16 = jnp.bfloat16
f32 = jnp.float32
i32 = jnp.int32
MIB = 1 << 20
REP, ZZ, XX, YL, CC, LEN = range(6)


def shifted(by, count=4):
    return [(i, (i + by) % count) for i in range(count)]


def xored(by, count):
    return [(i, i ^ by) for i in range(count)]


def from_offset(value, axes, offset):
    return lax.ppermute(value, axes, shifted(-offset))


def to_core(value):
    return lax.ppermute(value, "c", xored(1, 2))


def y_gather(value):
    return [value] + [from_offset(value, Y4, d) for d in (1, 2, 3)]


def x_gather(value):
    return [value] + [from_offset(value, "x", d) for d in (1, 2, 3)]


def sum_parts(parts, axis):
    return [parts[0]] + [lax.ppermute(parts[d], axis, shifted(d)) for d in (1, 2, 3)]


def diagonal(value, to_z, by):
    pairs = []
    for rep in range(2):
        for yl in range(2):
            y = rep * 2 + yl
            at = lambda z: rep * 8 + (z % 4) * 2 + yl
            pairs.append((at(y), at(y + by)) if to_z else (at(y - by), at(y)))
    return lax.ppermute(value, ("rep", "z", "yl"), pairs)


def along_y(value, by):
    pairs = []
    for y in range(4):
        at = lambda v: ((v % 4) // 2) * 8 + y * 2 + v % 2
        pairs.append((at(y), at(y + by)))
    return lax.ppermute(value, ("rep", "z", "yl"), pairs)


def call(kernel, outs, operands, specs, out_specs, grid=(1,), scalars=(), scratch=(), vmem=28, cost=1000):
    return pl.pallas_call(
        kernel,
        grid_spec=pltpu.PrefetchScalarGridSpec(
            num_scalar_prefetch=len(scalars),
            grid=grid,
            in_specs=specs,
            out_specs=out_specs,
            scratch_shapes=scratch,
        ),
        out_shape=outs,
        compiler_params=pltpu.CompilerParams(vmem_limit_bytes=vmem * MIB),
        cost_estimate=pl.CostEstimate(flops=cost, bytes_accessed=1000, transcendentals=0),
    )(*scalars, *operands)


def call_resident(kernel, outs, operands, weights, vmem=14):
    place = pl.BlockSpec(memory_space=pltpu.VMEM)
    held = [pltpu.with_memory_space_constraint(w, pltpu.VMEM) for w in weights]
    return pl.pallas_call(
        kernel,
        in_specs=[place] * (len(operands) - 1)
        + [pl.BlockSpec(memory_space=pl.ANY)]
        + [place] * len(weights),
        out_specs=[place] * len(outs),
        out_shape=outs,
        compiler_params=pltpu.CompilerParams(vmem_limit_bytes=vmem * MIB),
        cost_estimate=pl.CostEstimate(flops=1000, bytes_accessed=1000, transcendentals=0),
    )(*operands, *held)


def out(shape, dtype=bf16):
    return jax.ShapeDtypeStruct(shape, dtype)


def whole(shape):
    return pl.BlockSpec(shape, lambda *_: (0,) * len(shape))


def swap_middle(value):
    width = value.shape[1]
    chunk = (lax.broadcasted_iota(i32, value.shape, 1) >> 5) & 3
    ahead = pltpu.roll(value, width - 32, 1)
    behind = pltpu.roll(value, 32, 1)
    return jnp.where(chunk == 1, ahead, jnp.where(chunk == 2, behind, value))


def swap_kernel(tok_ref, out_ref):
    out_ref[...] = swap_middle(tok_ref[...].astype(f32)).astype(bf16)


def prep_kernel(sp, wq_ref, wk_ref, wv_ref, g1, s1, g2, s2, keep_ref, send_ref):
    rep, yl = sp[REP], sp[YL]
    s = yl * 2 + sp[CC]
    lane = lax.broadcasted_iota(i32, (1, 128), 1)
    rows = []
    for ref in (g1, s1, g2, s2):
        value = ref[...].astype(f32)
        tiled = jnp.concatenate([value, value, value, value], axis=1)
        rows.append(jnp.where((lane >> 5) == s, tiled, 0.0))
    rows.append(jnp.where(lane == s, sp[LEN].astype(f32), 0.0))
    vec = jnp.concatenate(rows + [jnp.zeros((27, 128), f32)], axis=0).astype(bf16)
    keep_ref[:, 1536:] = vec
    send_ref[:, 1536:] = vec
    for target, dest in ((yl, keep_ref), (1 - yl, send_ref)):
        for i, ref in enumerate((wq_ref, wk_ref, wv_ref)):
            start = pl.multiple_of((rep * 2 + target) * 512, 512)
            block = ref[:, pl.ds(start, 512)]
            for head in range(4):
                dest[:, (head * 3 + i) * 128 : (head * 3 + i + 1) * 128] = block[
                    :, head * 128 : (head + 1) * 128
                ]


def prep_up_kernel(sp, up_ref, keep_ref, send_ref):
    rep, yl = sp[REP], sp[YL]
    for target, dest in ((yl, keep_ref), (1 - yl, send_ref)):
        for zx in range(16):
            start = pl.multiple_of(zx * 512 + target * 256, 256)
            block = up_ref[:, pl.ds(start, 256)]
            low = jnp.concatenate([block[:, 0:64], block[:, 128:192]], axis=1)
            high = jnp.concatenate([block[:, 64:128], block[:, 192:256]], axis=1)
            dest[:, zx * 128 : (zx + 1) * 128] = jnp.where(rep == 0, low, high)


def qkv_piece_kernel(sp, keep_ref, got_ref, out_ref):
    own = pl.ds(pl.multiple_of(sp[YL] * 32, 32), 32)
    other = pl.ds(pl.multiple_of((1 - sp[YL]) * 32, 32), 32)
    out_ref[own, :1536] = keep_ref[:, :1536]
    out_ref[other, :1536] = got_ref[:, :1536]
    vec = (keep_ref[:, 1536:].astype(f32) + got_ref[:, 1536:].astype(f32)).astype(bf16)
    out_ref[0:32, 1536:] = vec
    out_ref[32:64, 1536:] = jnp.zeros_like(vec)


def mlp_piece_kernel(sp, keep_ref, got_ref, down_ref, after1_ref, after2_ref, out_ref):
    own = pl.ds(pl.multiple_of(sp[YL] * 32, 32), 32)
    other = pl.ds(pl.multiple_of((1 - sp[YL]) * 32, 32), 32)
    out_ref[0, own, :] = keep_ref[...]
    out_ref[0, other, :] = got_ref[...]
    out_ref[1] = down_ref[pl.ds(pl.multiple_of(sp[REP] * 64, 64), 64), :]


def cat_kernel(t0, t1, t2, t3, after_ref, out_ref):
    for d, ref in enumerate((t0, t1, t2, t3)):
        out_ref[d * 128 : (d + 1) * 128, :] = ref[...]


def out_rows_kernel(sp, own_ref, got_ref, out_ref):
    out_ref[pl.ds(pl.multiple_of(sp[YL] * 32, 32), 32), :] = own_ref[...]
    out_ref[pl.ds(pl.multiple_of((1 - sp[YL]) * 32, 32), 32), :] = got_ref[...]


def proj_kernel(sp, own_ref, other_ref, proj_ref):
    for d in range(4):
        for ref, core in ((own_ref, sp[CC]), (other_ref, 1 - sp[CC])):
            for yl_of in range(2):
                row = pl.multiple_of(((sp[XX] + d) & 3) * 128 + yl_of * 64 + core * 32, 32)
                proj_ref[pl.ds(row, 32), :] = ref[d, yl_of * 32 : (yl_of + 1) * 32, :]


def qkv_kernel(sp, tok_ref, w_ref, vec_in_ref, out_ref, vec_ref, len_ref):
    @pl.when(pl.program_id(0) == 0)
    def _():
        for zx in range(16):
            pair = vec_in_ref[2 * zx].astype(f32) + vec_in_ref[2 * zx + 1].astype(f32)
            vec_ref[:, zx * 128 : (zx + 1) * 128] = pair
        own = (sp[ZZ] * 4 + sp[XX]) * 2
        len_ref[...] = vec_in_ref[own].astype(f32) + vec_in_ref[own + 1].astype(f32)

    weights = w_ref[...].reshape(2048, 256)
    out_ref[...] = jnp.dot(tok_ref[...], weights, preferred_element_type=f32).astype(bf16)


def softmax_of(q, k, open_row):
    raw = lax.dot_general(q, k, (((1,), (1,)), ((), ())), preferred_element_type=f32)
    scores = jnp.where(open_row, raw * (HEAD_DIM**-0.5), masked_score)
    top = jnp.max(scores, axis=-1, keepdims=True)
    exponent = jnp.exp(scores - top)
    return exponent * (1.0 / jnp.sum(exponent, axis=-1, keepdims=True))


def open_keys(sp, lens):
    e, p = pl.program_id(0), pl.program_id(1)
    length = lens[((sp[YL] + p) & 1) * 2 + ((sp[CC] + e) & 1)]
    swap = ((sp[REP] * 2 + sp[YL] + p) & 3) >> 1
    lane = lax.broadcasted_iota(i32, (1, 256), 1)
    position = jnp.where(swap == 1, (lane + 128) & 255, lane)
    return position < length


def head_part(ref, head, i):
    return ref[0, :, 0, :, (head * 3 + i) * 128 : (head * 3 + i + 1) * 128].reshape(256, 128)


def attend_kernel(sp, lens, qkv_ref, ctx_ref):
    open_row = open_keys(sp, lens)
    for head in range(2):
        q, k, v = (head_part(qkv_ref, head, i) for i in range(3))
        probs = softmax_of(q, k, open_row).astype(bf16)
        ctx = jnp.dot(probs, v, preferred_element_type=f32).astype(bf16)
        ctx_ref[0, :, 0, :, head * 128 : (head + 1) * 128] = ctx.reshape(2, 128, 128)


def attend_back_kernel(sp, lens, qkv_ref, own_ref, other_ref, out_ref):
    open_row = open_keys(sp, lens)
    scale = HEAD_DIM**-0.5
    first = pl.program_id(0) == 0
    for head in range(2):
        q, k, v = (head_part(qkv_ref, head, i) for i in range(3))
        cols = slice(head * 128, (head + 1) * 128)
        grad = jnp.where(first, own_ref[:, 0, :, cols], other_ref[:, 0, :, cols]).reshape(256, 128)
        probs = softmax_of(q, k, open_row)
        grad_probs = lax.dot_general(grad, v, (((1,), (1,)), ((), ())), preferred_element_type=f32)
        inner = jnp.sum(probs * grad_probs, axis=-1, keepdims=True)
        grad_scores = (probs * (grad_probs - inner)).astype(bf16)
        grad_q = jnp.dot(grad_scores, k, preferred_element_type=f32) * scale
        over = (((0,), (0,)), ((), ()))
        grad_k = lax.dot_general(grad_scores, q, over, preferred_element_type=f32) * scale
        grad_v = lax.dot_general(probs.astype(bf16), grad, over, preferred_element_type=f32)
        for i, part in enumerate((grad_q, grad_k, grad_v)):
            out_ref[0, :, 0, :, (head * 3 + i) * 128 : (head * 3 + i + 1) * 128] = part.astype(
                bf16
            ).reshape(2, 128, 128)


def group_block(columns):
    return pl.BlockSpec((1, 2, 1, 128, columns), lambda e, p, *_: (e, 0, p, 0, 0))


def to_four(result, refs):
    rows = result.shape[0] // len(refs)
    for d, ref in enumerate(refs):
        ref[...] = result[d * rows : (d + 1) * rows].astype(bf16)


def out_kernel(sp, own_ref, got_ref, proj_ref, ctx_ref, *refs):
    @pl.when(pl.program_id(0) == 0)
    def _():
        ctx_ref[:, pl.ds(pl.multiple_of(sp[CC] * 256, 256), 256)] = own_ref[0]
        ctx_ref[:, pl.ds(pl.multiple_of((1 - sp[CC]) * 256, 256), 256)] = got_ref[0]

    to_four(jnp.dot(ctx_ref[...], proj_ref[...], preferred_element_type=f32), refs)


def terms_of(refs):
    return sum(r[...].astype(f32) for r in refs[1:]) + refs[0][...].astype(f32)


def valid_rows(sp, half):
    position = sp[REP] * 128 + half * 64 + lax.broadcasted_iota(i32, (64, 1), 0)
    return (position < sp[LEN]).astype(f32)


def lane_of(values):
    lane = lax.broadcasted_iota(i32, (8, 128), 1)
    total = jnp.zeros((8, 128), f32)
    for i, value in enumerate(values):
        total = jnp.where(lane == i, value, total)
    return total


def normed(values):
    center = values - jnp.mean(values, axis=-1, keepdims=True)
    spread = jnp.mean(center * center, axis=-1, keepdims=True)
    scale = lax.rsqrt(spread + norm_eps)
    return center * scale, scale


def norm_one_kernel(half, sp, p0, p1, p2, p3, tok_ref, vec_ref, hidden_ref, norm_ref, scale_ref, stat_ref):
    attn = terms_of((p0, p1, p2, p3))
    resid = tok_ref[...].astype(f32) + attn
    norm, scale = normed(resid)
    hidden = norm * vec_ref[0:1, :] + vec_ref[1:2, :]
    hidden_ref[...] = swap_middle(hidden).astype(bf16)
    norm_ref[...] = norm
    scale_ref[...] = jnp.broadcast_to(scale, scale_ref.shape)
    valid = valid_rows(sp, half)
    stat_ref[...] = lane_of((jnp.sum(valid * (resid * resid)), jnp.sum(valid * (attn * attn))))


def norm_two_kernel(
    half, sp, p0, p1, p2, p3, norm_ref, vec_ref, cot_ref, stat_ref, out_ref, low_ref, grad_ref, vg_ref, st_ref
):
    mlp = terms_of((p0, p1, p2, p3))
    resid = norm_ref[...] * vec_ref[0:1, :] + vec_ref[1:2, :] + mlp
    norm, scale = normed(resid)
    out_ref[...] = (norm * vec_ref[2:3, :] + vec_ref[3:4, :]).astype(bf16)
    valid = valid_rows(sp, half)
    grad_out = cot_ref[...].astype(f32) * valid
    vg_ref[0:1, :] = jnp.sum(grad_out * norm, axis=0, keepdims=True)
    vg_ref[1:2, :] = jnp.sum(grad_out, axis=0, keepdims=True)
    e = grad_out * vec_ref[2:3, :]
    mean_e = jnp.mean(e, axis=-1, keepdims=True)
    mean_en = jnp.mean(e * norm, axis=-1, keepdims=True)
    grad = scale * (e - mean_e - norm * mean_en)
    grad_ref[...] = grad
    low_ref[...] = grad.astype(bf16)
    lane = lax.broadcasted_iota(i32, (8, 128), 1)
    more = jnp.where(lane == 2, jnp.sum(valid * (mlp * mlp)), jnp.sum(valid))
    st_ref[...] = jnp.where(lane < 2, stat_ref[...], more)


def norm_one_back_kernel(
    p0, p1, p2, p3, grad2_ref, norm_ref, scale_ref, vec_ref, after_ref, low_ref, grad_ref, vg_ref
):
    grad = grad2_ref[...] + swap_middle(terms_of((p0, p1, p2, p3)))
    norm = norm_ref[...]
    vg_ref[0:1, :] = jnp.sum(grad * norm, axis=0, keepdims=True)
    vg_ref[1:2, :] = jnp.sum(grad, axis=0, keepdims=True)
    e = grad * vec_ref[0:1, :]
    mean_e = jnp.mean(e, axis=-1, keepdims=True)
    mean_en = jnp.mean(e * norm, axis=-1, keepdims=True)
    back = scale_ref[:, 0:1] * (e - mean_e - norm * mean_en)
    grad_ref[...] = back
    low_ref[...] = back.astype(bf16)


def last_kernel(p0, p1, p2, p3, grad_a_ref, grad_b_ref, out_ref, mark_ref):
    mark_ref[...] = jnp.zeros_like(mark_ref)
    total = swap_middle(terms_of((p0, p1, p2, p3)))
    out_ref[0:64, :] = grad_a_ref[...] + total[0:64]
    out_ref[64:128, :] = grad_b_ref[...] + total[64:128]


CHUNKS = [slice(i * 512, (i + 1) * 512) for i in range(4)]
UNITS = [slice(i * 8, (i + 1) * 8) for i in range(4)]


def join(refs, all_ref):
    for d, ref in enumerate(refs):
        all_ref[d * 64 : (d + 1) * 64, :] = ref[...]


def split_rows(result, refs, columns):
    for d, ref in enumerate(refs):
        ref[:, columns] = result[d * 64 : (d + 1) * 64].astype(bf16)


def mlp_kernel(
    h0, h1, h2, h3, after_ref, up_ref, down_ref, act_ref, slope_ref, all_ref, mark_ref, *refs,
    arrived=lambda i: None,
):
    mark_ref[...] = jnp.zeros_like(mark_ref)
    join((h0, h1, h2, h3), all_ref)
    root = 0.7978845608028654
    for i, chunk in enumerate(CHUNKS):
        arrived(i)
        up = up_ref[:, :, chunk].reshape(2048, 512)
        v = jnp.dot(all_ref[...], up, preferred_element_type=f32)
        square = v * v
        t = jnp.tanh(root * v * (1.0 + 0.044715 * square))
        half = 0.5 * (1.0 + t)
        act_ref[:, chunk] = (v * half).astype(bf16)
        slope = half + 0.5 * v * (1.0 - t * t) * (root * (1.0 + 3 * 0.044715 * square))
        slope_ref[:, chunk] = slope.astype(bf16)
    for i, chunk in enumerate(CHUNKS):
        arrived(4 + i)
        down = down_ref[:, :, chunk].reshape(2048, 512)
        split_rows(jnp.dot(act_ref[...], down, preferred_element_type=f32), refs, chunk)


def mlp_first_kernel(h0, h1, h2, h3, after_ref, w_ref, act_ref, slope_ref, all_ref, mark_ref, *rest):
    refs, (up_ref, down_ref, sem) = rest[:4], rest[4:]
    copies = [
        pltpu.make_async_copy(w_ref.at[:, i, :, chunk], ref.at[:, :, chunk], sem.at[i * 4 + j])
        for i, ref in enumerate((up_ref, down_ref))
        for j, chunk in enumerate(pl.ds(k * 512, 512) for k in range(4))
    ]
    for copy in copies[:3]:
        copy.start()

    def arrived(i):
        copies[i].wait()
        if i + 3 < 8:
            copies[i + 3].start()

    mlp_kernel(
        h0, h1, h2, h3, after_ref, up_ref, down_ref, act_ref, slope_ref, all_ref, mark_ref, *refs,
        arrived=arrived,
    )


BACK = (((1,), (1,)), ((), ()))
OVER = (((0,), (0,)), ((), ()))


def mlp_back_kernel(
    g0, g1, g2, g3, slope_ref, after_ref, up_ref, down_ref, pre_ref, all_ref, mark_ref, *refs
):
    mark_ref[...] = jnp.zeros_like(mark_ref)
    join((g0, g1, g2, g3), all_ref)
    for chunk, units in zip(CHUNKS, UNITS):
        down = down_ref[units].reshape(512, 2048)
        grad = lax.dot_general(all_ref[...], down, BACK, preferred_element_type=f32)
        pre_ref[:, chunk] = (grad * slope_ref[:, chunk].astype(f32)).astype(bf16)
    for chunk, units in zip(CHUNKS, UNITS):
        up = up_ref[units].reshape(512, 2048)
        term = lax.dot_general(pre_ref[...], up, BACK, preferred_element_type=f32)
        split_rows(term, refs, chunk)


def mlp_terms_kernel(h0, h1, p0, p1, a0, a1, g0, g1, after_ref, out_ref, mark_ref):
    mark_ref[...] = jnp.zeros_like(mark_ref)

    def both(left, right):
        total = sum(
            lax.dot_general(l[...], r[...], OVER, preferred_element_type=f32)
            for l, r in zip(left, right)
        )
        out_ref[...] = total.astype(bf16).reshape(out_ref.shape)

    @pl.when(pl.program_id(0) == 0)
    def _():
        both((h0, h1), (p0, p1))

    @pl.when(pl.program_id(0) == 1)
    def _():
        both((a0, a1), (g0, g1))


def ctx_back_kernel(sp, *refs):
    proj_ref, own_ref, other_ref, all_ref = refs[8:]
    for i, ref in enumerate(refs[:8]):
        row = (i % 4) * 128 + (i // 4) * 64
        all_ref[row : row + 64, :] = ref[...]
    for ref, core in ((own_ref, sp[CC]), (other_ref, 1 - sp[CC])):
        weights = proj_ref[pl.ds(pl.multiple_of(core * 256, 256), 256), :]
        ref[...] = lax.dot_general(
            all_ref[...], weights, BACK, preferred_element_type=f32
        ).astype(bf16)


def proj_terms_kernel(sp, ctx_ref, grad_ref, mine_ref, send_ref, term_ref):
    term = lax.dot_general(ctx_ref[...], grad_ref[...], OVER, preferred_element_type=f32)
    term_ref[...] = term.astype(bf16)
    for d in range(4):
        for ref, core in ((mine_ref, sp[CC]), (send_ref, 1 - sp[CC])):
            for yl_of in range(2):
                row = pl.multiple_of(((sp[XX] + d) & 3) * 128 + yl_of * 64 + core * 32, 32)
                ref[d, yl_of * 32 : (yl_of + 1) * 32, :] = term_ref[pl.ds(row, 32), :]


def qkv_terms_kernel(
    sp, tok_ref, grad_ref, v1a, v1b, v2a, v2b, sta, stb, mine_ref, got_ref, after_ref, *rest
):
    a_refs, b_refs, term_ref = rest[:4], rest[4:8], rest[8]
    term = lax.dot_general(tok_ref[...], grad_ref[...], OVER, preferred_element_type=f32)
    term_ref[...] = term.astype(bf16)
    step = pl.program_id(0)
    dz = (step - sp[ZZ]) & 3
    for dx in range(4):
        start = pl.multiple_of(((sp[XX] + dx) & 3) * 128, 128)
        rows = pl.ds(start, 128)
        vec = [v1a[0:2, rows] + v1b[0:2, rows], v2a[0:2, rows] + v2b[0:2, rows]]
        vec += [sta[0:4] + stb[0:4]]
        vec = jnp.concatenate(vec + [jnp.zeros((8, 128), f32)], axis=0).astype(bf16)
        vec = jnp.concatenate([vec, jnp.zeros((16, 384), bf16)], axis=1)
        for j in range(2):
            at = pl.multiple_of((dz * 2 + j) * 128, 128)
            b_refs[dx][pl.ds(at, 128), :] = term_ref[rows, 512 + j * 128 : 640 + j * 128]
        total = mine_ref[dx].astype(f32) + got_ref[dx].astype(f32)
        total = total.astype(bf16)
        for j in range(4):
            at = pl.multiple_of(1024 + (step * 4 + j) * 64, 64)
            b_refs[dx][pl.ds(at, 64), :] = total[:, j * 128 : (j + 1) * 128]
        for k in range(4):

            @pl.when(dz == k)
            def _():
                a_refs[k][(sp[XX] + dx) & 3, 0:128, :] = term_ref[rows, :512]
                a_refs[k][(sp[XX] + dx) & 3, 128:144, :] = vec


def middle_kernel(*refs):
    a, b = refs[0:4], refs[4:8]
    a_ref, proj_ref, b_refs = refs[8], refs[9], refs[10:14]
    a_ref[...] = terms_of(a).astype(bf16)
    total = terms_of(b).astype(bf16)
    for d in range(4):
        for j in range(2):
            at = (d * 2 + j) * 128
            b_refs[d][:, j * 128 : (j + 1) * 128] = total[at : at + 128]
    for j in range(16):
        proj_ref[:, j * 128 : (j + 1) * 128] = total[1024 + j * 64 : 1088 + j * 64]


def tok_back_kernel(sp, own_ref, got_ref, w_ref, after_ref, *rest):
    refs, cat_ref = rest[:4], rest[4]

    @pl.when(pl.program_id(0) == 0)
    def _():
        cat_ref[:, pl.ds(pl.multiple_of(sp[CC] * 768, 256), 768)] = own_ref[0]
        cat_ref[:, pl.ds(pl.multiple_of((1 - sp[CC]) * 768, 256), 768)] = got_ref[0]

    weights = w_ref[...].reshape(256, 1536)
    to_four(lax.dot_general(cat_ref[...], weights, BACK, preferred_element_type=f32), refs)


def pieces_kernel(sp, *refs):
    b, proj = refs[1:5], refs[5:9]
    out_ref, near_ref, away_ref, proj_ref = refs[10:14]
    first = terms_of([refs[0].at[x] for x in range(4)]).astype(bf16)
    second = terms_of(b).astype(bf16)
    for m in range(8):
        row = (m & 1) * 64 + ((m >> 1) & 1) * 32
        out_ref[m, 0:32, :512] = first[row : row + 32]
        out_ref[m, 0:32, 512:] = second[row : row + 32]
        out_ref[m, 32:48, :512] = first[128:144]
        out_ref[m, 32:48, 512:] = jnp.zeros((16, 256), bf16)
    proj_ref[...] = terms_of(proj).astype(bf16)
    near_ref[...] = proj_ref[pl.ds(pl.multiple_of(sp[YL] * 32, 32), 32), :]
    away_ref[...] = proj_ref[pl.ds(pl.multiple_of((1 - sp[YL]) * 32, 32), 32), :]


def final_kernel(sp, got_ref, *refs):
    near, given = refs[0], refs[1:4]
    q_ref, k_ref, v_ref, proj_ref, g1, s1, g2, s2, rms_ref = refs[6:]
    for m in range(8):
        for i, ref in enumerate((q_ref, k_ref, v_ref)):
            for head in range(2):
                at = m * 256 + head * 128
                ref[:, at : at + 128] = got_ref[
                    m, 0:32, (head * 3 + i) * 128 : (head * 3 + i + 1) * 128
                ].astype(f32)
    on_diagonal = sp[ZZ] == sp[REP] * 2 + sp[YL]
    proj_ref[...] = jnp.where(on_diagonal, near[...].astype(f32), terms_of(given))
    vec = sum(got_ref[m, 32:48, :128].astype(f32) for m in range(8))
    s = sp[YL] * 2 + sp[CC]
    own = jnp.where(s == 0, vec[:, 0:32], vec[:, 32:64])
    own = jnp.where(s == 2, vec[:, 64:96], own)
    own = jnp.where(s == 3, vec[:, 96:128], own)
    for i, ref in enumerate((g1, s1, g2, s2)):
        ref[...] = own[i : i + 1]
    rms_ref[...] = jnp.sqrt(vec[4:5] / (vec[4:5, 3:4] * 2048.0))


def mlp_split_kernel(sp, sum_ref, after_ref, rep_ref, away_ref):
    rep_ref[0:32, :] = sum_ref[0, pl.ds(pl.multiple_of(sp[YL] * 32, 32), 32), :]
    rep_ref[32:96, :] = sum_ref[1]
    away_ref[...] = sum_ref[0, pl.ds(pl.multiple_of((1 - sp[YL]) * 32, 32), 32), :]


def final_mlp_kernel(sp, own_ref, yl_ref, rep_ref, both_ref, up_ref, down_ref, mark_ref):
    mark_ref[...] = jnp.zeros_like(mark_ref)
    rep, yl = sp[REP], sp[YL]
    mine = own_ref[0, pl.ds(pl.multiple_of(yl * 32, 32), 32), :]
    first_rep, first_yl = rep == 0, yl == 0
    got = {(0, 0): mine, (0, 1): yl_ref[...], (1, 0): rep_ref[0:32], (1, 1): both_ref[...]}
    for yl_of in range(2):
        same = (yl == yl_of)
        near = jnp.where(same, got[0, 0], got[0, 1]).astype(f32)
        far = jnp.where(same, got[1, 0], got[1, 1]).astype(f32)
        low = jnp.where(first_rep, near, far)
        high = jnp.where(first_rep, far, near)
        for zx in range(16):
            for c in range(2):
                src = slice(zx * 128 + c * 64, zx * 128 + c * 64 + 64)
                at = zx * 512 + yl_of * 256 + c * 128
                up_ref[:, at : at + 128] = jnp.concatenate([low[:, src], high[:, src]], axis=1)
    own_rows = pl.ds(pl.multiple_of(rep * 64, 64), 64)
    far_rows = pl.ds(pl.multiple_of((1 - rep) * 64, 64), 64)
    down_ref[own_rows, :] = own_ref[1].astype(f32)
    down_ref[far_rows, :] = rep_ref[32:96].astype(f32)


def per_device(
    hidden_in,
    lengths,
    w_query,
    w_key,
    w_value,
    w_output,
    attn_gain,
    attn_shift,
    w_up,
    w_down,
    mlp_gain,
    mlp_shift,
    cotangent,
):
    rep, z, x, yl, c = (lax.axis_index(a) for a in AXES)
    s, y = yl * 2 + c, rep * 2 + yl
    any_place = pl.BlockSpec(memory_space=pl.ANY)
    tok = hidden_in.reshape(128, 2048)
    cot = cotangent.reshape(128, 2048)
    sp = jnp.stack([rep, z, x, yl, c, lengths[0], lengths[0], lengths[0]]).astype(i32)
    rows = whole((128, 2048))

    keep, send = call(
        prep_kernel,
        [out((32, 1664))] * 2,
        (
            w_query,
            w_key,
            w_value,
            *(v.reshape(1, 32) for v in (attn_gain, attn_shift, mlp_gain, mlp_shift)),
        ),
        [whole((32, 2048))] * 3 + [whole((1, 32))] * 4,
        [whole((32, 1664))] * 2,
        scalars=(sp,),
        vmem=60,
    )
    got = lax.ppermute(send, "yl", xored(1, 2))
    keep_up, send_up = call(
        prep_up_kernel,
        [out((32, 2048))] * 2,
        (w_up,),
        [whole((32, 8192))],
        [whole((32, 2048))] * 2,
        scalars=(sp,),
        vmem=60,
    )
    got_up = lax.ppermute(send_up, "yl", xored(1, 2))
    (qkv_piece,) = call(
        qkv_piece_kernel,
        [out((64, 1664))],
        (keep, got),
        [whole((32, 1664))] * 2,
        [whole((64, 1664))],
        scalars=(sp,),
        vmem=16,
    )
    qkv_w = lax.all_gather(qkv_piece, ZXC, axis=0)

    first_yl, on_diagonal = yl == 0, y == z
    out_got = lax.ppermute(w_output, "yl", xored(1, 2))
    (out_piece,) = call(
        out_rows_kernel,
        [out((64, 2048))],
        (w_output, out_got),
        [whole((32, 2048))] * 2,
        [whole((64, 2048))],
        scalars=(sp,),
        vmem=16,
    )
    spread = [diagonal(out_piece, True, by) for by in (1, 2, 3)]
    out_piece = jnp.where(on_diagonal, out_piece, spread[0] + spread[1] + spread[2])
    out_own = jnp.stack(x_gather(out_piece))
    block4 = whole((4, 64, 2048))
    (proj,) = call(
        proj_kernel,
        [out((512, 2048))],
        (out_own, to_core(out_own)),
        [block4, block4],
        [whole((512, 2048))],
        scalars=(sp,),
        vmem=16,
    )

    (tok_swapped,) = call(swap_kernel, [out((128, 2048))], (tok,), [rows], [rows], vmem=16)
    (tok_mine,) = call(
        cat_kernel,
        [out((512, 2048))],
        (*y_gather(tok_swapped), out_own),
        [rows] * 4 + [any_place],
        [whole((512, 2048))],
        vmem=16,
    )
    tok_all = jnp.concatenate([tok_mine, to_core(tok_mine)], axis=0)
    (mlp_piece,) = call(
        mlp_piece_kernel,
        [out((2, 64, 2048))],
        (keep_up, got_up, w_down, out_own, tok_mine),
        [whole((32, 2048))] * 2 + [whole((128, 2048)), any_place, any_place],
        [whole((2, 64, 2048))],
        scalars=(sp,),
        vmem=16,
    )
    mlp_w = lax.all_gather(mlp_piece, ZXC, axis=0)

    qkv_all, vecs, lens = call(
        qkv_kernel,
        [out((1024, 768)), out((16, 2048), f32), out((16, 128), f32)],
        (tok_all, qkv_w, qkv_w),
        [
            whole((1024, 2048)),
            pl.BlockSpec((32, 64, 256), lambda n, sp: (0, 0, sp[CC] * 3 + n)),
            pl.BlockSpec((32, 16, 128), lambda n, sp: (0, 0, 12)),
        ],
        [
            pl.BlockSpec((1024, 256), lambda n, sp: (0, n)),
            whole((16, 2048)),
            whole((16, 128)),
        ],
        grid=(3,),
        scalars=(sp,),
        vmem=60,
    )
    lens = lens[4, :4].astype(i32)
    qkv_all = qkv_all.reshape(2, 2, 2, 128, 768)
    (ctx_all,) = call(
        attend_kernel,
        [out((2, 2, 2, 128, 256))],
        (qkv_all,),
        [group_block(768)],
        [group_block(256)],
        grid=(2, 2),
        scalars=(sp, lens),
        vmem=16,
    )
    ctx_all = ctx_all.reshape(2, 512, 256)
    ctx_got = to_core(ctx_all)
    ctx, *attn_parts = call(
        out_kernel,
        [out((512, 512))] + [out((64, 2048))] * 8,
        (ctx_all, ctx_got, proj),
        [
            pl.BlockSpec((1, 512, 256), lambda n, sp: (0, 0, 0)),
            pl.BlockSpec((1, 512, 256), lambda n, sp: (1, 0, 0)),
            pl.BlockSpec((512, 512), lambda n, sp: (0, n)),
        ],
        [whole((512, 512))] + [pl.BlockSpec((64, 512), lambda n, sp: (0, n))] * 8,
        grid=(4,),
        scalars=(sp,),
    )
    vec_block, rows, halves = whole((16, 2048)), whole((64, 2048)), (0, 1)
    tok_half = [pl.BlockSpec((64, 2048), lambda *_, h=h: (h, 0)) for h in halves]
    norm_outs = [
        call(
            functools.partial(norm_one_kernel, h),
            [out((64, 2048)), out((64, 2048), f32), out((64, 128), f32), out((8, 128), f32)],
            (*sum_parts(attn_parts[h::2], Y4), tok, vecs),
            [rows] * 4 + [tok_half[h], vec_block],
            [rows, rows, whole((64, 128)), whole((8, 128))],
            scalars=(sp,),
            vmem=16,
        )
        for h in halves
    ]
    norm_one = [o[1] for o in norm_outs]
    scale_one = [o[2] for o in norm_outs]

    four = [rows] * 4
    group = whole((256, 2048))
    mark = out((8, 128), f32)
    mlp_out = [out((256, 2048))] * 3 + [mark] + [out((64, 2048))] * 4
    placed, anywhere = pl.BlockSpec(memory_space=pltpu.VMEM), pl.BlockSpec(memory_space=pl.ANY)
    *first_out, up_held, down_held = pl.pallas_call(
        mlp_first_kernel,
        in_specs=[placed] * 4 + [anywhere] * 2,
        out_specs=[placed] * 10,
        out_shape=mlp_out + [pltpu.VMEM((32, 64, 2048), bf16)] * 2,
        scratch_shapes=[pltpu.SemaphoreType.DMA((8,))],
        compiler_params=pltpu.CompilerParams(vmem_limit_bytes=14 * MIB),
        cost_estimate=pl.CostEstimate(flops=1000, bytes_accessed=1000, transcendentals=0),
    )(
        *y_gather(norm_outs[0][0]),
        norm_outs[0][3],
        pltpu.with_memory_space_constraint(mlp_w, pltpu.HBM),
    )
    mlp_held = (up_held, down_held)
    mlp_outs = [
        first_out,
        call_resident(
            mlp_kernel, mlp_out, (*y_gather(norm_outs[1][0]), first_out[3]), mlp_held
        ),
    ]
    two_outs = [
        call(
            functools.partial(norm_two_kernel, h),
            [
                out((64, 2048)),
                out((64, 2048)),
                out((64, 2048), f32),
                out((8, 2048), f32),
                out((8, 128), f32),
            ],
            (*sum_parts(mlp_outs[h][4:], Y4), norm_one[h], vecs, cot, norm_outs[h][3]),
            four + [rows, vec_block, tok_half[h], whole((8, 128))],
            [rows, rows, rows, whole((8, 2048)), whole((8, 128))],
            scalars=(sp,),
            vmem=16,
        )
        for h in halves
    ]
    output = jnp.concatenate([two_outs[h][0] for h in halves], axis=0)

    back_outs = []
    for h in halves:
        after = back_outs[0][2] if h else two_outs[0][4]
        back_outs.append(
            call_resident(
                mlp_back_kernel,
                [out((256, 2048))] * 2 + [mark] + [out((64, 2048))] * 4,
                (*y_gather(two_outs[h][1]), mlp_outs[h][1], after),
                mlp_held,
            )
        )
    hidden_terms = [sum_parts(back_outs[h][3:], Y4) for h in halves]

    def norm_one_back(h, after):
        return call(
            norm_one_back_kernel,
            [out((64, 2048)), out((64, 2048), f32), out((8, 2048), f32)],
            (*hidden_terms[h], two_outs[h][2], norm_one[h], scale_one[h], vecs, after),
            four + [rows, rows, whole((64, 128)), vec_block, any_place],
            [rows, rows, whole((8, 2048))],
            vmem=16,
            cost=300_000_000_000 if h else 1000,
        )

    one_outs = [norm_one_back(0, back_outs[0][2])]
    hidden_col = pl.BlockSpec((256, 512), lambda w, n: (0, jnp.where(w == 0, n, 3)))
    act_col = pl.BlockSpec((256, 512), lambda w, n: (0, jnp.where(w == 1, n, 0)))
    mlp_terms, terms_mark = call(
        mlp_terms_kernel,
        [out((32, 2, 64, 2048)), mark],
        (
            *(mlp_outs[h][2] for h in halves),
            *(back_outs[h][0] for h in halves),
            *(mlp_outs[h][0] for h in halves),
            *(back_outs[h][1] for h in halves),
            one_outs[0][2],
        ),
        [hidden_col] * 2 + [group] * 2 + [act_col] * 2 + [group] * 2 + [any_place],
        [pl.BlockSpec((8, 1, 64, 2048), lambda w, n: (n, w, 0, 0)), whole((8, 128))],
        grid=(2, 4),
        vmem=60,
    )
    one_outs.append(norm_one_back(1, terms_mark))
    attn_gathers = [y_gather(one_outs[h][0]) for h in halves]
    mlp_sum = lax.psum_scatter(mlp_terms, ZXC, scatter_dimension=0, tiled=True)
    mlp_sum = mlp_sum.reshape(2, 64, 2048)
    ctx_grad, ctx_grad_send, grad_attn = call(
        ctx_back_kernel,
        [out((512, 256)), out((512, 256)), out((512, 2048))],
        (*attn_gathers[0], *attn_gathers[1], proj),
        four * 2 + [whole((512, 2048))],
        [whole((512, 256)), whole((512, 256)), whole((512, 2048))],
        scalars=(sp,),
        vmem=16,
    )
    ctx_grad_got = to_core(ctx_grad_send)
    proj_block = pl.BlockSpec((4, 64, 512), lambda n, sp: (0, 0, n))
    proj_terms, proj_send = call(
        proj_terms_kernel,
        [out((4, 64, 2048))] * 2,
        (ctx, grad_attn),
        [whole((512, 512)), pl.BlockSpec((512, 512), lambda n, sp: (0, n))],
        [proj_block, proj_block],
        grid=(4,),
        scalars=(sp,),
        scratch=[pltpu.VMEM((512, 512), bf16)],
    )
    proj_got = to_core(proj_send)
    half_block = pl.BlockSpec((2, 1, 128, 256), lambda e, p, *_: (0, p, 0, 0))
    (qkv_grad,) = call(
        attend_back_kernel,
        [out((2, 2, 2, 128, 768))],
        (qkv_all, ctx_grad.reshape(2, 2, 128, 256), ctx_grad_got.reshape(2, 2, 128, 256)),
        [group_block(768), half_block, half_block],
        [group_block(768)],
        grid=(2, 2),
        scalars=(sp, lens),
        vmem=16,
        cost=20_000_000_000,
    )
    qkv_grad = qkv_grad.reshape(2, 512, 768)
    qkv_grad_got = to_core(qkv_grad)

    step_vec = pl.BlockSpec((8, 512), lambda n, sp: (0, n))
    blocks = call(
        qkv_terms_kernel,
        [out((4, 144, 512))] * 4 + [out((2048, 128))] * 4,
        (
            tok_all,
            qkv_grad.reshape(1024, 768),
            *(one_outs[h][2] for h in halves),
            *(two_outs[h][3] for h in halves),
            *(two_outs[h][4] for h in halves),
            proj_terms,
            proj_got,
            qkv_grad_got,
        ),
        [
            pl.BlockSpec((1024, 512), lambda n, sp: (0, n)),
            whole((1024, 768)),
            *[step_vec] * 4,
            whole((8, 128)),
            whole((8, 128)),
            proj_block,
            proj_block,
            any_place,
        ],
        [whole((4, 144, 512))] * 4 + [whole((2048, 128))] * 4,
        grid=(4,),
        scalars=(sp,),
        scratch=[pltpu.VMEM((512, 768), bf16)],
        cost=20_000_000_000,
    )
    a_terms, b_terms = sum_parts(blocks[:4], "z"), sum_parts(blocks[4:], "x")
    tok_parts = call(
        tok_back_kernel,
        [out((128, 2048))] * 4,
        (qkv_grad, qkv_grad_got, qkv_w, b_terms[1]),
        [
            pl.BlockSpec((1, 512, 768), lambda n, sp: (0, 0, 0)),
            pl.BlockSpec((1, 512, 768), lambda n, sp: (1, 0, 0)),
            pl.BlockSpec((4, 64, 1536), lambda n, sp: (n, 0, 0)),
            any_place,
        ],
        [pl.BlockSpec((128, 256), lambda n, sp: (0, n))] * 4,
        grid=(8,),
        scalars=(sp,),
        scratch=[pltpu.VMEM((512, 1536), bf16)],
    )
    input_grad, grad_mark = call(
        last_kernel,
        [out((128, 2048), f32), mark],
        (*sum_parts(tok_parts, Y4), one_outs[0][1], one_outs[1][1]),
        [whole((128, 2048))] * 4 + [rows] * 2,
        [whole((128, 2048)), whole((8, 128))],
        vmem=16,
    )

    a_line, proj_line, *b_line = call(
        middle_kernel,
        [out((4, 144, 512)), out((64, 2048))] + [out((128, 256))] * 4,
        (*a_terms, *b_terms),
        [whole((4, 144, 512))] * 4 + [whole((2048, 128))] * 4,
        [whole((4, 144, 512)), whole((64, 2048))] + [whole((128, 256))] * 4,
        vmem=60,
        cost=20_000_000_000,
    )
    pieces, near, away = call(
        pieces_kernel,
        [out((8, 48, 768))] + [out((32, 2048))] * 2,
        (
            lax.all_to_all(a_line, "x", 0, 0, tiled=True),
            *sum_parts(b_line, "z"),
            proj_line,
            *(diagonal(proj_line, False, by) for by in (1, 2, 3)),
            grad_mark,
        ),
        [whole((4, 144, 512))]
        + [whole((128, 256))] * 4
        + [whole((64, 2048))] * 4
        + [any_place],
        [whole((8, 48, 768))] + [whole((32, 2048))] * 2,
        scalars=(sp,),
        scratch=[pltpu.VMEM((64, 2048), bf16)],
        vmem=60,
        cost=20_000_000_000,
    )
    arrived = lax.all_to_all(pieces, Y8, 0, 0, tiled=True)
    given = [along_y(away, 1), along_y(near, 2), along_y(away, 3)]
    rep_part, up_away = call(
        mlp_split_kernel,
        [out((96, 2048)), out((32, 2048))],
        (mlp_sum, near),
        [whole((2, 64, 2048)), any_place],
        [whole((96, 2048)), whole((32, 2048))],
        scalars=(sp,),
        vmem=60,
    )
    up_yl, up_both = (lax.ppermute(up_away, Y4, xored(by, 4)) for by in (1, 3))
    grad_up, grad_down, mlp_mark = call(
        final_mlp_kernel,
        [out((32, 8192), f32), out((128, 2048), f32), mark],
        (
            mlp_sum,
            up_yl,
            lax.ppermute(rep_part, Y4, xored(2, 4)),
            up_both,
        ),
        [whole((2, 64, 2048)), whole((32, 2048)), whole((96, 2048)), whole((32, 2048))],
        [whole((32, 8192)), whole((128, 2048)), whole((8, 128))],
        scalars=(sp,),
        vmem=60,
    )
    one_row = whole((1, 32))
    grad_q, grad_k, grad_v, grad_proj, g1, s1, g2, s2, rms = call(
        final_kernel,
        [out((32, 2048), f32)] * 4 + [out((1, 32), f32)] * 4 + [out((1, 128), f32)],
        (arrived, near, *given, up_yl, up_both),
        [whole((8, 48, 768))] + [whole((32, 2048))] * 4 + [any_place] * 2,
        [whole((32, 2048))] * 4 + [one_row] * 4 + [whole((1, 128))],
        scalars=(sp,),
        vmem=60,
        cost=300_000_000_000,
    )
    vec_mine = [v.reshape(32) for v in (g1, s1, g2, s2)]
    rms_stats = rms[0, :3]
    return (
        output.reshape(1, 128, 2048),
        input_grad.reshape(1, 128, 2048),
        grad_q,
        grad_k,
        grad_v,
        grad_proj,
        vec_mine[0],
        vec_mine[1],
        grad_up,
        grad_down,
        vec_mine[2],
        vec_mine[3],
        rms_stats,
    )


def solution(mesh):
    split = Mesh(mesh.devices.reshape(2, 4, 4, 2, 2), AXES)
    rows, vec, seq = P(SHARD, None), P(SHARD), P(SHARD, "rep", None)
    return jax.shard_map(
        per_device,
        mesh=split,
        in_specs=(seq, vec, rows, rows, rows, rows, vec, vec, rows, rows, vec, vec, seq),
        out_specs=(seq, seq, rows, rows, rows, rows, vec, vec, rows, rows, vec, vec, P()),
        check_vma=False,
    )
```

```python
import functools

import jax
import jax.numpy as jnp
from jax import lax
from jax.experimental import pallas as pl
from jax.experimental.pallas import tpu as pltpu
from jax.sharding import Mesh
from jax.sharding import PartitionSpec as P

HEAD_DIM = 128
AXES = ("rep", "z", "x", "yl", "c")
SHARD = ("z", "x", "yl", "c")
ZXC = ("z", "x", "c")
Y4 = ("rep", "yl")
Y8 = ("rep", "yl", "c")
norm_eps = 1e-12
masked_score = -1e30
bf16 = jnp.bfloat16
f32 = jnp.float32
i32 = jnp.int32
MIB = 1 << 20
REP, ZZ, XX, YL, CC, LEN = range(6)


def shifted(by, count=4):
    return [(i, (i + by) % count) for i in range(count)]


def xored(by, count):
    return [(i, i ^ by) for i in range(count)]


def from_offset(value, axes, offset):
    return lax.ppermute(value, axes, shifted(-offset))


def to_core(value):
    return lax.ppermute(value, "c", xored(1, 2))


def y_gather(value):
    return [value] + [from_offset(value, Y4, d) for d in (1, 2, 3)]


def x_gather(value):
    return [value] + [from_offset(value, "x", d) for d in (1, 2, 3)]


def sum_parts(parts, axis):
    return [parts[0]] + [lax.ppermute(parts[d], axis, shifted(d)) for d in (1, 2, 3)]


def diagonal(value, to_z, by):
    pairs = []
    for rep in range(2):
        for yl in range(2):
            y = rep * 2 + yl
            at = lambda z: rep * 8 + (z % 4) * 2 + yl
            pairs.append((at(y), at(y + by)) if to_z else (at(y - by), at(y)))
    return lax.ppermute(value, ("rep", "z", "yl"), pairs)


def along_y(value, by):
    pairs = []
    for y in range(4):
        at = lambda v: ((v % 4) // 2) * 8 + y * 2 + v % 2
        pairs.append((at(y), at(y + by)))
    return lax.ppermute(value, ("rep", "z", "yl"), pairs)


def call(kernel, outs, operands, specs, out_specs, grid=(1,), scalars=(), scratch=(), vmem=28, cost=1000):
    return pl.pallas_call(
        kernel,
        grid_spec=pltpu.PrefetchScalarGridSpec(
            num_scalar_prefetch=len(scalars),
            grid=grid,
            in_specs=specs,
            out_specs=out_specs,
            scratch_shapes=scratch,
        ),
        out_shape=outs,
        compiler_params=pltpu.CompilerParams(vmem_limit_bytes=vmem * MIB),
        cost_estimate=pl.CostEstimate(flops=cost, bytes_accessed=1000, transcendentals=0),
    )(*scalars, *operands)


def call_resident(kernel, outs, operands, weights, vmem=14):
    place = pl.BlockSpec(memory_space=pltpu.VMEM)
    held = [pltpu.with_memory_space_constraint(w, pltpu.VMEM) for w in weights]
    return pl.pallas_call(
        kernel,
        in_specs=[place] * (len(operands) - 1)
        + [pl.BlockSpec(memory_space=pl.ANY)]
        + [place] * len(weights),
        out_specs=[place] * len(outs),
        out_shape=outs,
        compiler_params=pltpu.CompilerParams(vmem_limit_bytes=vmem * MIB),
        cost_estimate=pl.CostEstimate(flops=1000, bytes_accessed=1000, transcendentals=0),
    )(*operands, *held)


def out(shape, dtype=bf16):
    return jax.ShapeDtypeStruct(shape, dtype)


def whole(shape):
    return pl.BlockSpec(shape, lambda *_: (0,) * len(shape))


def swap_middle(value):
    width = value.shape[1]
    chunk = (lax.broadcasted_iota(i32, value.shape, 1) >> 5) & 3
    ahead = pltpu.roll(value, width - 32, 1)
    behind = pltpu.roll(value, 32, 1)
    return jnp.where(chunk == 1, ahead, jnp.where(chunk == 2, behind, value))


def swap_kernel(tok_ref, out_ref):
    out_ref[...] = swap_middle(tok_ref[...].astype(f32)).astype(bf16)


def prep_kernel(sp, wq_ref, wk_ref, wv_ref, g1, s1, g2, s2, keep_ref, send_ref):
    rep, yl = sp[REP], sp[YL]
    s = yl * 2 + sp[CC]
    lane = lax.broadcasted_iota(i32, (1, 128), 1)
    rows = []
    for ref in (g1, s1, g2, s2):
        value = ref[...].astype(f32)
        tiled = jnp.concatenate([value, value, value, value], axis=1)
        rows.append(jnp.where((lane >> 5) == s, tiled, 0.0))
    rows.append(jnp.where(lane == s, sp[LEN].astype(f32), 0.0))
    vec = jnp.concatenate(rows + [jnp.zeros((27, 128), f32)], axis=0).astype(bf16)
    keep_ref[:, 1536:] = vec
    send_ref[:, 1536:] = vec
    for target, dest in ((yl, keep_ref), (1 - yl, send_ref)):
        for i, ref in enumerate((wq_ref, wk_ref, wv_ref)):
            start = pl.multiple_of((rep * 2 + target) * 512, 512)
            block = ref[:, pl.ds(start, 512)]
            for head in range(4):
                dest[:, (head * 3 + i) * 128 : (head * 3 + i + 1) * 128] = block[
                    :, head * 128 : (head + 1) * 128
                ]


def prep_up_kernel(sp, up_ref, keep_ref, send_ref):
    rep, yl = sp[REP], sp[YL]
    for target, dest in ((yl, keep_ref), (1 - yl, send_ref)):
        for zx in range(16):
            start = pl.multiple_of(zx * 512 + target * 256, 256)
            block = up_ref[:, pl.ds(start, 256)]
            low = jnp.concatenate([block[:, 0:64], block[:, 128:192]], axis=1)
            high = jnp.concatenate([block[:, 64:128], block[:, 192:256]], axis=1)
            dest[:, zx * 128 : (zx + 1) * 128] = jnp.where(rep == 0, low, high)


def qkv_piece_kernel(sp, keep_ref, got_ref, out_ref):
    own = pl.ds(pl.multiple_of(sp[YL] * 32, 32), 32)
    other = pl.ds(pl.multiple_of((1 - sp[YL]) * 32, 32), 32)
    out_ref[own, :1536] = keep_ref[:, :1536]
    out_ref[other, :1536] = got_ref[:, :1536]
    vec = (keep_ref[:, 1536:].astype(f32) + got_ref[:, 1536:].astype(f32)).astype(bf16)
    out_ref[0:32, 1536:] = vec
    out_ref[32:64, 1536:] = jnp.zeros_like(vec)


def mlp_piece_kernel(sp, keep_ref, got_ref, down_ref, after1_ref, after2_ref, out_ref):
    own = pl.ds(pl.multiple_of(sp[YL] * 32, 32), 32)
    other = pl.ds(pl.multiple_of((1 - sp[YL]) * 32, 32), 32)
    out_ref[0, own, :] = keep_ref[...]
    out_ref[0, other, :] = got_ref[...]
    out_ref[1] = down_ref[pl.ds(pl.multiple_of(sp[REP] * 64, 64), 64), :]


def cat_kernel(t0, t1, t2, t3, after_ref, out_ref):
    for d, ref in enumerate((t0, t1, t2, t3)):
        out_ref[d * 128 : (d + 1) * 128, :] = ref[...]


def out_rows_kernel(sp, own_ref, got_ref, out_ref):
    out_ref[pl.ds(pl.multiple_of(sp[YL] * 32, 32), 32), :] = own_ref[...]
    out_ref[pl.ds(pl.multiple_of((1 - sp[YL]) * 32, 32), 32), :] = got_ref[...]


def proj_kernel(sp, own_ref, other_ref, proj_ref):
    for d in range(4):
        for ref, core in ((own_ref, sp[CC]), (other_ref, 1 - sp[CC])):
            for yl_of in range(2):
                row = pl.multiple_of(((sp[XX] + d) & 3) * 128 + yl_of * 64 + core * 32, 32)
                proj_ref[pl.ds(row, 32), :] = ref[d, yl_of * 32 : (yl_of + 1) * 32, :]


def qkv_kernel(sp, tok_ref, w_ref, vec_in_ref, out_ref, vec_ref, len_ref):
    @pl.when(pl.program_id(0) == 0)
    def _():
        for zx in range(16):
            pair = vec_in_ref[2 * zx].astype(f32) + vec_in_ref[2 * zx + 1].astype(f32)
            vec_ref[:, zx * 128 : (zx + 1) * 128] = pair
        own = (sp[ZZ] * 4 + sp[XX]) * 2
        len_ref[...] = vec_in_ref[own].astype(f32) + vec_in_ref[own + 1].astype(f32)

    weights = w_ref[...].reshape(2048, 256)
    out_ref[...] = jnp.dot(tok_ref[...], weights, preferred_element_type=f32).astype(bf16)


def softmax_of(q, k, open_row):
    raw = lax.dot_general(q, k, (((1,), (1,)), ((), ())), preferred_element_type=f32)
    scores = jnp.where(open_row, raw * (HEAD_DIM**-0.5), masked_score)
    top = jnp.max(scores, axis=-1, keepdims=True)
    exponent = jnp.exp(scores - top)
    return exponent * (1.0 / jnp.sum(exponent, axis=-1, keepdims=True))


def open_keys(sp, lens):
    e, p = pl.program_id(0), pl.program_id(1)
    length = lens[((sp[YL] + p) & 1) * 2 + ((sp[CC] + e) & 1)]
    swap = ((sp[REP] * 2 + sp[YL] + p) & 3) >> 1
    lane = lax.broadcasted_iota(i32, (1, 256), 1)
    position = jnp.where(swap == 1, (lane + 128) & 255, lane)
    return position < length


def head_part(ref, head, i):
    return ref[0, :, 0, :, (head * 3 + i) * 128 : (head * 3 + i + 1) * 128].reshape(256, 128)


def attend_kernel(sp, lens, qkv_ref, ctx_ref):
    open_row = open_keys(sp, lens)
    for head in range(2):
        q, k, v = (head_part(qkv_ref, head, i) for i in range(3))
        probs = softmax_of(q, k, open_row).astype(bf16)
        ctx = jnp.dot(probs, v, preferred_element_type=f32).astype(bf16)
        ctx_ref[0, :, 0, :, head * 128 : (head + 1) * 128] = ctx.reshape(2, 128, 128)


def attend_back_kernel(sp, lens, qkv_ref, own_ref, other_ref, out_ref):
    open_row = open_keys(sp, lens)
    scale = HEAD_DIM**-0.5
    first = pl.program_id(0) == 0
    for head in range(2):
        q, k, v = (head_part(qkv_ref, head, i) for i in range(3))
        cols = slice(head * 128, (head + 1) * 128)
        grad = jnp.where(first, own_ref[:, 0, :, cols], other_ref[:, 0, :, cols]).reshape(256, 128)
        probs = softmax_of(q, k, open_row)
        grad_probs = lax.dot_general(grad, v, (((1,), (1,)), ((), ())), preferred_element_type=f32)
        inner = jnp.sum(probs * grad_probs, axis=-1, keepdims=True)
        grad_scores = (probs * (grad_probs - inner)).astype(bf16)
        grad_q = jnp.dot(grad_scores, k, preferred_element_type=f32) * scale
        over = (((0,), (0,)), ((), ()))
        grad_k = lax.dot_general(grad_scores, q, over, preferred_element_type=f32) * scale
        grad_v = lax.dot_general(probs.astype(bf16), grad, over, preferred_element_type=f32)
        for i, part in enumerate((grad_q, grad_k, grad_v)):
            out_ref[0, :, 0, :, (head * 3 + i) * 128 : (head * 3 + i + 1) * 128] = part.astype(
                bf16
            ).reshape(2, 128, 128)


def group_block(columns):
    return pl.BlockSpec((1, 2, 1, 128, columns), lambda e, p, *_: (e, 0, p, 0, 0))


def to_four(result, refs):
    rows = result.shape[0] // len(refs)
    for d, ref in enumerate(refs):
        ref[...] = result[d * rows : (d + 1) * rows].astype(bf16)


def out_kernel(sp, own_ref, got_ref, proj_ref, ctx_ref, *refs):
    @pl.when(pl.program_id(0) == 0)
    def _():
        ctx_ref[:, pl.ds(pl.multiple_of(sp[CC] * 256, 256), 256)] = own_ref[0]
        ctx_ref[:, pl.ds(pl.multiple_of((1 - sp[CC]) * 256, 256), 256)] = got_ref[0]

    to_four(jnp.dot(ctx_ref[...], proj_ref[...], preferred_element_type=f32), refs)


def terms_of(refs):
    return sum(r[...].astype(f32) for r in refs[1:]) + refs[0][...].astype(f32)


def valid_rows(sp, half):
    position = sp[REP] * 128 + half * 64 + lax.broadcasted_iota(i32, (64, 1), 0)
    return (position < sp[LEN]).astype(f32)


def lane_of(values):
    lane = lax.broadcasted_iota(i32, (8, 128), 1)
    total = jnp.zeros((8, 128), f32)
    for i, value in enumerate(values):
        total = jnp.where(lane == i, value, total)
    return total


def normed(values):
    center = values - jnp.mean(values, axis=-1, keepdims=True)
    spread = jnp.mean(center * center, axis=-1, keepdims=True)
    scale = lax.rsqrt(spread + norm_eps)
    return center * scale, scale


def norm_one_kernel(half, sp, p0, p1, p2, p3, tok_ref, vec_ref, hidden_ref, norm_ref, scale_ref, stat_ref):
    attn = terms_of((p0, p1, p2, p3))
    resid = tok_ref[...].astype(f32) + attn
    norm, scale = normed(resid)
    hidden = norm * vec_ref[0:1, :] + vec_ref[1:2, :]
    hidden_ref[...] = swap_middle(hidden).astype(bf16)
    norm_ref[...] = norm
    scale_ref[...] = jnp.broadcast_to(scale, scale_ref.shape)
    valid = valid_rows(sp, half)
    stat_ref[...] = lane_of((jnp.sum(valid * (resid * resid)), jnp.sum(valid * (attn * attn))))


def norm_two_kernel(
    half, sp, p0, p1, p2, p3, norm_ref, vec_ref, cot_ref, stat_ref, out_ref, low_ref, grad_ref, vg_ref, st_ref
):
    mlp = terms_of((p0, p1, p2, p3))
    resid = norm_ref[...] * vec_ref[0:1, :] + vec_ref[1:2, :] + mlp
    norm, scale = normed(resid)
    out_ref[...] = (norm * vec_ref[2:3, :] + vec_ref[3:4, :]).astype(bf16)
    valid = valid_rows(sp, half)
    grad_out = cot_ref[...].astype(f32) * valid
    vg_ref[0:1, :] = jnp.sum(grad_out * norm, axis=0, keepdims=True)
    vg_ref[1:2, :] = jnp.sum(grad_out, axis=0, keepdims=True)
    e = grad_out * vec_ref[2:3, :]
    mean_e = jnp.mean(e, axis=-1, keepdims=True)
    mean_en = jnp.mean(e * norm, axis=-1, keepdims=True)
    grad = scale * (e - mean_e - norm * mean_en)
    grad_ref[...] = grad
    low_ref[...] = grad.astype(bf16)
    lane = lax.broadcasted_iota(i32, (8, 128), 1)
    more = jnp.where(lane == 2, jnp.sum(valid * (mlp * mlp)), jnp.sum(valid))
    st_ref[...] = jnp.where(lane < 2, stat_ref[...], more)


def norm_one_back_kernel(
    p0, p1, p2, p3, grad2_ref, norm_ref, scale_ref, vec_ref, after_ref, low_ref, grad_ref, vg_ref
):
    grad = grad2_ref[...] + swap_middle(terms_of((p0, p1, p2, p3)))
    norm = norm_ref[...]
    vg_ref[0:1, :] = jnp.sum(grad * norm, axis=0, keepdims=True)
    vg_ref[1:2, :] = jnp.sum(grad, axis=0, keepdims=True)
    e = grad * vec_ref[0:1, :]
    mean_e = jnp.mean(e, axis=-1, keepdims=True)
    mean_en = jnp.mean(e * norm, axis=-1, keepdims=True)
    back = scale_ref[:, 0:1] * (e - mean_e - norm * mean_en)
    grad_ref[...] = back
    low_ref[...] = back.astype(bf16)


def last_kernel(p0, p1, p2, p3, grad_a_ref, grad_b_ref, out_ref, mark_ref):
    mark_ref[...] = jnp.zeros_like(mark_ref)
    total = swap_middle(terms_of((p0, p1, p2, p3)))
    out_ref[0:64, :] = grad_a_ref[...] + total[0:64]
    out_ref[64:128, :] = grad_b_ref[...] + total[64:128]


CHUNKS = [slice(i * 512, (i + 1) * 512) for i in range(4)]
UNITS = [slice(i * 8, (i + 1) * 8) for i in range(4)]


def join(refs, all_ref):
    for d, ref in enumerate(refs):
        all_ref[d * 64 : (d + 1) * 64, :] = ref[...]


def split_rows(result, refs, columns):
    for d, ref in enumerate(refs):
        ref[:, columns] = result[d * 64 : (d + 1) * 64].astype(bf16)


def mlp_kernel(
    h0, h1, h2, h3, after_ref, up_ref, down_ref, act_ref, slope_ref, all_ref, mark_ref, *refs,
    arrived=lambda i: None,
):
    mark_ref[...] = jnp.zeros_like(mark_ref)
    join((h0, h1, h2, h3), all_ref)
    root = 0.7978845608028654
    for i, chunk in enumerate(CHUNKS):
        arrived(i)
        up = up_ref[:, :, chunk].reshape(2048, 512)
        v = jnp.dot(all_ref[...], up, preferred_element_type=f32)
        square = v * v
        t = jnp.tanh(root * v * (1.0 + 0.044715 * square))
        half = 0.5 * (1.0 + t)
        act_ref[:, chunk] = (v * half).astype(bf16)
        slope = half + 0.5 * v * (1.0 - t * t) * (root * (1.0 + 3 * 0.044715 * square))
        slope_ref[:, chunk] = slope.astype(bf16)
    for i, chunk in enumerate(CHUNKS):
        arrived(4 + i)
        down = down_ref[:, :, chunk].reshape(2048, 512)
        split_rows(jnp.dot(act_ref[...], down, preferred_element_type=f32), refs, chunk)


def mlp_first_kernel(h0, h1, h2, h3, after_ref, w_ref, act_ref, slope_ref, all_ref, mark_ref, *rest):
    refs, (up_ref, down_ref, sem) = rest[:4], rest[4:]
    copies = [
        pltpu.make_async_copy(w_ref.at[:, i, :, chunk], ref.at[:, :, chunk], sem.at[i * 4 + j])
        for i, ref in enumerate((up_ref, down_ref))
        for j, chunk in enumerate(pl.ds(k * 512, 512) for k in range(4))
    ]
    for copy in copies[:3]:
        copy.start()

    def arrived(i):
        copies[i].wait()
        if i + 3 < 8:
            copies[i + 3].start()

    mlp_kernel(
        h0, h1, h2, h3, after_ref, up_ref, down_ref, act_ref, slope_ref, all_ref, mark_ref, *refs,
        arrived=arrived,
    )


BACK = (((1,), (1,)), ((), ()))
OVER = (((0,), (0,)), ((), ()))


def mlp_back_kernel(
    g0, g1, g2, g3, slope_ref, after_ref, up_ref, down_ref, pre_ref, all_ref, mark_ref, *refs
):
    mark_ref[...] = jnp.zeros_like(mark_ref)
    join((g0, g1, g2, g3), all_ref)
    for chunk, units in zip(CHUNKS, UNITS):
        down = down_ref[units].reshape(512, 2048)
        grad = lax.dot_general(all_ref[...], down, BACK, preferred_element_type=f32)
        pre_ref[:, chunk] = (grad * slope_ref[:, chunk].astype(f32)).astype(bf16)
    for chunk, units in zip(CHUNKS, UNITS):
        up = up_ref[units].reshape(512, 2048)
        term = lax.dot_general(pre_ref[...], up, BACK, preferred_element_type=f32)
        split_rows(term, refs, chunk)


def mlp_terms_kernel(h0, h1, p0, p1, a0, a1, g0, g1, after_ref, out_ref, mark_ref):
    mark_ref[...] = jnp.zeros_like(mark_ref)

    def both(left, right):
        total = sum(
            lax.dot_general(l[...], r[...], OVER, preferred_element_type=f32)
            for l, r in zip(left, right)
        )
        out_ref[...] = total.astype(bf16).reshape(out_ref.shape)

    @pl.when(pl.program_id(0) == 0)
    def _():
        both((h0, h1), (p0, p1))

    @pl.when(pl.program_id(0) == 1)
    def _():
        both((a0, a1), (g0, g1))


def ctx_back_kernel(sp, *refs):
    proj_ref, own_ref, other_ref, all_ref = refs[8:]
    for i, ref in enumerate(refs[:8]):
        row = (i % 4) * 128 + (i // 4) * 64
        all_ref[row : row + 64, :] = ref[...]
    for ref, core in ((own_ref, sp[CC]), (other_ref, 1 - sp[CC])):
        weights = proj_ref[pl.ds(pl.multiple_of(core * 256, 256), 256), :]
        ref[...] = lax.dot_general(
            all_ref[...], weights, BACK, preferred_element_type=f32
        ).astype(bf16)


def proj_terms_kernel(sp, ctx_ref, grad_ref, mine_ref, send_ref, term_ref):
    term = lax.dot_general(ctx_ref[...], grad_ref[...], OVER, preferred_element_type=f32)
    term_ref[...] = term.astype(bf16)
    for d in range(4):
        for ref, core in ((mine_ref, sp[CC]), (send_ref, 1 - sp[CC])):
            for yl_of in range(2):
                row = pl.multiple_of(((sp[XX] + d) & 3) * 128 + yl_of * 64 + core * 32, 32)
                ref[d, yl_of * 32 : (yl_of + 1) * 32, :] = term_ref[pl.ds(row, 32), :]


def qkv_terms_kernel(
    sp, tok_ref, grad_ref, v1a, v1b, v2a, v2b, sta, stb, mine_ref, got_ref, after_ref, *rest
):
    a_refs, b_refs, term_ref = rest[:4], rest[4:8], rest[8]
    term = lax.dot_general(tok_ref[...], grad_ref[...], OVER, preferred_element_type=f32)
    term_ref[...] = term.astype(bf16)
    step = pl.program_id(0)
    dz = (step - sp[ZZ]) & 3
    for dx in range(4):
        start = pl.multiple_of(((sp[XX] + dx) & 3) * 128, 128)
        rows = pl.ds(start, 128)
        vec = [v1a[0:2, rows] + v1b[0:2, rows], v2a[0:2, rows] + v2b[0:2, rows]]
        vec += [sta[0:4] + stb[0:4]]
        vec = jnp.concatenate(vec + [jnp.zeros((8, 128), f32)], axis=0).astype(bf16)
        vec = jnp.concatenate([vec, jnp.zeros((16, 384), bf16)], axis=1)
        for j in range(2):
            at = pl.multiple_of((dz * 2 + j) * 128, 128)
            b_refs[dx][pl.ds(at, 128), :] = term_ref[rows, 512 + j * 128 : 640 + j * 128]
        total = mine_ref[dx].astype(f32) + got_ref[dx].astype(f32)
        total = total.astype(bf16)
        for j in range(4):
            at = pl.multiple_of(1024 + (step * 4 + j) * 64, 64)
            b_refs[dx][pl.ds(at, 64), :] = total[:, j * 128 : (j + 1) * 128]
        for k in range(4):

            @pl.when(dz == k)
            def _():
                a_refs[k][(sp[XX] + dx) & 3, 0:128, :] = term_ref[rows, :512]
                a_refs[k][(sp[XX] + dx) & 3, 128:144, :] = vec


def middle_kernel(*refs):
    a, b = refs[0:4], refs[4:8]
    a_ref, proj_ref, b_refs = refs[8], refs[9], refs[10:14]
    a_ref[...] = terms_of(a).astype(bf16)
    total = terms_of(b).astype(bf16)
    for d in range(4):
        for j in range(2):
            at = (d * 2 + j) * 128
            b_refs[d][:, j * 128 : (j + 1) * 128] = total[at : at + 128]
    for j in range(16):
        proj_ref[:, j * 128 : (j + 1) * 128] = total[1024 + j * 64 : 1088 + j * 64]


def tok_back_kernel(sp, own_ref, got_ref, w_ref, after_a, after_b, *rest):
    refs, cat_ref = rest[:4], rest[4]

    @pl.when(pl.program_id(0) == 0)
    def _():
        cat_ref[:, pl.ds(pl.multiple_of(sp[CC] * 768, 256), 768)] = own_ref[0]
        cat_ref[:, pl.ds(pl.multiple_of((1 - sp[CC]) * 768, 256), 768)] = got_ref[0]

    weights = w_ref[...].reshape(256, 1536)
    to_four(lax.dot_general(cat_ref[...], weights, BACK, preferred_element_type=f32), refs)


def pieces_kernel(sp, *refs):
    b, proj = refs[1:5], refs[5:9]
    out_ref, near_ref, away_ref, proj_ref = refs[10:14]
    first = terms_of([refs[0].at[x] for x in range(4)]).astype(bf16)
    second = terms_of(b).astype(bf16)
    for m in range(8):
        row = (m & 1) * 64 + ((m >> 1) & 1) * 32
        out_ref[m, 0:32, :512] = first[row : row + 32]
        out_ref[m, 0:32, 512:] = second[row : row + 32]
        out_ref[m, 32:48, :512] = first[128:144]
        out_ref[m, 32:48, 512:] = jnp.zeros((16, 256), bf16)
    proj_ref[...] = terms_of(proj).astype(bf16)
    near_ref[...] = proj_ref[pl.ds(pl.multiple_of(sp[YL] * 32, 32), 32), :]
    away_ref[...] = proj_ref[pl.ds(pl.multiple_of((1 - sp[YL]) * 32, 32), 32), :]


def final_kernel(sp, got_ref, *refs):
    near, given = refs[0], refs[1:4]
    q_ref, k_ref, v_ref, proj_ref, g1, s1, g2, s2, rms_ref = refs[6:]
    for m in range(8):
        for i, ref in enumerate((q_ref, k_ref, v_ref)):
            for head in range(2):
                at = m * 256 + head * 128
                ref[:, at : at + 128] = got_ref[
                    m, 0:32, (head * 3 + i) * 128 : (head * 3 + i + 1) * 128
                ].astype(f32)
    on_diagonal = sp[ZZ] == sp[REP] * 2 + sp[YL]
    proj_ref[...] = jnp.where(on_diagonal, near[...].astype(f32), terms_of(given))
    vec = sum(got_ref[m, 32:48, :128].astype(f32) for m in range(8))
    s = sp[YL] * 2 + sp[CC]
    own = jnp.where(s == 0, vec[:, 0:32], vec[:, 32:64])
    own = jnp.where(s == 2, vec[:, 64:96], own)
    own = jnp.where(s == 3, vec[:, 96:128], own)
    for i, ref in enumerate((g1, s1, g2, s2)):
        ref[...] = own[i : i + 1]
    rms_ref[...] = jnp.sqrt(vec[4:5] / (vec[4:5, 3:4] * 2048.0))


def mlp_split_kernel(sp, sum_ref, after_ref, rep_ref, away_ref):
    rep_ref[0:32, :] = sum_ref[0, pl.ds(pl.multiple_of(sp[YL] * 32, 32), 32), :]
    rep_ref[32:96, :] = sum_ref[1]
    away_ref[...] = sum_ref[0, pl.ds(pl.multiple_of((1 - sp[YL]) * 32, 32), 32), :]


def final_mlp_kernel(sp, own_ref, yl_ref, rep_ref, both_ref, up_ref, down_ref, mark_ref):
    mark_ref[...] = jnp.zeros_like(mark_ref)
    rep, yl = sp[REP], sp[YL]
    mine = own_ref[0, pl.ds(pl.multiple_of(yl * 32, 32), 32), :]
    first_rep, first_yl = rep == 0, yl == 0
    got = {(0, 0): mine, (0, 1): yl_ref[...], (1, 0): rep_ref[0:32], (1, 1): both_ref[...]}
    for yl_of in range(2):
        same = (yl == yl_of)
        near = jnp.where(same, got[0, 0], got[0, 1]).astype(f32)
        far = jnp.where(same, got[1, 0], got[1, 1]).astype(f32)
        low = jnp.where(first_rep, near, far)
        high = jnp.where(first_rep, far, near)
        for zx in range(16):
            for c in range(2):
                src = slice(zx * 128 + c * 64, zx * 128 + c * 64 + 64)
                at = zx * 512 + yl_of * 256 + c * 128
                up_ref[:, at : at + 128] = jnp.concatenate([low[:, src], high[:, src]], axis=1)
    own_rows = pl.ds(pl.multiple_of(rep * 64, 64), 64)
    far_rows = pl.ds(pl.multiple_of((1 - rep) * 64, 64), 64)
    down_ref[own_rows, :] = own_ref[1].astype(f32)
    down_ref[far_rows, :] = rep_ref[32:96].astype(f32)


def per_device(
    hidden_in,
    lengths,
    w_query,
    w_key,
    w_value,
    w_output,
    attn_gain,
    attn_shift,
    w_up,
    w_down,
    mlp_gain,
    mlp_shift,
    cotangent,
):
    rep, z, x, yl, c = (lax.axis_index(a) for a in AXES)
    s, y = yl * 2 + c, rep * 2 + yl
    any_place = pl.BlockSpec(memory_space=pl.ANY)
    tok = hidden_in.reshape(128, 2048)
    cot = cotangent.reshape(128, 2048)
    sp = jnp.stack([rep, z, x, yl, c, lengths[0], lengths[0], lengths[0]]).astype(i32)
    rows = whole((128, 2048))

    keep, send = call(
        prep_kernel,
        [out((32, 1664))] * 2,
        (
            w_query,
            w_key,
            w_value,
            *(v.reshape(1, 32) for v in (attn_gain, attn_shift, mlp_gain, mlp_shift)),
        ),
        [whole((32, 2048))] * 3 + [whole((1, 32))] * 4,
        [whole((32, 1664))] * 2,
        scalars=(sp,),
        vmem=60,
    )
    got = lax.ppermute(send, "yl", xored(1, 2))
    keep_up, send_up = call(
        prep_up_kernel,
        [out((32, 2048))] * 2,
        (w_up,),
        [whole((32, 8192))],
        [whole((32, 2048))] * 2,
        scalars=(sp,),
        vmem=60,
    )
    got_up = lax.ppermute(send_up, "yl", xored(1, 2))
    (qkv_piece,) = call(
        qkv_piece_kernel,
        [out((64, 1664))],
        (keep, got),
        [whole((32, 1664))] * 2,
        [whole((64, 1664))],
        scalars=(sp,),
        vmem=16,
    )
    qkv_w = lax.all_gather(qkv_piece, ZXC, axis=0)

    first_yl, on_diagonal = yl == 0, y == z
    out_got = lax.ppermute(w_output, "yl", xored(1, 2))
    (out_piece,) = call(
        out_rows_kernel,
        [out((64, 2048))],
        (w_output, out_got),
        [whole((32, 2048))] * 2,
        [whole((64, 2048))],
        scalars=(sp,),
        vmem=16,
    )
    spread = [diagonal(out_piece, True, by) for by in (1, 2, 3)]
    out_piece = jnp.where(on_diagonal, out_piece, spread[0] + spread[1] + spread[2])
    out_own = jnp.stack(x_gather(out_piece))
    block4 = whole((4, 64, 2048))
    (proj,) = call(
        proj_kernel,
        [out((512, 2048))],
        (out_own, to_core(out_own)),
        [block4, block4],
        [whole((512, 2048))],
        scalars=(sp,),
        vmem=16,
    )

    (tok_swapped,) = call(swap_kernel, [out((128, 2048))], (tok,), [rows], [rows], vmem=16)
    (tok_mine,) = call(
        cat_kernel,
        [out((512, 2048))],
        (*y_gather(tok_swapped), out_own),
        [rows] * 4 + [any_place],
        [whole((512, 2048))],
        vmem=16,
    )
    tok_all = jnp.concatenate([tok_mine, to_core(tok_mine)], axis=0)
    (mlp_piece,) = call(
        mlp_piece_kernel,
        [out((2, 64, 2048))],
        (keep_up, got_up, w_down, out_own, tok_mine),
        [whole((32, 2048))] * 2 + [whole((128, 2048)), any_place, any_place],
        [whole((2, 64, 2048))],
        scalars=(sp,),
        vmem=16,
    )
    mlp_w = lax.all_gather(mlp_piece, ZXC, axis=0)

    qkv_all, vecs, lens = call(
        qkv_kernel,
        [out((1024, 768)), out((16, 2048), f32), out((16, 128), f32)],
        (tok_all, qkv_w, qkv_w),
        [
            whole((1024, 2048)),
            pl.BlockSpec((32, 64, 256), lambda n, sp: (0, 0, sp[CC] * 3 + n)),
            pl.BlockSpec((32, 16, 128), lambda n, sp: (0, 0, 12)),
        ],
        [
            pl.BlockSpec((1024, 256), lambda n, sp: (0, n)),
            whole((16, 2048)),
            whole((16, 128)),
        ],
        grid=(3,),
        scalars=(sp,),
        vmem=60,
    )
    lens = lens[4, :4].astype(i32)
    qkv_all = qkv_all.reshape(2, 2, 2, 128, 768)
    (ctx_all,) = call(
        attend_kernel,
        [out((2, 2, 2, 128, 256))],
        (qkv_all,),
        [group_block(768)],
        [group_block(256)],
        grid=(2, 2),
        scalars=(sp, lens),
        vmem=16,
    )
    ctx_all = ctx_all.reshape(2, 512, 256)
    ctx_got = to_core(ctx_all)
    ctx, *attn_parts = call(
        out_kernel,
        [out((512, 512))] + [out((64, 2048))] * 8,
        (ctx_all, ctx_got, proj),
        [
            pl.BlockSpec((1, 512, 256), lambda n, sp: (0, 0, 0)),
            pl.BlockSpec((1, 512, 256), lambda n, sp: (1, 0, 0)),
            pl.BlockSpec((512, 512), lambda n, sp: (0, n)),
        ],
        [whole((512, 512))] + [pl.BlockSpec((64, 512), lambda n, sp: (0, n))] * 8,
        grid=(4,),
        scalars=(sp,),
    )
    vec_block, rows, halves = whole((16, 2048)), whole((64, 2048)), (0, 1)
    tok_half = [pl.BlockSpec((64, 2048), lambda *_, h=h: (h, 0)) for h in halves]
    norm_outs = [
        call(
            functools.partial(norm_one_kernel, h),
            [out((64, 2048)), out((64, 2048), f32), out((64, 128), f32), out((8, 128), f32)],
            (*sum_parts(attn_parts[h::2], Y4), tok, vecs),
            [rows] * 4 + [tok_half[h], vec_block],
            [rows, rows, whole((64, 128)), whole((8, 128))],
            scalars=(sp,),
            vmem=16,
        )
        for h in halves
    ]
    norm_one = [o[1] for o in norm_outs]
    scale_one = [o[2] for o in norm_outs]

    four = [rows] * 4
    group = whole((256, 2048))
    mark = out((8, 128), f32)
    mlp_out = [out((256, 2048))] * 3 + [mark] + [out((64, 2048))] * 4
    placed, anywhere = pl.BlockSpec(memory_space=pltpu.VMEM), pl.BlockSpec(memory_space=pl.ANY)
    *first_out, up_held, down_held = pl.pallas_call(
        mlp_first_kernel,
        in_specs=[placed] * 4 + [anywhere] * 2,
        out_specs=[placed] * 10,
        out_shape=mlp_out + [pltpu.VMEM((32, 64, 2048), bf16)] * 2,
        scratch_shapes=[pltpu.SemaphoreType.DMA((8,))],
        compiler_params=pltpu.CompilerParams(vmem_limit_bytes=14 * MIB),
        cost_estimate=pl.CostEstimate(flops=1000, bytes_accessed=1000, transcendentals=0),
    )(
        *y_gather(norm_outs[0][0]),
        norm_outs[0][3],
        pltpu.with_memory_space_constraint(mlp_w, pltpu.HBM),
    )
    mlp_held = (up_held, down_held)
    mlp_outs = [
        first_out,
        call_resident(
            mlp_kernel, mlp_out, (*y_gather(norm_outs[1][0]), first_out[3]), mlp_held
        ),
    ]
    two_outs = [
        call(
            functools.partial(norm_two_kernel, h),
            [
                out((64, 2048)),
                out((64, 2048)),
                out((64, 2048), f32),
                out((8, 2048), f32),
                out((8, 128), f32),
            ],
            (*sum_parts(mlp_outs[h][4:], Y4), norm_one[h], vecs, cot, norm_outs[h][3]),
            four + [rows, vec_block, tok_half[h], whole((8, 128))],
            [rows, rows, rows, whole((8, 2048)), whole((8, 128))],
            scalars=(sp,),
            vmem=16,
        )
        for h in halves
    ]
    output = jnp.concatenate([two_outs[h][0] for h in halves], axis=0)

    back_outs = []
    for h in halves:
        after = back_outs[0][2] if h else two_outs[0][4]
        back_outs.append(
            call_resident(
                mlp_back_kernel,
                [out((256, 2048))] * 2 + [mark] + [out((64, 2048))] * 4,
                (*y_gather(two_outs[h][1]), mlp_outs[h][1], after),
                mlp_held,
            )
        )
    hidden_terms = [sum_parts(back_outs[h][3:], Y4) for h in halves]

    def norm_one_back(h, after):
        return call(
            norm_one_back_kernel,
            [out((64, 2048)), out((64, 2048), f32), out((8, 2048), f32)],
            (*hidden_terms[h], two_outs[h][2], norm_one[h], scale_one[h], vecs, after),
            four + [rows, rows, whole((64, 128)), vec_block, any_place],
            [rows, rows, whole((8, 2048))],
            vmem=16,
            cost=300_000_000_000 if h else 1000,
        )

    one_outs = [norm_one_back(0, back_outs[0][2])]
    hidden_col = pl.BlockSpec((256, 512), lambda w, n: (0, jnp.where(w == 0, n, 3)))
    act_col = pl.BlockSpec((256, 512), lambda w, n: (0, jnp.where(w == 1, n, 0)))
    mlp_terms, terms_mark = call(
        mlp_terms_kernel,
        [out((32, 2, 64, 2048)), mark],
        (
            *(mlp_outs[h][2] for h in halves),
            *(back_outs[h][0] for h in halves),
            *(mlp_outs[h][0] for h in halves),
            *(back_outs[h][1] for h in halves),
            one_outs[0][2],
        ),
        [hidden_col] * 2 + [group] * 2 + [act_col] * 2 + [group] * 2 + [any_place],
        [pl.BlockSpec((8, 1, 64, 2048), lambda w, n: (n, w, 0, 0)), whole((8, 128))],
        grid=(2, 4),
        vmem=60,
    )
    one_outs.append(norm_one_back(1, terms_mark))
    attn_gathers = [y_gather(one_outs[h][0]) for h in halves]
    mlp_sum = lax.psum_scatter(mlp_terms, ZXC, scatter_dimension=0, tiled=True)
    mlp_sum = mlp_sum.reshape(2, 64, 2048)
    ctx_grad, ctx_grad_send, grad_attn = call(
        ctx_back_kernel,
        [out((512, 256)), out((512, 256)), out((512, 2048))],
        (*attn_gathers[0], *attn_gathers[1], proj),
        four * 2 + [whole((512, 2048))],
        [whole((512, 256)), whole((512, 256)), whole((512, 2048))],
        scalars=(sp,),
        vmem=16,
    )
    ctx_grad_got = to_core(ctx_grad_send)
    proj_block = pl.BlockSpec((4, 64, 512), lambda n, sp: (0, 0, n))
    proj_terms, proj_send = call(
        proj_terms_kernel,
        [out((4, 64, 2048))] * 2,
        (ctx, grad_attn),
        [whole((512, 512)), pl.BlockSpec((512, 512), lambda n, sp: (0, n))],
        [proj_block, proj_block],
        grid=(4,),
        scalars=(sp,),
        scratch=[pltpu.VMEM((512, 512), bf16)],
    )
    proj_got = to_core(proj_send)
    half_block = pl.BlockSpec((2, 1, 128, 256), lambda e, p, *_: (0, p, 0, 0))
    (qkv_grad,) = call(
        attend_back_kernel,
        [out((2, 2, 2, 128, 768))],
        (qkv_all, ctx_grad.reshape(2, 2, 128, 256), ctx_grad_got.reshape(2, 2, 128, 256)),
        [group_block(768), half_block, half_block],
        [group_block(768)],
        grid=(2, 2),
        scalars=(sp, lens),
        vmem=16,
        cost=20_000_000_000,
    )
    qkv_grad = qkv_grad.reshape(2, 512, 768)
    qkv_grad_got = to_core(qkv_grad)

    step_vec = pl.BlockSpec((8, 512), lambda n, sp: (0, n))
    blocks = call(
        qkv_terms_kernel,
        [out((4, 144, 512))] * 4 + [out((2048, 128))] * 4,
        (
            tok_all,
            qkv_grad.reshape(1024, 768),
            *(one_outs[h][2] for h in halves),
            *(two_outs[h][3] for h in halves),
            *(two_outs[h][4] for h in halves),
            proj_terms,
            proj_got,
            qkv_grad_got,
        ),
        [
            pl.BlockSpec((1024, 512), lambda n, sp: (0, n)),
            whole((1024, 768)),
            *[step_vec] * 4,
            whole((8, 128)),
            whole((8, 128)),
            proj_block,
            proj_block,
            any_place,
        ],
        [whole((4, 144, 512))] * 4 + [whole((2048, 128))] * 4,
        grid=(4,),
        scalars=(sp,),
        scratch=[pltpu.VMEM((512, 768), bf16)],
        cost=20_000_000_000,
    )
    a_terms, b_terms = sum_parts(blocks[:4], "z"), sum_parts(blocks[4:], "x")
    tok_parts = call(
        tok_back_kernel,
        [out((128, 2048))] * 4,
        (qkv_grad, qkv_grad_got, qkv_w, b_terms[1], b_terms[3]),
        [
            pl.BlockSpec((1, 512, 768), lambda n, sp: (0, 0, 0)),
            pl.BlockSpec((1, 512, 768), lambda n, sp: (1, 0, 0)),
            pl.BlockSpec((4, 64, 1536), lambda n, sp: (n, 0, 0)),
            any_place,
            any_place,
        ],
        [pl.BlockSpec((128, 256), lambda n, sp: (0, n))] * 4,
        grid=(8,),
        scalars=(sp,),
        scratch=[pltpu.VMEM((512, 1536), bf16)],
    )
    input_grad, grad_mark = call(
        last_kernel,
        [out((128, 2048), f32), mark],
        (*sum_parts(tok_parts, Y4), one_outs[0][1], one_outs[1][1]),
        [whole((128, 2048))] * 4 + [rows] * 2,
        [whole((128, 2048)), whole((8, 128))],
        vmem=16,
    )

    a_line, proj_line, *b_line = call(
        middle_kernel,
        [out((4, 144, 512)), out((64, 2048))] + [out((128, 256))] * 4,
        (*a_terms, *b_terms),
        [whole((4, 144, 512))] * 4 + [whole((2048, 128))] * 4,
        [whole((4, 144, 512)), whole((64, 2048))] + [whole((128, 256))] * 4,
        vmem=60,
        cost=20_000_000_000,
    )
    pieces, near, away = call(
        pieces_kernel,
        [out((8, 48, 768))] + [out((32, 2048))] * 2,
        (
            lax.all_to_all(a_line, "x", 0, 0, tiled=True),
            *sum_parts(b_line, "z"),
            proj_line,
            *(diagonal(proj_line, False, by) for by in (1, 2, 3)),
            grad_mark,
        ),
        [whole((4, 144, 512))]
        + [whole((128, 256))] * 4
        + [whole((64, 2048))] * 4
        + [any_place],
        [whole((8, 48, 768))] + [whole((32, 2048))] * 2,
        scalars=(sp,),
        scratch=[pltpu.VMEM((64, 2048), bf16)],
        vmem=60,
        cost=20_000_000_000,
    )
    arrived = lax.all_to_all(pieces, Y8, 0, 0, tiled=True)
    given = [along_y(away, 1), along_y(near, 2), along_y(away, 3)]
    rep_part, up_away = call(
        mlp_split_kernel,
        [out((96, 2048)), out((32, 2048))],
        (mlp_sum, near),
        [whole((2, 64, 2048)), any_place],
        [whole((96, 2048)), whole((32, 2048))],
        scalars=(sp,),
        vmem=60,
    )
    up_yl, up_both = (lax.ppermute(up_away, Y4, xored(by, 4)) for by in (1, 3))
    grad_up, grad_down, mlp_mark = call(
        final_mlp_kernel,
        [out((32, 8192), f32), out((128, 2048), f32), mark],
        (
            mlp_sum,
            up_yl,
            lax.ppermute(rep_part, Y4, xored(2, 4)),
            up_both,
        ),
        [whole((2, 64, 2048)), whole((32, 2048)), whole((96, 2048)), whole((32, 2048))],
        [whole((32, 8192)), whole((128, 2048)), whole((8, 128))],
        scalars=(sp,),
        vmem=60,
    )
    one_row = whole((1, 32))
    grad_q, grad_k, grad_v, grad_proj, g1, s1, g2, s2, rms = call(
        final_kernel,
        [out((32, 2048), f32)] * 4 + [out((1, 32), f32)] * 4 + [out((1, 128), f32)],
        (arrived, near, *given, up_yl, up_both),
        [whole((8, 48, 768))] + [whole((32, 2048))] * 4 + [any_place] * 2,
        [whole((32, 2048))] * 4 + [one_row] * 4 + [whole((1, 128))],
        scalars=(sp,),
        vmem=60,
        cost=300_000_000_000,
    )
    vec_mine = [v.reshape(32) for v in (g1, s1, g2, s2)]
    rms_stats = rms[0, :3]
    return (
        output.reshape(1, 128, 2048),
        input_grad.reshape(1, 128, 2048),
        grad_q,
        grad_k,
        grad_v,
        grad_proj,
        vec_mine[0],
        vec_mine[1],
        grad_up,
        grad_down,
        vec_mine[2],
        vec_mine[3],
        rms_stats,
    )


def solution(mesh):
    split = Mesh(mesh.devices.reshape(2, 4, 4, 2, 2), AXES)
    rows, vec, seq = P(SHARD, None), P(SHARD), P(SHARD, "rep", None)
    return jax.shard_map(
        per_device,
        mesh=split,
        in_specs=(seq, vec, rows, rows, rows, rows, vec, vec, rows, rows, vec, vec, seq),
        out_specs=(seq, seq, rows, rows, rows, rows, vec, vec, rows, rows, vec, vec, P()),
        check_vma=False,
    )
```
